512 devices in a mesh: seq: 32 (over z_lo, y), rep: 16 (over z_hi, x, core).
Axes of the slice: x: 4, y: 8, z: 8 (z_hi: 2, z_lo: 4; z = z_hi * 4 + z_lo), core: 2. Of those that a mesh axis runs over, the one named last changes fastest.
Arguments:
- hidden: bfloat16 [16, 4096, 4096], P('rep', 'seq'), may hold values from -6 to 6
- queries: bfloat16 [16, 4096, 4096], P('rep', 'seq'), may hold values from -110 to 110, as said below
- weight_copies: bfloat16 [16, 4096, 1024], P('rep', 'seq'), may hold values from -0.09375 to 0.09375
- segment_ids: int32 [16, 4096], P('rep'), may hold values from 0 to 5, never falling along the last dimension, each value on 1 to 2048 neighbouring positions
- owner: int32 [1], replicated, may hold values from 0 to 1048575
Outputs:
- attended: bfloat16 [16, 4096, 4096], P('rep', 'seq')
The draws below stay inside these ranges and needn't reach their ends.
Inputs may be any that keep to these rules, and one draw needn't show every extreme that they name: `queries`: query features of each token and head.
All inputs are finite; a program needn't handle non-finite values.
Results may differ from the reference program's by a relative error of at most 0.007.
The reference program's roundings to bfloat16 on the way (of `current`, `keys`, `values`, `rotated` and `weights`) count: a program that leaves them out, or rounds other values in their place, can miss the bound.
Values may be sent and summed in bfloat16 or wider, within the bound.
No kernel may reach another device: no remote copies, remote signals or barrier semaphores. Data moves between devices by JAX's collectives and lax.ppermute only.
A program may use at most 64 MiB of HBM per device.

```python
import math
import jax
import jax.numpy as jnp
import numpy as np
from jax import lax

D = 4096
HEADS = 32
KV_HEADS = 4
HEAD_DIM = 128
DOCS = 6
LENGTH = 4096
MOST = 2048
N_REP = 16


def draw_queries(key, part):
    full_shape = (N_REP, LENGTH, HEADS * HEAD_DIM)
    return jnp.clip(jax.random.normal(key, full_shape, jnp.float32), -6.0, 6.0).astype(jnp.bfloat16)


def shard_levels(rng, shape, shards, low, largest):
    def one(dim, parts):
        heights = jax.random.uniform(jax.random.fold_in(jax.random.fold_in(rng, 6), dim), (parts,), jnp.float32, low / len(shards), largest / len(shards))
        return jnp.repeat(jnp.exp(heights), shape[dim] // parts).reshape((-1,) + (1,) * (len(shape) - dim - 1))

    loudness = one(*shards[0])
    for cut in shards[1:]:
        loudness = loudness * one(*cut)
    return loudness


def split_up(count, total, reach, skew):
    portions = [(1 << 20) // math.isqrt(standing ** skew) + 1 for standing in range(2, count + 1)]
    spare, counts = total - reach - (count - 1), [1] * (count - 1)
    while spare > 0:
        movable = [i for i in range(count - 1) if counts[i] < reach]
        pool, remaining = sum([portions[i] for i in movable]), spare
        for i in movable:
            extra = min(reach - counts[i], max(1, remaining * portions[i] // pool), spare)
            counts[i] = counts[i] + extra
            spare = spare - extra
    return np.array([reach] + counts)


def uneven_parts(stream_key, number_of, total, reach, skew):
    if number_of == 2:
        one = jax.random.randint(stream_key, (), max(1, total - reach), min(reach, total - 1) + 1)
        return jnp.stack([one, total - one])
    tallies = jnp.asarray(split_up(number_of, total, reach, skew), jnp.int32)
    twos = (number_of - 1) // 2
    giver, sink = tallies[1:1 + 2 * twos:2], tallies[2:2 + 2 * twos:2]
    slack = jnp.minimum(giver - 1, reach - sink)
    passed = jax.random.randint(jax.random.fold_in(stream_key, 1), (twos,), 0, 1 << 20) % (slack + 1)
    tallies = tallies.at[1:1 + 2 * twos:2].set(giver - passed).at[2:2 + 2 * twos:2].set(sink + passed)
    return tallies[jax.random.permutation(jax.random.fold_in(stream_key, 2), number_of)]


def scatter_about(key, extent, deviation, most, cuts=(), held_as=jnp.bfloat16):
    array = jax.random.normal(key, extent, jnp.float32) * deviation
    if len(cuts) > 0:
        array = shard_levels(key, extent, cuts, -0.22, 0.18) * array
    return jnp.clip(array, min=-most, max=most).astype(held_as)


def setup_inputs(seed: int = 0) -> dict:
    seeds = jax.random.split(jax.random.key(seed), 6)
    return {
        "hidden": scatter_about(seeds[0], (N_REP, LENGTH, D), 1.0, 6.0, ((0, 16), (1, 32))),
        "queries": draw_queries(jax.random.fold_in(seeds[5], 71), 0),
        "weight_copies": scatter_about(seeds[2], (N_REP, D, 2 * KV_HEADS * HEAD_DIM), D ** -0.5, 0.09375, ((0, 16), (1, 32))),
        "segment_ids": jax.vmap(lambda own: jnp.searchsorted(jnp.cumsum(uneven_parts(own, DOCS, LENGTH, MOST, 2)), jnp.arange(LENGTH), side="right"))(jax.random.split(seeds[3], N_REP)).reshape((N_REP, LENGTH)).astype(jnp.int32),
        "owner": jax.random.randint(seeds[4], (1,), 0, 1048576).astype(jnp.int32),
    }


THETA = 1000000.0


def rotary(tensor, positions):
    half_dim = tensor.shape[-1] // 2
    freqs = THETA ** (-(jnp.arange(half_dim, dtype=jnp.float32) * 2.0) / tensor.shape[-1])
    angles = positions.astype(jnp.float32)[:, None] * freqs[None, :]
    cosine = jnp.cos(angles)[:, None, :]
    sine = jnp.sin(angles)[:, None, :]
    first_half = tensor[..., :half_dim]
    second_half = tensor[..., half_dim:]
    return jnp.concatenate([first_half * cosine - second_half * sine, second_half * cosine + first_half * sine], axis=-1)


def doc_starts(segment_row, own_segments):
    return jnp.sum((segment_row[None, :] < own_segments[:, None]).astype(jnp.int32), axis=1)


def attend(query_all, key_all, value_all, segment_row):
    length = query_all.shape[0]
    block_rows = min(length, max(512, length // 8))
    score_scale = 1.0 / (query_all.shape[-1] ** 0.5)
    outputs = []
    for row_begin in range(0, length, block_rows):
        row_end = row_begin + block_rows
        query_block = query_all[row_begin:row_end].astype(jnp.float32)
        key_block = key_all[:row_end].astype(jnp.float32)
        value_block = value_all[:row_end].astype(jnp.float32)
        scores = jnp.einsum("qhd,khd->hqk", query_block, key_block) * score_scale
        query_index = jnp.arange(row_begin, row_end, dtype=jnp.int32)[:, None]
        key_index = jnp.arange(row_end, dtype=jnp.int32)[None, :]
        allowed = (key_index <= query_index) & (segment_row[row_begin:row_end][:, None] == segment_row[:row_end][None, :])
        masked = jnp.where(allowed[None], scores, -1e30)
        row_max = jnp.max(masked, axis=-1, keepdims=True)
        exponent = jnp.where(allowed[None], jnp.exp(masked - row_max), 0.0)
        totals = jnp.sum(exponent, axis=-1, keepdims=True)
        weights = exponent.astype(jnp.bfloat16)
        mixed = jnp.einsum("hqk,khd->qhd", weights.astype(jnp.float32), value_block)
        mixed = mixed / jnp.transpose(totals, (1, 0, 2))
        outputs.append(mixed.astype(jnp.bfloat16))
    return jnp.concatenate(outputs, axis=0)


def reference(hidden, queries, weight_copies, segment_ids, owner):
    root_copy = (owner[0] % N_REP).astype(jnp.int32)
    current = lax.dynamic_index_in_dim(weight_copies, root_copy, 0, keepdims=False)
    kv_width = KV_HEADS * HEAD_DIM

    def one_pack(packed):
        hidden_pack, query_pack, segment_row = packed
        length = hidden_pack.shape[0]
        projected = jnp.dot(hidden_pack, current, preferred_element_type=jnp.float32)
        positions = jnp.arange(length, dtype=jnp.int32) - doc_starts(segment_row, segment_row)
        keys = rotary(projected[:, :kv_width].reshape(length, KV_HEADS, HEAD_DIM), positions).astype(jnp.bfloat16)
        values = projected[:, kv_width:].reshape(length, KV_HEADS, HEAD_DIM).astype(jnp.bfloat16)
        rotated = rotary(query_pack.astype(jnp.float32).reshape(length, HEADS, HEAD_DIM), positions).astype(jnp.bfloat16)
        key_heads = jnp.repeat(keys, HEADS // KV_HEADS, axis=1)
        value_heads = jnp.repeat(values, HEADS // KV_HEADS, axis=1)
        result = attend(rotated, key_heads, value_heads, segment_row)
        return result.reshape(length, HEADS * HEAD_DIM)

    return lax.map(one_pack, (hidden, queries, segment_ids))
```

```python
import math

import jax
import jax.numpy as jnp
from jax import lax
from jax.experimental import pallas as pl
from jax.experimental.pallas import tpu as pltpu
from jax.sharding import Mesh
from jax.sharding import PartitionSpec as P

HEADS = 32
KV_HEADS = 4
HEAD_DIM = 128
GROUP = HEADS // KV_HEADS
THETA = 1000000.0
BLOCK = 128
LOW = -1e30
DOCS = 6

AXES = ("z1", "z0", "y1", "y0", "zh", "x", "c")
SIZES = (2, 2, 4, 2, 2, 4, 2)
SEQ = ("z1", "z0", "y1", "y0")
REP = ("zh", "x", "c")
Y = ("y1", "y0")
Z = ("z1", "z0")


def ring(size, shift):
    return [(i, (i + shift) % size) for i in range(size)]


def exchange(value, axes):
    return lax.all_to_all(value, axes, split_axis=0, concat_axis=0, tiled=True)


def spread(value, axes, members):
    return exchange(jnp.broadcast_to(value[None], (members,) + value.shape), axes)


def angles_of(positions):
    half = HEAD_DIM // 2
    freqs = THETA ** (-(jnp.arange(half, dtype=jnp.float32) * 2.0) / HEAD_DIM)
    return positions.astype(jnp.float32)[..., None] * freqs


def starts_of(segment_row, segments):
    first = jnp.zeros(segments.shape, jnp.int32)
    for doc in range(1, DOCS):
        begin = jnp.sum((segment_row < doc).astype(jnp.int32))
        first = jnp.where(segments >= doc, begin, first)
    return first


def turn_kernel(q_ref, cos_ref, sin_ref, out_ref):
    half = HEAD_DIM // 2

    @pl.loop(0, 4)
    def _(z):
        cosine, sine = cos_ref[z], sin_ref[z]
        for h in range(GROUP):
            cols = slice(h * HEAD_DIM, (h + 1) * HEAD_DIM)
            t = q_ref[z, :, cols].astype(jnp.float32).T
            a, b = t[:half], t[half:]
            out_ref[z, :half, cols] = (a * cosine - b * sine).astype(jnp.bfloat16)
            out_ref[z, half:, cols] = (b * cosine + a * sine).astype(jnp.bfloat16)


def turn_queries(q, cosine, sine):
    vm = pl.BlockSpec(memory_space=pltpu.VMEM)
    return pl.pallas_call(
        turn_kernel,
        out_shape=jax.ShapeDtypeStruct((4, HEAD_DIM, GROUP * BLOCK), jnp.bfloat16),
        in_specs=[vm] * 3,
        out_specs=vm,
        compiler_params=pltpu.CompilerParams(vmem_limit_bytes=32 * 2**20),
        cost_estimate=pl.CostEstimate(flops=4 * 2**20, bytes_accessed=2 * 2**20, transcendentals=0),
    )(q, cosine, sine)


def attend_kernel(where_ref, q_ref, start_ref, kv_ref, out_ref, acc, top, total):
    factor = math.log2(math.e) / math.sqrt(HEAD_DIM)
    wide = 2 * BLOCK
    y = where_ref[0]

    @pl.loop(0, 4)
    def _(z):
        block = z * 8 + y
        last = block // 2
        first = where_ref[1 + z]
        top[...] = jnp.full(top.shape, LOW, jnp.float32)
        total[...] = jnp.zeros(total.shape, jnp.float32)
        acc[...] = jnp.zeros(acc.shape, jnp.float32)
        start = start_ref[z]

        def pair_step(step, carry):
            pair = last - step
            zz = pair // 4
            y0 = (pair % 4) * 2
            r0, r1 = (y - y0) & 7, (y - y0 - 1) & 7
            key = jnp.concatenate([kv_ref[r0, zz, 0], kv_ref[r1, zz, 0]], axis=0)
            val = jnp.concatenate([kv_ref[r0, zz, 1], kv_ref[r1, zz, 1]], axis=1)
            key_at = pair * wide + lax.broadcasted_iota(jnp.int32, (wide, BLOCK), 0)
            row_at = block * BLOCK + lax.broadcasted_iota(jnp.int32, (wide, BLOCK), 1)
            allowed = (key_at >= start) & (key_at <= row_at)
            for h in range(GROUP):
                cols = slice(h * BLOCK, (h + 1) * BLOCK)
                s = jnp.dot(key, q_ref[z, :, cols], preferred_element_type=jnp.float32)
                s = jnp.where(allowed, s, LOW)
                old = top[:, cols]
                new = jnp.maximum(old, jnp.max(s, axis=0, keepdims=True))
                p = jnp.exp2((s - new) * factor)
                scale = jnp.exp2((old - new) * factor)
                top[:, cols] = new
                total[:, cols] = total[:, cols] * scale + jnp.sum(p, axis=0, keepdims=True)
                acc[:, cols] = acc[:, cols] * scale + jnp.dot(
                    val, p.astype(jnp.bfloat16), preferred_element_type=jnp.float32
                )
            return carry

        lax.fori_loop(0, last - first + 1, pair_step, 0)
        for h in range(GROUP):
            cols = slice(h * BLOCK, (h + 1) * BLOCK)
            mixed = acc[:, cols] / total[:, cols]
            out_ref[z, :, cols] = mixed.T.astype(jnp.bfloat16)


def attend(where, q, start, kv):
    vm = pl.BlockSpec(memory_space=pltpu.VMEM)
    rows = GROUP * BLOCK
    return pl.pallas_call(
        attend_kernel,
        out_shape=jax.ShapeDtypeStruct((4, BLOCK, rows), jnp.bfloat16),
        in_specs=[pl.BlockSpec(memory_space=pltpu.SMEM), vm, vm, vm],
        out_specs=vm,
        scratch_shapes=[
            pltpu.VMEM((HEAD_DIM, rows), jnp.float32),
            pltpu.VMEM((1, rows), jnp.float32),
            pltpu.VMEM((1, rows), jnp.float32),
        ],
        compiler_params=pltpu.CompilerParams(vmem_limit_bytes=32 * 2**20),
        cost_estimate=pl.CostEstimate(
            flops=2 * 2**30, bytes_accessed=4 * 2**20, transcendentals=4 * 2**20
        ),
    )(where, q, start, kv)


def on_device(hidden, queries, weight_copies, segment_ids, owner):
    y, z = lax.axis_index(Y), lax.axis_index(Z)
    x, c = lax.axis_index("x"), lax.axis_index("c")
    half = HEAD_DIM // 2

    pieces = weight_copies[0].reshape(2, 64, 2, 4, 128).transpose(0, 3, 2, 1, 4)
    got = exchange(pieces.reshape(16, 64, 128), REP)
    piece = lax.dynamic_index_in_dim(got, owner[0] % 16, 0, keepdims=False)
    part = spread(piece, ("zh", "z1", "y1"), 16).reshape(16 * 64, 128)
    part = spread(part, ("z0", "y0"), 4)
    mine = part.reshape(2, 2, 2, 2, 4, 64, 128).transpose(3, 0, 4, 1, 2, 5, 6).reshape(4096, 128)
    other = lax.ppermute(mine, "c", ring(2, 1))

    own = hidden[0]
    left = lax.ppermute(own, "x", ring(4, 1))
    right = lax.ppermute(own, "x", ring(4, -1))
    far0 = lax.ppermute(left[:64], "x", ring(4, 1))
    far1 = lax.ppermute(right[64:], "x", ring(4, -1))
    rows = jnp.concatenate([own, left, far0, far1, right], axis=0)

    split = queries[0].reshape(BLOCK, 4, GROUP * HEAD_DIM).transpose(1, 0, 2)
    q_part = exchange(split, Z)

    segment_row = segment_ids[0]
    blocks = segment_row.reshape(4, 8, BLOCK)
    mine_segments = lax.dynamic_index_in_dim(blocks, y, 1, keepdims=False)
    start = starts_of(segment_row, mine_segments)
    token = (jnp.arange(4)[:, None] * 8 + y) * BLOCK + jnp.arange(BLOCK)[None]
    positions = (token - start).astype(jnp.int32)
    q_angles = jnp.swapaxes(angles_of(positions), 1, 2)
    q_turned = turn_queries(q_part, jnp.cos(q_angles), jnp.sin(q_angles))
    own_positions = lax.dynamic_index_in_dim(positions, z, 0, keepdims=False)
    k_angles = angles_of(lax.all_gather(own_positions, "x", axis=0))

    first = jnp.dot(rows, mine, preferred_element_type=jnp.float32)
    second = jnp.dot(rows, other, preferred_element_type=jnp.float32)
    order = (x - jnp.arange(4)) % 4
    first = first.reshape(4, BLOCK, HEAD_DIM)[order]
    second = second.reshape(4, BLOCK, HEAD_DIM)[order]
    key = jnp.where(c == 0, first, second)
    value = jnp.where(c == 0, second, first).astype(jnp.bfloat16)
    cosine, sine = jnp.cos(k_angles), jnp.sin(k_angles)
    a, b = key[..., :half], key[..., half:]
    key = jnp.concatenate([a * cosine - b * sine, b * cosine + a * sine], axis=-1)
    both = jnp.stack([key.astype(jnp.bfloat16), jnp.swapaxes(value, 1, 2)], axis=1)
    kv = exchange(exchange(both, "x"), Z)

    up1 = lax.ppermute(kv, Y, ring(8, 1))
    down1 = lax.ppermute(kv, Y, ring(8, -1))
    up2 = lax.ppermute(up1, Y, ring(8, 1))
    down2 = lax.ppermute(down1, Y, ring(8, -1))
    up3 = lax.ppermute(up2, Y, ring(8, 1))
    down3 = lax.ppermute(down2, Y, ring(8, -1))
    up4 = lax.ppermute(up3, Y, ring(8, 1))
    kv_all = jnp.stack([kv, up1, up2, up3, up4, down3, down2, down1])

    where = jnp.concatenate([y[None], start[:, 0] // (2 * BLOCK)]).astype(jnp.int32)
    mixed = attend(where, q_turned, start[:, None, :], kv_all)
    back = exchange(mixed, Z)
    return back.transpose(1, 0, 2).reshape(1, BLOCK, HEADS * HEAD_DIM)


def solution(mesh):
    fine = Mesh(mesh.devices.reshape(SIZES), AXES)
    placed = (
        P(REP, SEQ, None),
        P(REP, SEQ, None),
        P(REP, SEQ, None),
        P(REP, None),
        P(),
    )
    return jax.shard_map(
        on_device, mesh=fine, in_specs=placed, out_specs=P(REP, SEQ, None), check_vma=False
    )
```

```python
import functools
import math

import jax
import jax.numpy as jnp
from jax import lax
from jax.experimental import pallas as pl
from jax.experimental.pallas import tpu as pltpu
from jax.sharding import Mesh
from jax.sharding import PartitionSpec as P

HEADS = 32
KV_HEADS = 4
HEAD_DIM = 128
GROUP = HEADS // KV_HEADS
THETA = 1000000.0
BLOCK = 128
LOW = -1e30
DOCS = 6

AXES = ("z1", "z0", "y1", "y0", "zh", "x", "c")
SIZES = (2, 2, 4, 2, 2, 4, 2)
SEQ = ("z1", "z0", "y1", "y0")
REP = ("zh", "x", "c")
Y = ("y1", "y0")
Z = ("z1", "z0")


def ring(size, shift):
    return [(i, (i + shift) % size) for i in range(size)]


def pick(value, index, axis=0):
    return lax.dynamic_index_in_dim(value, index, axis, keepdims=False)


def exchange(value, axes):
    return lax.all_to_all(value, axes, split_axis=0, concat_axis=0, tiled=True)


def spread(value, axes, members):
    return exchange(jnp.broadcast_to(value[None], (members,) + value.shape), axes)


def angles_of(positions):
    half = HEAD_DIM // 2
    freqs = THETA ** (-(jnp.arange(half, dtype=jnp.float32) * 2.0) / HEAD_DIM)
    return positions.astype(jnp.float32)[..., None] * freqs


def starts_of(segment_row, segments):
    first = jnp.zeros(segments.shape, jnp.int32)
    for doc in range(1, DOCS):
        begin = jnp.sum((segment_row < doc).astype(jnp.int32))
        first = jnp.where(segments >= doc, begin, first)
    return first


VMEM = pl.BlockSpec(memory_space=pltpu.VMEM)
SMEM = pl.BlockSpec(memory_space=pltpu.SMEM)


def call(kernel, out_shape, specs, cost, scratch=()):
    flops, moved = cost
    return pl.pallas_call(
        kernel,
        out_shape=out_shape,
        in_specs=specs,
        out_specs=jax.tree.map(lambda _: VMEM, out_shape),
        scratch_shapes=list(scratch),
        compiler_params=pltpu.CompilerParams(vmem_limit_bytes=32 * 2**20),
        cost_estimate=pl.CostEstimate(flops=flops, bytes_accessed=moved, transcendentals=0),
    )


def turn_kernel(where_ref, *refs):
    parts, (cos_ref, sin_ref, out_ref) = refs[:4], refs[4:]
    half = HEAD_DIM // 2
    for d in range(4):
        z = (where_ref[0] - d) & 3
        cosine, sine = cos_ref[z], sin_ref[z]
        for h in range(GROUP):
            cols = slice(h * HEAD_DIM, (h + 1) * HEAD_DIM)
            t = parts[d][:, cols].astype(jnp.float32).T
            a, b = t[:half], t[half:]
            out_ref[z, :half, cols] = (a * cosine - b * sine).astype(jnp.bfloat16)
            out_ref[z, half:, cols] = (b * cosine + a * sine).astype(jnp.bfloat16)


def turn_queries(where, parts, cosine, sine):
    return call(
        turn_kernel,
        jax.ShapeDtypeStruct((4, HEAD_DIM, GROUP * BLOCK), jnp.bfloat16),
        [SMEM] + [VMEM] * 6,
        (4 * 2**20, 2 * 2**20),
    )(where, *parts, cosine, sine)


def multiply(hidden_refs, weight_ref, out_ref):
    for row, hidden_ref in enumerate(hidden_refs):
        at = (0, 128, 256, 320, 384)[row]
        total = None
        for block in range(0, 32, 2):
            z1, z0, y1 = block // 16, block // 8 % 2, block // 2 % 4
            low = z0 * 16 + z1 * 4 + y1
            weight = jnp.concatenate([weight_ref[low], weight_ref[low + 8]], axis=0)
            term = jnp.dot(
                hidden_ref[:, block * 128 : block * 128 + 256],
                weight,
                preferred_element_type=jnp.float32,
            )
            total = term if total is None else total + term
        out_ref[at : at + hidden_ref.shape[0]] = total


def project_first_kernel(*refs):
    multiply(refs[:5], refs[5], refs[6])


def project_first(hidden, weight):
    return call(
        project_first_kernel,
        jax.ShapeDtypeStruct((4 * BLOCK, HEAD_DIM), jnp.float32),
        [VMEM] * 6,
        (2**29, 5 * 2**20),
    )(*hidden, weight)


def project_second_kernel(*refs):
    where_ref, first_ref, cos_ref, sin_ref, out_ref, second = (refs[0],) + refs[7:]
    half = HEAD_DIM // 2
    multiply(refs[1:6], refs[6], second)
    x, keys_first = where_ref[0], where_ref[1] == 0
    for d in range(4):
        pack = (x - d) & 3
        one, two = first_ref[d * BLOCK : (d + 1) * BLOCK], second[d * BLOCK : (d + 1) * BLOCK]
        key = jnp.where(keys_first, one, two)
        value = jnp.where(keys_first, two, one)
        a, b = key[:, :half], key[:, half:]
        cosine, sine = cos_ref[pack], sin_ref[pack]
        turned = jnp.concatenate([a * cosine - b * sine, b * cosine + a * sine], axis=1)
        out_ref[pack, 0] = turned.astype(jnp.bfloat16)
        out_ref[pack, 1] = value.T.astype(jnp.bfloat16)


def project_second(where, hidden, weight, first, cosine, sine):
    return call(
        project_second_kernel,
        jax.ShapeDtypeStruct((4, 2, BLOCK, HEAD_DIM), jnp.bfloat16),
        [SMEM] + [VMEM] * 9,
        (2**29, 5 * 2**20),
        [pltpu.VMEM((4 * BLOCK, HEAD_DIM), jnp.float32)],
    )(where, *hidden, weight, first, cosine, sine)


def attend_kernel(tiles, opening, closing, where_ref, q_ref, start_ref, *refs):
    factor = math.log2(math.e) / math.sqrt(HEAD_DIM)
    y = where_ref[0]
    shifts = [shift for tile in tiles for shift in tile]
    kv, rest = dict(zip(shifts, refs)), refs[len(shifts) :]
    if not opening:
        given, rest = rest[:3], rest[3:]
    if closing:
        out_ref, acc, top, total = rest
    else:
        acc, top, total = rest

    @pl.loop(0, 4)
    def _(z):
        block = z * 8 + y
        slot = 0 if closing else z
        start = start_ref[z]
        row_at = block * BLOCK + lax.broadcasted_iota(jnp.int32, (BLOCK, BLOCK), 1)
        if opening:
            top[slot] = jnp.full(top.shape[1:], LOW, jnp.float32)
            total[slot] = jnp.zeros(total.shape[1:], jnp.float32)
            acc[slot] = jnp.zeros(acc.shape[1:], jnp.float32)
        else:
            for ref, source in zip((acc, top, total), given):
                ref[slot] = source[z]

        def turn(step, carry):
            zz = z - step
            for tile in tiles:
                places = [zz * 8 + ((y - shift) & 7) for shift in tile]
                needed = [
                    (place <= block) & ((place + 1) * BLOCK > where_ref[1 + z])
                    for place in places
                ]

                @pl.when(functools.reduce(jnp.logical_or, needed))
                def _():
                    key = jnp.concatenate([kv[shift][zz, 0] for shift in tile], axis=0)
                    val = jnp.concatenate([kv[shift][zz, 1] for shift in tile], axis=1)
                    allowed = []
                    for place in places:
                        at = place * BLOCK + lax.broadcasted_iota(jnp.int32, (BLOCK, BLOCK), 0)
                        allowed.append((at >= start) & (at <= row_at))
                    allowed = jnp.concatenate(allowed, axis=0)
                    for h in range(GROUP):
                        cols = slice(h * BLOCK, (h + 1) * BLOCK)
                        s = jnp.dot(key, q_ref[z, :, cols], preferred_element_type=jnp.float32)
                        s = jnp.where(allowed, s, LOW)
                        old = top[slot, :, cols]
                        new = jnp.maximum(old, jnp.max(s, axis=0, keepdims=True))
                        p = jnp.exp2((s - new) * factor)
                        scale = jnp.exp2((old - new) * factor)
                        top[slot, :, cols] = new
                        total[slot, :, cols] = total[slot, :, cols] * scale + jnp.sum(
                            p, axis=0, keepdims=True
                        )
                        acc[slot, :, cols] = acc[slot, :, cols] * scale + jnp.dot(
                            val, p.astype(jnp.bfloat16), preferred_element_type=jnp.float32
                        )

            return carry

        lax.fori_loop(0, z + 1, turn, 0)
        if closing:
            for h in range(GROUP):
                cols = slice(h * BLOCK, (h + 1) * BLOCK)
                mixed = acc[slot, :, cols] / total[slot, :, cols]
                out_ref[z, :, cols] = mixed.T.astype(jnp.bfloat16)


def attend(tiles, where, q, start, kv, state=None, closing=False):
    rows = GROUP * BLOCK
    slots = 1 if closing else 4
    shapes = [(slots, HEAD_DIM, rows), (slots, 1, rows), (slots, 1, rows)]
    held = [jax.ShapeDtypeStruct(shape, jnp.float32) for shape in shapes]
    given = [] if state is None else list(state)
    shifts = [shift for tile in tiles for shift in tile]
    out = jax.ShapeDtypeStruct((4, BLOCK, rows), jnp.bfloat16)
    return call(
        functools.partial(attend_kernel, tiles, state is None, closing),
        out if closing else held,
        [SMEM] + [VMEM] * (2 + len(shifts) + len(given)),
        (len(shifts) * 2**30, 4 * 2**20),
        [pltpu.VMEM(shape, jnp.float32) for shape in shapes] if closing else (),
    )(where, q, start, *[kv[shift] for shift in shifts], *given)


def on_device(hidden, queries, weight_copies, segment_ids, owner):
    y, z = lax.axis_index(Y), lax.axis_index(Z)
    x, c, zh = lax.axis_index("x"), lax.axis_index("c"), lax.axis_index("zh")
    segment_row = segment_ids[0]
    origin = owner[0] % 16

    pieces = weight_copies[0].reshape(BLOCK, 2, 4, 128).transpose(2, 1, 0, 3)
    row = segment_row.astype(jnp.bfloat16).reshape(1, 1, 32, 128)
    pieces = jnp.concatenate([pieces, jnp.broadcast_to(row, (4, 2, 32, 128))], axis=2)
    got = exchange(pieces.reshape(8, 160, 128), ("x", "c"))
    piece = pick(got[:, :BLOCK], origin % 8)
    rows_along = pick(got.reshape(4, 2, 160, 128)[:, :, BLOCK:], c, 1)
    piece = jnp.where(zh == origin // 8, piece, lax.ppermute(piece, "zh", ring(2, 1)))
    part = spread(piece, ("z1", "y1"), 8).reshape(8 * BLOCK, 128)
    mine = spread(part, ("z0", "y0"), 4).reshape(32, BLOCK, 128)
    other = lax.ppermute(mine, "c", ring(2, 1))

    own = hidden[0]
    left = lax.ppermute(own, "x", ring(4, 1))
    right = lax.ppermute(own, "x", ring(4, -1))
    far0 = lax.ppermute(left[:64], "x", ring(4, 1))
    far1 = lax.ppermute(right[64:], "x", ring(4, -1))
    rows = [own, left, far0, far1, right]

    after_part = lax.optimization_barrier((queries[0], part))[0].reshape(BLOCK, 4, -1)
    q_parts = []
    for d in range(4):
        chunk = pick(after_part, (z + d) % 4, 1)
        q_parts.append(lax.ppermute(chunk, Z, ring(4, d)) if d else chunk)

    blocks = segment_row.reshape(4, 8, BLOCK)
    start = starts_of(segment_row, pick(blocks, y, 1))
    token = (jnp.arange(4)[:, None] * 8 + y) * BLOCK + jnp.arange(BLOCK)[None]
    q_angles = jnp.swapaxes(angles_of(token - start), 1, 2)
    q_turned = turn_queries(
        z[None].astype(jnp.int32), q_parts, jnp.cos(q_angles), jnp.sin(q_angles)
    )

    rows_along = rows_along.astype(jnp.int32)
    along = pick(rows_along, z * 8 + y, 1)
    start_along = jax.vmap(starts_of)(rows_along, along)
    k_angles = angles_of((z * 8 + y) * BLOCK + jnp.arange(BLOCK)[None] - start_along)

    first = project_first(rows, mine)
    both = project_second(
        jnp.stack([x, c]).astype(jnp.int32), rows, other, first, jnp.cos(k_angles), jnp.sin(k_angles)
    )
    own_kv = exchange(exchange(both, "x"), Z)

    kv = {0: own_kv}
    for step in range(1, 5):
        kv[step] = lax.ppermute(kv[step - 1], Y, ring(8, 1))
        if step < 4:
            kv[-step] = lax.ppermute(kv[1 - step], Y, ring(8, -1))
    where = jnp.concatenate([y[None], start[:, 0]]).astype(jnp.int32)
    start = start[:, None, :]
    state = attend(((0,), (1, 2), (-1, -2)), where, q_turned, start, kv)
    mixed = attend(((-3,), (3, 4)), where, q_turned, start, kv, state, closing=True)
    back = exchange(mixed, Z)
    return back.transpose(1, 0, 2).reshape(1, BLOCK, HEADS * HEAD_DIM)


def solution(mesh):
    fine = Mesh(mesh.devices.reshape(SIZES), AXES)
    placed = (
        P(REP, SEQ, None),
        P(REP, SEQ, None),
        P(REP, SEQ, None),
        P(REP, None),
        P(),
    )
    return jax.shard_map(
        on_device, mesh=fine, in_specs=placed, out_specs=P(REP, SEQ, None), check_vma=False
    )
```

```python
import functools
import math

import jax
import jax.numpy as jnp
from jax import lax
from jax.experimental import pallas as pl
from jax.experimental.pallas import tpu as pltpu
from jax.sharding import Mesh
from jax.sharding import PartitionSpec as P

HEADS = 32
KV_HEADS = 4
HEAD_DIM = 128
GROUP = HEADS // KV_HEADS
THETA = 1000000.0
BLOCK = 128
LOW = -1e30
DOCS = 6

AXES = ("z1", "z0", "y1", "y0", "zh", "x", "c")
SIZES = (2, 2, 4, 2, 2, 4, 2)
SEQ = ("z1", "z0", "y1", "y0")
REP = ("zh", "x", "c")
Y = ("y1", "y0")
Z = ("z1", "z0")


def ring(size, shift):
    return [(i, (i + shift) % size) for i in range(size)]


def pick(value, index, axis=0):
    return lax.dynamic_index_in_dim(value, index, axis, keepdims=False)


def exchange(value, axes):
    return lax.all_to_all(value, axes, split_axis=0, concat_axis=0, tiled=True)


def spread(value, axes, members):
    return exchange(jnp.broadcast_to(value[None], (members,) + value.shape), axes)


def angles_of(positions):
    half = HEAD_DIM // 2
    freqs = THETA ** (-(jnp.arange(half, dtype=jnp.float32) * 2.0) / HEAD_DIM)
    return positions.astype(jnp.float32)[..., None] * freqs


def starts_of(segment_row, segments):
    first = jnp.zeros(segments.shape, jnp.int32)
    for doc in range(1, DOCS):
        begin = jnp.sum((segment_row < doc).astype(jnp.int32))
        first = jnp.where(segments >= doc, begin, first)
    return first


VMEM = pl.BlockSpec(memory_space=pltpu.VMEM)
SMEM = pl.BlockSpec(memory_space=pltpu.SMEM)


def call(kernel, out_shape, specs, cost, scratch=()):
    flops, moved = cost
    return pl.pallas_call(
        kernel,
        out_shape=out_shape,
        in_specs=specs,
        out_specs=jax.tree.map(lambda _: VMEM, out_shape),
        scratch_shapes=list(scratch),
        compiler_params=pltpu.CompilerParams(vmem_limit_bytes=32 * 2**20),
        cost_estimate=pl.CostEstimate(flops=flops, bytes_accessed=moved, transcendentals=0),
    )


def turn_kernel(where_ref, *refs):
    parts, (cos_ref, sin_ref, out_ref) = refs[:4], refs[4:]
    half = HEAD_DIM // 2
    for d in range(4):
        z = (where_ref[0] - d) & 3
        cosine, sine = cos_ref[z], sin_ref[z]
        for h in range(GROUP):
            cols = slice(h * HEAD_DIM, (h + 1) * HEAD_DIM)
            t = parts[d][:, cols].astype(jnp.float32).T
            a, b = t[:half], t[half:]
            out_ref[z, :half, cols] = (a * cosine - b * sine).astype(jnp.bfloat16)
            out_ref[z, half:, cols] = (b * cosine + a * sine).astype(jnp.bfloat16)


def turn_queries(where, parts, cosine, sine):
    return call(
        turn_kernel,
        jax.ShapeDtypeStruct((4, HEAD_DIM, GROUP * BLOCK), jnp.bfloat16),
        [SMEM] + [VMEM] * 6,
        (4 * 2**20, 2 * 2**20),
    )(where, *parts, cosine, sine)


def multiply(hidden_refs, weight_ref, out_ref):
    at = 0
    for hidden_ref in hidden_refs:
        total = None
        for block in range(0, 32, 2):
            z1, z0, y1 = block // 16, block // 8 % 2, block // 2 % 4
            low = z0 * 16 + z1 * 4 + y1
            weight = jnp.concatenate([weight_ref[low], weight_ref[low + 8]], axis=0)
            term = jnp.dot(
                hidden_ref[:, block * 128 : block * 128 + 256],
                weight,
                preferred_element_type=jnp.float32,
            )
            total = term if total is None else total + term
        out_ref[at : at + hidden_ref.shape[0]] = total
        at += hidden_ref.shape[0]


def project_first_kernel(*refs):
    multiply(refs[:7], refs[7], refs[8])


def project_first(hidden, weight):
    return call(
        project_first_kernel,
        jax.ShapeDtypeStruct((4 * BLOCK, HEAD_DIM), jnp.float32),
        [VMEM] * 8,
        (2**29, 5 * 2**20),
    )(*hidden, weight)


def project_second_kernel(*refs):
    where_ref, first_ref, cos_ref, sin_ref, out_ref, second = (refs[0],) + refs[9:]
    half = HEAD_DIM // 2
    multiply(refs[1:8], refs[8], second)
    x, keys_first = where_ref[0], where_ref[1] == 0
    for d in range(4):
        pack = (x - d) & 3
        one, two = first_ref[d * BLOCK : (d + 1) * BLOCK], second[d * BLOCK : (d + 1) * BLOCK]
        key = jnp.where(keys_first, one, two)
        value = jnp.where(keys_first, two, one)
        a, b = key[:, :half], key[:, half:]
        cosine, sine = cos_ref[pack], sin_ref[pack]
        turned = jnp.concatenate([a * cosine - b * sine, b * cosine + a * sine], axis=1)
        out_ref[pack, 0] = turned.astype(jnp.bfloat16)
        out_ref[pack, 1] = value.T.astype(jnp.bfloat16)


def project_second(where, hidden, weight, first, cosine, sine):
    return call(
        project_second_kernel,
        jax.ShapeDtypeStruct((4, 2, BLOCK, HEAD_DIM), jnp.bfloat16),
        [SMEM] + [VMEM] * 11,
        (2**29, 5 * 2**20),
        [pltpu.VMEM((4 * BLOCK, HEAD_DIM), jnp.float32)],
    )(where, *hidden, weight, first, cosine, sine)


def attend_kernel(tiles, opening, closing, where_ref, q_ref, start_ref, *refs):
    factor = math.log2(math.e) / math.sqrt(HEAD_DIM)
    y = where_ref[0]
    shifts = [shift for tile in tiles for shift in tile]
    kv, rest = dict(zip(shifts, refs)), refs[len(shifts) :]
    if not opening:
        given, rest = rest[:3], rest[3:]
    if closing:
        out_ref, acc, top, total = rest
    else:
        acc, top, total = rest

    @pl.loop(0, 4)
    def _(z):
        block = z * 8 + y
        slot = 0 if closing else z
        start = start_ref[z]
        row_at = block * BLOCK + lax.broadcasted_iota(jnp.int32, (BLOCK, BLOCK), 1)
        if opening:
            top[slot] = jnp.full(top.shape[1:], LOW, jnp.float32)
            total[slot] = jnp.zeros(total.shape[1:], jnp.float32)
            acc[slot] = jnp.zeros(acc.shape[1:], jnp.float32)
        else:
            for ref, source in zip((acc, top, total), given):
                ref[slot] = source[z]

        def turn(step, carry):
            zz = z - step
            for tile in tiles:
                places = [zz * 8 + ((y - shift) & 7) for shift in tile]
                needed = [
                    (place <= block) & ((place + 1) * BLOCK > where_ref[1 + z])
                    for place in places
                ]

                @pl.when(functools.reduce(jnp.logical_or, needed))
                def _():
                    key = jnp.concatenate([kv[shift][zz, 0] for shift in tile], axis=0)
                    val = jnp.concatenate([kv[shift][zz, 1] for shift in tile], axis=1)
                    allowed = []
                    for place in places:
                        at = place * BLOCK + lax.broadcasted_iota(jnp.int32, (BLOCK, BLOCK), 0)
                        allowed.append((at >= start) & (at <= row_at))
                    allowed = jnp.concatenate(allowed, axis=0)
                    for h in range(GROUP):
                        cols = slice(h * BLOCK, (h + 1) * BLOCK)
                        s = jnp.dot(key, q_ref[z, :, cols], preferred_element_type=jnp.float32)
                        s = jnp.where(allowed, s, LOW)
                        old = top[slot, :, cols]
                        new = jnp.maximum(old, jnp.max(s, axis=0, keepdims=True))
                        p = jnp.exp2((s - new) * factor)
                        scale = jnp.exp2((old - new) * factor)
                        top[slot, :, cols] = new
                        total[slot, :, cols] = total[slot, :, cols] * scale + jnp.sum(
                            p, axis=0, keepdims=True
                        )
                        acc[slot, :, cols] = acc[slot, :, cols] * scale + jnp.dot(
                            val, p.astype(jnp.bfloat16), preferred_element_type=jnp.float32
                        )

            return carry

        lax.fori_loop(0, z + 1, turn, 0)
        if closing:
            for h in range(GROUP):
                cols = slice(h * BLOCK, (h + 1) * BLOCK)
                mixed = acc[slot, :, cols] / total[slot, :, cols]
                out_ref[z, :, cols] = mixed.T.astype(jnp.bfloat16)


def attend(tiles, where, q, start, kv, state=None, closing=False):
    rows = GROUP * BLOCK
    slots = 1 if closing else 4
    shapes = [(slots, HEAD_DIM, rows), (slots, 1, rows), (slots, 1, rows)]
    held = [jax.ShapeDtypeStruct(shape, jnp.float32) for shape in shapes]
    given = [] if state is None else list(state)
    shifts = [shift for tile in tiles for shift in tile]
    out = jax.ShapeDtypeStruct((4, BLOCK, rows), jnp.bfloat16)
    return call(
        functools.partial(attend_kernel, tiles, state is None, closing),
        out if closing else held,
        [SMEM] + [VMEM] * (2 + len(shifts) + len(given)),
        (len(shifts) * 2**30, 4 * 2**20),
        [pltpu.VMEM(shape, jnp.float32) for shape in shapes] if closing else (),
    )(where, q, start, *[kv[shift] for shift in shifts], *given)


def on_device(hidden, queries, weight_copies, segment_ids, owner):
    y, z = lax.axis_index(Y), lax.axis_index(Z)
    x, c, zh = lax.axis_index("x"), lax.axis_index("c"), lax.axis_index("zh")
    segment_row = segment_ids[0]
    origin = owner[0] % 16

    pieces = weight_copies[0].reshape(BLOCK, 2, 4, 128).transpose(2, 1, 0, 3)
    row = segment_row.astype(jnp.bfloat16).reshape(1, 1, 32, 128)
    pieces = jnp.concatenate([pieces, jnp.broadcast_to(row, (4, 2, 32, 128))], axis=2)
    got = exchange(pieces.reshape(8, 160, 128), ("x", "c"))
    piece = pick(got[:, :BLOCK], origin % 8)
    rows_along = pick(got.reshape(4, 2, 160, 128)[:, :, BLOCK:], c, 1)
    piece = jnp.where(zh == origin // 8, piece, lax.ppermute(piece, "zh", ring(2, 1)))

    own = hidden[0]
    low, high = own[:64], own[64:]
    left_low = lax.ppermute(low, "x", ring(4, 1))
    right_high = lax.ppermute(high, "x", ring(4, -1))
    piece, left_low, right_high = lax.optimization_barrier((piece, left_low, right_high))
    part = spread(piece, ("z1", "y1"), 8).reshape(8 * BLOCK, 128)
    left_high = lax.ppermute(high, "x", ring(4, 1))
    right_low = lax.ppermute(low, "x", ring(4, -1))
    far_low = lax.ppermute(left_low, "x", ring(4, 1))
    far_high = lax.ppermute(right_high, "x", ring(4, -1))
    part, left_high, right_low, far_low, far_high = lax.optimization_barrier(
        (part, left_high, right_low, far_low, far_high)
    )
    mine = spread(part, ("z0", "y0"), 4).reshape(32, BLOCK, 128)
    rows = [own, left_low, left_high, far_low, far_high, right_low, right_high]

    chunks = [
        lax.dynamic_slice_in_dim(queries[0], (z + d) % 4 * GROUP * HEAD_DIM, GROUP * HEAD_DIM, 1)
        for d in range(4)
    ]
    mine, *chunks = lax.optimization_barrier((mine, *chunks))
    q_parts = [lax.ppermute(chunk, Z, ring(4, d)) if d else chunk for d, chunk in enumerate(chunks)]
    other = lax.ppermute(mine, "c", ring(2, 1))

    blocks = segment_row.reshape(4, 8, BLOCK)
    start = starts_of(segment_row, pick(blocks, y, 1))
    token = (jnp.arange(4)[:, None] * 8 + y) * BLOCK + jnp.arange(BLOCK)[None]
    q_angles = jnp.swapaxes(angles_of(token - start), 1, 2)

    rows_along = rows_along.astype(jnp.int32)
    along = pick(rows_along, z * 8 + y, 1)
    start_along = jax.vmap(starts_of)(rows_along, along)
    k_angles = angles_of((z * 8 + y) * BLOCK + jnp.arange(BLOCK)[None] - start_along)

    first = project_first(rows, mine)
    both = project_second(
        jnp.stack([x, c]).astype(jnp.int32), rows, other, first, jnp.cos(k_angles), jnp.sin(k_angles)
    )
    near, *q_parts = lax.optimization_barrier((exchange(both, "x"), *q_parts))
    q_turned = turn_queries(
        z[None].astype(jnp.int32), q_parts, jnp.cos(q_angles), jnp.sin(q_angles)
    )
    own_kv = exchange(near, Z)

    where = jnp.concatenate([y[None], start[:, 0]]).astype(jnp.int32)
    start = start[:, None, :]
    kv = {0: own_kv}
    for step in range(1, 5):
        if step == 4:
            state = attend(((0,), (1, 2), (-1, -2)), where, q_turned, start, kv)
            kv[3], kv[-3], *state = lax.optimization_barrier((kv[3], kv[-3], *state))
        kv[step] = lax.ppermute(kv[step - 1], Y, ring(8, 1))
        if step < 4:
            kv[-step] = lax.ppermute(kv[1 - step], Y, ring(8, -1))
    state = attend(((3,), (-3,)), where, q_turned, start, kv, state)
    mixed = attend(((4,),), where, q_turned, start, kv, state, closing=True)
    back = exchange(mixed, Z)
    return back.transpose(1, 0, 2).reshape(1, BLOCK, HEADS * HEAD_DIM)


def solution(mesh):
    fine = Mesh(mesh.devices.reshape(SIZES), AXES)
    placed = (
        P(REP, SEQ, None),
        P(REP, SEQ, None),
        P(REP, SEQ, None),
        P(REP, None),
        P(),
    )
    return jax.shard_map(
        on_device, mesh=fine, in_specs=placed, out_specs=P(REP, SEQ, None), check_vma=False
    )
```

```python
import functools
import math

import jax
import jax.numpy as jnp
from jax import lax
from jax.experimental import pallas as pl
from jax.experimental.pallas import tpu as pltpu
from jax.sharding import Mesh
from jax.sharding import PartitionSpec as P

HEADS = 32
KV_HEADS = 4
HEAD_DIM = 128
GROUP = HEADS // KV_HEADS
THETA = 1000000.0
BLOCK = 128
LOW = -1e30
DOCS = 6

AXES = ("z1", "z0", "y1", "y0", "zh", "x", "c")
SIZES = (2, 2, 4, 2, 2, 4, 2)
SEQ = ("z1", "z0", "y1", "y0")
REP = ("zh", "x", "c")
Y = ("y1", "y0")
Z = ("z1", "z0")


def ring(size, shift):
    return [(i, (i + shift) % size) for i in range(size)]


def pick(value, index, axis=0):
    return lax.dynamic_index_in_dim(value, index, axis, keepdims=False)


def exchange(value, axes):
    return lax.all_to_all(value, axes, split_axis=0, concat_axis=0, tiled=True)


def spread(value, axes, members):
    return exchange(jnp.broadcast_to(value[None], (members,) + value.shape), axes)


def angles_of(positions):
    half = HEAD_DIM // 2
    freqs = THETA ** (-(jnp.arange(half, dtype=jnp.float32) * 2.0) / HEAD_DIM)
    return positions.astype(jnp.float32)[..., None] * freqs


def starts_of(segment_row, segments):
    first = jnp.zeros(segments.shape, jnp.int32)
    for doc in range(1, DOCS):
        begin = jnp.sum((segment_row < doc).astype(jnp.int32))
        first = jnp.where(segments >= doc, begin, first)
    return first


VMEM = pl.BlockSpec(memory_space=pltpu.VMEM)
SMEM = pl.BlockSpec(memory_space=pltpu.SMEM)


def call(kernel, out_shape, specs, cost, scratch=()):
    flops, moved = cost
    return pl.pallas_call(
        kernel,
        out_shape=out_shape,
        in_specs=specs,
        out_specs=jax.tree.map(lambda _: VMEM, out_shape),
        scratch_shapes=list(scratch),
        compiler_params=pltpu.CompilerParams(vmem_limit_bytes=32 * 2**20),
        cost_estimate=pl.CostEstimate(flops=flops, bytes_accessed=moved, transcendentals=0),
    )


def turn_kernel(q_ref, cos_ref, sin_ref, out_ref):
    half = HEAD_DIM // 2

    @pl.loop(0, 4)
    def _(z):
        cosine, sine = cos_ref[z], sin_ref[z]
        for h in range(GROUP):
            cols = slice(h * HEAD_DIM, (h + 1) * HEAD_DIM)
            t = q_ref[z, :, cols].astype(jnp.float32).T
            a, b = t[:half], t[half:]
            out_ref[z, :half, cols] = (a * cosine - b * sine).astype(jnp.bfloat16)
            out_ref[z, half:, cols] = (b * cosine + a * sine).astype(jnp.bfloat16)


def turn_queries(q, cosine, sine):
    return call(
        turn_kernel,
        jax.ShapeDtypeStruct((4, HEAD_DIM, GROUP * BLOCK), jnp.bfloat16),
        [VMEM] * 3,
        (4 * 2**20, 2 * 2**20),
    )(q, cosine, sine)


def multiply(hidden_refs, weight_ref, out_ref):
    at = 0
    for hidden_ref in hidden_refs:
        total = None
        for block in range(0, 32, 2):
            z1, z0, y1 = block // 16, block // 8 % 2, block // 2 % 4
            low = z0 * 16 + z1 * 4 + y1
            weight = jnp.concatenate([weight_ref[low], weight_ref[low + 8]], axis=0)
            term = jnp.dot(
                hidden_ref[:, block * 128 : block * 128 + 256],
                weight,
                preferred_element_type=jnp.float32,
            )
            total = term if total is None else total + term
        out_ref[at : at + hidden_ref.shape[0]] = total
        at += hidden_ref.shape[0]


def project_first_kernel(*refs):
    multiply(refs[:5], refs[5], refs[6])


def project_first(hidden, weight):
    return call(
        project_first_kernel,
        jax.ShapeDtypeStruct((4 * BLOCK, HEAD_DIM), jnp.float32),
        [VMEM] * 6,
        (2**29, 5 * 2**20),
    )(*hidden, weight)


def project_second_kernel(*refs):
    where_ref, first_ref, cos_ref, sin_ref, out_ref, second = (refs[0],) + refs[7:]
    half = HEAD_DIM // 2
    multiply(refs[1:6], refs[6], second)
    x, keys_first = where_ref[0], where_ref[1] == 0
    for d in range(4):
        pack = (x - d) & 3
        one, two = first_ref[d * BLOCK : (d + 1) * BLOCK], second[d * BLOCK : (d + 1) * BLOCK]
        key = jnp.where(keys_first, one, two)
        value = jnp.where(keys_first, two, one)
        a, b = key[:, :half], key[:, half:]
        cosine, sine = cos_ref[pack], sin_ref[pack]
        turned = jnp.concatenate([a * cosine - b * sine, b * cosine + a * sine], axis=1)
        out_ref[pack, 0] = turned.astype(jnp.bfloat16)
        out_ref[pack, 1] = value.T.astype(jnp.bfloat16)


def project_second(where, hidden, weight, first, cosine, sine):
    return call(
        project_second_kernel,
        jax.ShapeDtypeStruct((4, 2, BLOCK, HEAD_DIM), jnp.bfloat16),
        [SMEM] + [VMEM] * 9,
        (2**29, 5 * 2**20),
        [pltpu.VMEM((4 * BLOCK, HEAD_DIM), jnp.float32)],
    )(where, *hidden, weight, first, cosine, sine)


def attend_kernel(tiles, opening, closing, where_ref, q_ref, start_ref, *refs):
    factor = math.log2(math.e) / math.sqrt(HEAD_DIM)
    y = where_ref[0]
    shifts = [shift for tile in tiles for shift in tile]
    kv, rest = dict(zip(shifts, refs)), refs[len(shifts) :]
    if not opening:
        given, rest = rest[:3], rest[3:]
    if closing:
        out_ref, acc, top, total = rest
    else:
        acc, top, total = rest

    @pl.loop(0, 4)
    def _(z):
        block = z * 8 + y
        slot = 0 if closing else z
        start = start_ref[z]
        row_at = block * BLOCK + lax.broadcasted_iota(jnp.int32, (BLOCK, BLOCK), 1)
        if opening:
            top[slot] = jnp.full(top.shape[1:], LOW, jnp.float32)
            total[slot] = jnp.zeros(total.shape[1:], jnp.float32)
            acc[slot] = jnp.zeros(acc.shape[1:], jnp.float32)
        else:
            for ref, source in zip((acc, top, total), given):
                ref[slot] = source[z]

        def turn(step, carry):
            zz = z - step
            for tile in tiles:
                places = [zz * 8 + ((y - shift) & 7) for shift in tile]
                needed = [
                    (place <= block) & ((place + 1) * BLOCK > where_ref[1 + z])
                    for place in places
                ]

                @pl.when(functools.reduce(jnp.logical_or, needed))
                def _():
                    key = jnp.concatenate([kv[shift][zz, 0] for shift in tile], axis=0)
                    val = jnp.concatenate([kv[shift][zz, 1] for shift in tile], axis=1)
                    allowed = []
                    for place in places:
                        at = place * BLOCK + lax.broadcasted_iota(jnp.int32, (BLOCK, BLOCK), 0)
                        allowed.append((at >= start) & (at <= row_at))
                    allowed = jnp.concatenate(allowed, axis=0)
                    for h in range(GROUP):
                        cols = slice(h * BLOCK, (h + 1) * BLOCK)
                        s = jnp.dot(key, q_ref[z, :, cols], preferred_element_type=jnp.float32)
                        s = jnp.where(allowed, s, LOW)
                        old = top[slot, :, cols]
                        new = jnp.maximum(old, jnp.max(s, axis=0, keepdims=True))
                        p = jnp.exp2((s - new) * factor)
                        scale = jnp.exp2((old - new) * factor)
                        top[slot, :, cols] = new
                        total[slot, :, cols] = total[slot, :, cols] * scale + jnp.sum(
                            p, axis=0, keepdims=True
                        )
                        acc[slot, :, cols] = acc[slot, :, cols] * scale + jnp.dot(
                            val, p.astype(jnp.bfloat16), preferred_element_type=jnp.float32
                        )

            return carry

        lax.fori_loop(0, z + 1, turn, 0)
        if closing:
            for h in range(GROUP):
                cols = slice(h * BLOCK, (h + 1) * BLOCK)
                mixed = acc[slot, :, cols] / total[slot, :, cols]
                out_ref[z, :, cols] = mixed.T.astype(jnp.bfloat16)


def attend(tiles, where, q, start, kv, state=None, closing=False):
    rows = GROUP * BLOCK
    slots = 1 if closing else 4
    shapes = [(slots, HEAD_DIM, rows), (slots, 1, rows), (slots, 1, rows)]
    held = [jax.ShapeDtypeStruct(shape, jnp.float32) for shape in shapes]
    given = [] if state is None else list(state)
    shifts = [shift for tile in tiles for shift in tile]
    out = jax.ShapeDtypeStruct((4, BLOCK, rows), jnp.bfloat16)
    return call(
        functools.partial(attend_kernel, tiles, state is None, closing),
        out if closing else held,
        [SMEM] + [VMEM] * (2 + len(shifts) + len(given)),
        (len(shifts) * 2**30, 4 * 2**20),
        [pltpu.VMEM(shape, jnp.float32) for shape in shapes] if closing else (),
    )(where, q, start, *[kv[shift] for shift in shifts], *given)


def on_device(hidden, queries, weight_copies, segment_ids, owner):
    y, z = lax.axis_index(Y), lax.axis_index(Z)
    x, c, zh = lax.axis_index("x"), lax.axis_index("c"), lax.axis_index("zh")
    segment_row = segment_ids[0]
    origin = owner[0] % 16

    pieces = weight_copies[0].reshape(BLOCK, 2, 4, 128).transpose(2, 1, 0, 3)
    row = segment_row.astype(jnp.bfloat16).reshape(1, 1, 32, 128)
    pieces = jnp.concatenate([pieces, jnp.broadcast_to(row, (4, 2, 32, 128))], axis=2)
    got = exchange(pieces.reshape(8, 160, 128), ("x", "c"))
    piece = pick(got[:, :BLOCK], origin % 8)
    rows_along = pick(got.reshape(4, 2, 160, 128)[:, :, BLOCK:], c, 1)
    piece = jnp.where(zh == origin // 8, piece, lax.ppermute(piece, "zh", ring(2, 1)))

    own = hidden[0]
    left = lax.ppermute(own, "x", ring(4, 1))
    right = lax.ppermute(own, "x", ring(4, -1))
    part = spread(piece, ("z1", "y1"), 8).reshape(8 * BLOCK, 128)
    part, left, right = lax.optimization_barrier((part, left, right))
    mine = spread(part, ("z0", "y0"), 4).reshape(32, BLOCK, 128)
    other = lax.ppermute(mine, "c", ring(2, 1))
    far_low = lax.ppermute(left[:64], "x", ring(4, 1))
    far_high = lax.ppermute(right[64:], "x", ring(4, -1))
    rows = [own, left, far_low, far_high, right]

    blocks = segment_row.reshape(4, 8, BLOCK)
    start = starts_of(segment_row, pick(blocks, y, 1))
    token = (jnp.arange(4)[:, None] * 8 + y) * BLOCK + jnp.arange(BLOCK)[None]
    q_angles = jnp.swapaxes(angles_of(token - start), 1, 2)

    rows_along = rows_along.astype(jnp.int32)
    along = pick(rows_along, z * 8 + y, 1)
    start_along = jax.vmap(starts_of)(rows_along, along)
    k_angles = angles_of((z * 8 + y) * BLOCK + jnp.arange(BLOCK)[None] - start_along)

    first = project_first(rows, mine)
    both = project_second(
        jnp.stack([x, c]).astype(jnp.int32), rows, other, first, jnp.cos(k_angles), jnp.sin(k_angles)
    )
    own_kv = exchange(exchange(both, "x"), Z)

    split = queries[0].reshape(BLOCK, 4, GROUP * HEAD_DIM).transpose(1, 0, 2)
    own_kv, split = lax.optimization_barrier((own_kv, split))
    q_turned = turn_queries(exchange(split, Z), jnp.cos(q_angles), jnp.sin(q_angles))

    where = jnp.concatenate([y[None], start[:, 0]]).astype(jnp.int32)
    start = start[:, None, :]
    kv = {0: own_kv}
    for step in range(1, 5):
        if step == 4:
            state = attend(((0,), (1, 2), (-1, -2)), where, q_turned, start, kv)
            kv[3], kv[-3], *state = lax.optimization_barrier((kv[3], kv[-3], *state))
        kv[step] = lax.ppermute(kv[step - 1], Y, ring(8, 1))
        if step < 4:
            kv[-step] = lax.ppermute(kv[1 - step], Y, ring(8, -1))
    state = attend(((3,), (-3,)), where, q_turned, start, kv, state)
    mixed = attend(((4,),), where, q_turned, start, kv, state, closing=True)
    back = exchange(mixed, Z)
    return back.transpose(1, 0, 2).reshape(1, BLOCK, HEADS * HEAD_DIM)


def solution(mesh):
    fine = Mesh(mesh.devices.reshape(SIZES), AXES)
    placed = (
        P(REP, SEQ, None),
        P(REP, SEQ, None),
        P(REP, SEQ, None),
        P(REP, None),
        P(),
    )
    return jax.shard_map(
        on_device, mesh=fine, in_specs=placed, out_specs=P(REP, SEQ, None), check_vma=False
    )
```

```python
import functools
import math

import jax
import jax.numpy as jnp
from jax import lax
from jax.experimental import pallas as pl
from jax.experimental.pallas import tpu as pltpu
from jax.sharding import Mesh
from jax.sharding import PartitionSpec as P

HEADS = 32
KV_HEADS = 4
HEAD_DIM = 128
GROUP = HEADS // KV_HEADS
THETA = 1000000.0
BLOCK = 128
LOW = -1e30
DOCS = 6
FAR_LOW, FAR_HIGH = 4, -4

AXES = ("z1", "z0", "y1", "y0", "zh", "x", "c")
SIZES = (2, 2, 4, 2, 2, 4, 2)
SEQ = ("z1", "z0", "y1", "y0")
REP = ("zh", "x", "c")
Y = ("y1", "y0")
Z = ("z1", "z0")


def ring(size, shift):
    return [(i, (i + shift) % size) for i in range(size)]


def pick(value, index, axis=0):
    return lax.dynamic_index_in_dim(value, index, axis, keepdims=False)


def exchange(value, axes):
    return lax.all_to_all(value, axes, split_axis=0, concat_axis=0, tiled=True)


def spread(value, axes, members):
    return exchange(jnp.broadcast_to(value[None], (members,) + value.shape), axes)


def angles_of(positions):
    half = HEAD_DIM // 2
    freqs = THETA ** (-(jnp.arange(half, dtype=jnp.float32) * 2.0) / HEAD_DIM)
    return positions.astype(jnp.float32)[..., None] * freqs


def starts_of(segment_row, segments):
    first = jnp.zeros(segments.shape, jnp.int32)
    for doc in range(1, DOCS):
        begin = jnp.sum((segment_row < doc).astype(jnp.int32))
        first = jnp.where(segments >= doc, begin, first)
    return first


VMEM = pl.BlockSpec(memory_space=pltpu.VMEM)
SMEM = pl.BlockSpec(memory_space=pltpu.SMEM)


def call(kernel, out_shape, specs, cost, scratch=()):
    flops, moved = cost
    return pl.pallas_call(
        kernel,
        out_shape=out_shape,
        in_specs=specs,
        out_specs=jax.tree.map(lambda _: VMEM, out_shape),
        scratch_shapes=list(scratch),
        compiler_params=pltpu.CompilerParams(vmem_limit_bytes=32 * 2**20),
        cost_estimate=pl.CostEstimate(flops=flops, bytes_accessed=moved, transcendentals=0),
    )


def turn_kernel(q_ref, cos_ref, sin_ref, out_ref):
    half = HEAD_DIM // 2

    @pl.loop(0, 4)
    def _(z):
        cosine, sine = cos_ref[z], sin_ref[z]
        for h in range(GROUP):
            cols = slice(h * HEAD_DIM, (h + 1) * HEAD_DIM)
            t = q_ref[z, :, cols].astype(jnp.float32).T
            a, b = t[:half], t[half:]
            out_ref[z, :half, cols] = (a * cosine - b * sine).astype(jnp.bfloat16)
            out_ref[z, half:, cols] = (b * cosine + a * sine).astype(jnp.bfloat16)


def turn_queries(q, cosine, sine):
    return call(
        turn_kernel,
        jax.ShapeDtypeStruct((4, HEAD_DIM, GROUP * BLOCK), jnp.bfloat16),
        [VMEM] * 3,
        (4 * 2**20, 2 * 2**20),
    )(q, cosine, sine)


def multiply(hidden_refs, weight_ref, out_ref):
    at = 0
    for hidden_ref in hidden_refs:
        total = None
        for block in range(0, 32, 2):
            z1, z0, y1 = block // 16, block // 8 % 2, block // 2 % 4
            low = z0 * 16 + z1 * 4 + y1
            weight = jnp.concatenate([weight_ref[low], weight_ref[low + 8]], axis=0)
            term = jnp.dot(
                hidden_ref[:, block * 128 : block * 128 + 256],
                weight,
                preferred_element_type=jnp.float32,
            )
            total = term if total is None else total + term
        out_ref[at : at + hidden_ref.shape[0]] = total
        at += hidden_ref.shape[0]


def project_first_kernel(*refs):
    multiply(refs[:5], refs[5], refs[6])


def project_first(hidden, weight):
    return call(
        project_first_kernel,
        jax.ShapeDtypeStruct((4 * BLOCK, HEAD_DIM), jnp.float32),
        [VMEM] * 6,
        (2**29, 5 * 2**20),
    )(*hidden, weight)


def project_second_kernel(*refs):
    where_ref, first_ref, cos_ref, sin_ref, out_ref, second = (refs[0],) + refs[7:]
    half = HEAD_DIM // 2
    multiply(refs[1:6], refs[6], second)
    x, keys_first = where_ref[0], where_ref[1] == 0
    for d in range(4):
        pack = (x - d) & 3
        one, two = first_ref[d * BLOCK : (d + 1) * BLOCK], second[d * BLOCK : (d + 1) * BLOCK]
        key = jnp.where(keys_first, one, two)
        value = jnp.where(keys_first, two, one)
        a, b = key[:, :half], key[:, half:]
        cosine, sine = cos_ref[pack], sin_ref[pack]
        turned = jnp.concatenate([a * cosine - b * sine, b * cosine + a * sine], axis=1)
        out_ref[pack, 0] = turned.astype(jnp.bfloat16)
        out_ref[pack, 1] = value.T.astype(jnp.bfloat16)


def project_second(where, hidden, weight, first, cosine, sine):
    return call(
        project_second_kernel,
        jax.ShapeDtypeStruct((4, 2, BLOCK, HEAD_DIM), jnp.bfloat16),
        [SMEM] + [VMEM] * 9,
        (2**29, 5 * 2**20),
        [pltpu.VMEM((4 * BLOCK, HEAD_DIM), jnp.float32)],
    )(where, *hidden, weight, first, cosine, sine)


def attend_kernel(tiles, opening, closing, where_ref, q_ref, start_ref, *refs):
    factor = math.log2(math.e) / math.sqrt(HEAD_DIM)
    y = where_ref[0]
    shifts = [shift for tile in tiles for shift in tile]
    kv, rest = dict(zip(shifts, refs)), refs[len(shifts) :]
    if not opening:
        given, rest = rest[:3], rest[3:]
    if closing:
        out_ref, acc, top, total = rest
    else:
        acc, top, total = rest

    @pl.loop(0, 4)
    def _(z):
        block = z * 8 + y
        slot = 0 if closing else z
        start = start_ref[z]
        row_at = block * BLOCK + lax.broadcasted_iota(jnp.int32, (BLOCK, BLOCK), 1)
        if opening:
            top[slot] = jnp.full(top.shape[1:], LOW, jnp.float32)
            total[slot] = jnp.zeros(total.shape[1:], jnp.float32)
            acc[slot] = jnp.zeros(acc.shape[1:], jnp.float32)
        else:
            for ref, source in zip((acc, top, total), given):
                ref[slot] = source[z]

        def turn(step, carry):
            zz = z - step
            for tile in tiles:
                places = [zz * 8 + ((y - shift) & 7) for shift in tile]
                needed = [
                    (place <= block) & ((place + 1) * BLOCK > where_ref[1 + z])
                    for place in places
                ]

                if tile == (FAR_LOW,):
                    needed.append(zz < 2)
                if tile == (FAR_HIGH,):
                    needed.append(zz >= 2)
                halved = tile in ((FAR_LOW,), (FAR_HIGH,))
                row = zz & 1 if halved else zz

                @pl.when(functools.reduce(jnp.logical_and if halved else jnp.logical_or, needed))
                def _(row=row, tile=tile, places=places):
                    key = jnp.concatenate([kv[shift][row, 0] for shift in tile], axis=0)
                    val = jnp.concatenate([kv[shift][row, 1] for shift in tile], axis=1)
                    allowed = []
                    for place in places:
                        at = place * BLOCK + lax.broadcasted_iota(jnp.int32, (BLOCK, BLOCK), 0)
                        allowed.append((at >= start) & (at <= row_at))
                    allowed = jnp.concatenate(allowed, axis=0)
                    for h in range(GROUP):
                        cols = slice(h * BLOCK, (h + 1) * BLOCK)
                        s = jnp.dot(key, q_ref[z, :, cols], preferred_element_type=jnp.float32)
                        s = jnp.where(allowed, s, LOW)
                        old = top[slot, :, cols]
                        new = jnp.maximum(old, jnp.max(s, axis=0, keepdims=True))
                        p = jnp.exp2((s - new) * factor)
                        scale = jnp.exp2((old - new) * factor)
                        top[slot, :, cols] = new
                        total[slot, :, cols] = total[slot, :, cols] * scale + jnp.sum(
                            p, axis=0, keepdims=True
                        )
                        acc[slot, :, cols] = acc[slot, :, cols] * scale + jnp.dot(
                            val, p.astype(jnp.bfloat16), preferred_element_type=jnp.float32
                        )

            return carry

        lax.fori_loop(0, z + 1, turn, 0)
        if closing:
            for h in range(GROUP):
                cols = slice(h * BLOCK, (h + 1) * BLOCK)
                mixed = acc[slot, :, cols] / total[slot, :, cols]
                out_ref[z, :, cols] = mixed.T.astype(jnp.bfloat16)


def attend(tiles, where, q, start, kv, state=None, closing=False):
    rows = GROUP * BLOCK
    slots = 1 if closing else 4
    shapes = [(slots, HEAD_DIM, rows), (slots, 1, rows), (slots, 1, rows)]
    held = [jax.ShapeDtypeStruct(shape, jnp.float32) for shape in shapes]
    given = [] if state is None else list(state)
    shifts = [shift for tile in tiles for shift in tile]
    out = jax.ShapeDtypeStruct((4, BLOCK, rows), jnp.bfloat16)
    return call(
        functools.partial(attend_kernel, tiles, state is None, closing),
        out if closing else held,
        [SMEM] + [VMEM] * (2 + len(shifts) + len(given)),
        (len(shifts) * 2**30, 4 * 2**20),
        [pltpu.VMEM(shape, jnp.float32) for shape in shapes] if closing else (),
    )(where, q, start, *[kv[shift] for shift in shifts], *given)


def on_device(hidden, queries, weight_copies, segment_ids, owner):
    y, z = lax.axis_index(Y), lax.axis_index(Z)
    x, c, zh = lax.axis_index("x"), lax.axis_index("c"), lax.axis_index("zh")
    segment_row = segment_ids[0]
    origin = owner[0] % 16

    pieces = weight_copies[0].reshape(BLOCK, 2, 4, 128).transpose(2, 1, 0, 3)
    row = segment_row.astype(jnp.bfloat16).reshape(1, 1, 32, 128)
    pieces = jnp.concatenate([pieces, jnp.broadcast_to(row, (4, 2, 32, 128))], axis=2)
    got = exchange(pieces.reshape(8, 160, 128), ("x", "c"))
    piece = pick(got[:, :BLOCK], origin % 8)
    rows_along = pick(got.reshape(4, 2, 160, 128)[:, :, BLOCK:], c, 1)
    piece = jnp.where(zh == origin // 8, piece, lax.ppermute(piece, "zh", ring(2, 1)))

    own = hidden[0]
    left = lax.ppermute(own, "x", ring(4, 1))
    right = lax.ppermute(own, "x", ring(4, -1))
    part = spread(piece, ("z1", "y1"), 8).reshape(8 * BLOCK, 128)
    part, left, right = lax.optimization_barrier((part, left, right))
    mine = spread(part, ("z0", "y0"), 4).reshape(32, BLOCK, 128)
    far_low = lax.ppermute(left[:64], "x", ring(4, 1))
    far_high = lax.ppermute(right[64:], "x", ring(4, -1))

    blocks = segment_row.reshape(4, 8, BLOCK)
    start = starts_of(segment_row, pick(blocks, y, 1))
    token = (jnp.arange(4)[:, None] * 8 + y) * BLOCK + jnp.arange(BLOCK)[None]
    q_angles = jnp.swapaxes(angles_of(token - start), 1, 2)
    q_turns = (jnp.cos(q_angles), jnp.sin(q_angles))
    split = queries[0].reshape(BLOCK, 4, GROUP * HEAD_DIM).transpose(1, 0, 2)

    rows_along = rows_along.astype(jnp.int32)
    along = pick(rows_along, z * 8 + y, 1)
    start_along = jax.vmap(starts_of)(rows_along, along)
    k_angles = angles_of((z * 8 + y) * BLOCK + jnp.arange(BLOCK)[None] - start_along)
    k_turns = (jnp.cos(k_angles), jnp.sin(k_angles))

    mine, far_low, far_high, start, q_turns, split, k_turns = lax.optimization_barrier(
        (mine, far_low, far_high, start, q_turns, split, k_turns)
    )
    other = lax.ppermute(mine, "c", ring(2, 1))
    rows = [own, left, far_low, far_high, right]
    first = project_first(rows, mine)
    both = project_second(
        jnp.stack([x, c]).astype(jnp.int32), rows, other, first, *k_turns
    )
    own_kv = exchange(exchange(both, "x"), Z)

    own_kv, split = lax.optimization_barrier((own_kv, split))
    q_turned = turn_queries(exchange(split, Z), *q_turns)

    where = jnp.concatenate([y[None], start[:, 0]]).astype(jnp.int32)
    start = start[:, None, :]
    kv = {0: own_kv}
    for step in range(1, 5):
        if step == 4:
            state = attend(((0,), (1, 2), (-1, -2)), where, q_turned, start, kv)
            kv[3], kv[-3], *state = lax.optimization_barrier((kv[3], kv[-3], *state))
            kv[FAR_LOW] = lax.ppermute(kv[3][:2], Y, ring(8, 1))
            kv[FAR_HIGH] = lax.ppermute(kv[-3][2:], Y, ring(8, -1))
        else:
            kv[step] = lax.ppermute(kv[step - 1], Y, ring(8, 1))
            kv[-step] = lax.ppermute(kv[1 - step], Y, ring(8, -1))
    state = attend(((3,), (-3,)), where, q_turned, start, kv, state)
    mixed = attend(((FAR_LOW,), (FAR_HIGH,)), where, q_turned, start, kv, state, closing=True)
    back = exchange(mixed, Z)
    return back.transpose(1, 0, 2).reshape(1, BLOCK, HEADS * HEAD_DIM)


def solution(mesh):
    fine = Mesh(mesh.devices.reshape(SIZES), AXES)
    placed = (
        P(REP, SEQ, None),
        P(REP, SEQ, None),
        P(REP, SEQ, None),
        P(REP, None),
        P(),
    )
    return jax.shard_map(
        on_device, mesh=fine, in_specs=placed, out_specs=P(REP, SEQ, None), check_vma=False
    )
```

```python
import functools
import math

import jax
import jax.numpy as jnp
from jax import lax
from jax.experimental import pallas as pl
from jax.experimental.pallas import tpu as pltpu
from jax.sharding import Mesh
from jax.sharding import PartitionSpec as P

HEADS = 32
KV_HEADS = 4
HEAD_DIM = 128
GROUP = HEADS // KV_HEADS
THETA = 1000000.0
BLOCK = 128
LOW = -1e30
DOCS = 6
FAR_LOW, FAR_HIGH = 4, -4

AXES = ("z1", "z0", "y1", "y0", "zh", "x", "c")
SIZES = (2, 2, 4, 2, 2, 4, 2)
SEQ = ("z1", "z0", "y1", "y0")
REP = ("zh", "x", "c")
Y = ("y1", "y0")
Z = ("z1", "z0")


def ring(size, shift):
    return [(i, (i + shift) % size) for i in range(size)]


def pick(value, index, axis=0):
    return lax.dynamic_index_in_dim(value, index, axis, keepdims=False)


def exchange(value, axes):
    return lax.all_to_all(value, axes, split_axis=0, concat_axis=0, tiled=True)


def spread(value, axes, members):
    return exchange(jnp.broadcast_to(value[None], (members,) + value.shape), axes)


def angles_of(positions):
    half = HEAD_DIM // 2
    freqs = THETA ** (-(jnp.arange(half, dtype=jnp.float32) * 2.0) / HEAD_DIM)
    return positions.astype(jnp.float32)[..., None] * freqs


def starts_of(segment_row, segments):
    first = jnp.zeros(segments.shape, jnp.int32)
    for doc in range(1, DOCS):
        begin = jnp.sum((segment_row < doc).astype(jnp.int32))
        first = jnp.where(segments >= doc, begin, first)
    return first


VMEM = pl.BlockSpec(memory_space=pltpu.VMEM)
SMEM = pl.BlockSpec(memory_space=pltpu.SMEM)


def call(kernel, out_shape, specs, cost, scratch=()):
    flops, moved = cost
    return pl.pallas_call(
        kernel,
        out_shape=out_shape,
        in_specs=specs,
        out_specs=jax.tree.map(lambda _: VMEM, out_shape),
        scratch_shapes=list(scratch),
        compiler_params=pltpu.CompilerParams(vmem_limit_bytes=32 * 2**20),
        cost_estimate=pl.CostEstimate(flops=flops, bytes_accessed=moved, transcendentals=0),
    )


def turn_kernel(q_ref, cos_ref, sin_ref, out_ref):
    half = HEAD_DIM // 2

    @pl.loop(0, 4)
    def _(z):
        cosine, sine = cos_ref[z], sin_ref[z]
        for h in range(GROUP):
            cols = slice(h * HEAD_DIM, (h + 1) * HEAD_DIM)
            t = q_ref[z, :, cols].astype(jnp.float32).T
            a, b = t[:half], t[half:]
            out_ref[z, :half, cols] = (a * cosine - b * sine).astype(jnp.bfloat16)
            out_ref[z, half:, cols] = (b * cosine + a * sine).astype(jnp.bfloat16)


def turn_queries(q, cosine, sine):
    return call(
        turn_kernel,
        jax.ShapeDtypeStruct((4, HEAD_DIM, GROUP * BLOCK), jnp.bfloat16),
        [VMEM] * 3,
        (4 * 2**20, 2 * 2**20),
    )(q, cosine, sine)


def multiply(hidden_refs, weight_ref, out_ref):
    at = 0
    for hidden_ref in hidden_refs:
        total = None
        for block in range(0, 32, 2):
            z1, z0, y1 = block // 16, block // 8 % 2, block // 2 % 4
            low = z0 * 16 + z1 * 4 + y1
            weight = jnp.concatenate([weight_ref[low], weight_ref[low + 8]], axis=0)
            term = jnp.dot(
                hidden_ref[:, block * 128 : block * 128 + 256],
                weight,
                preferred_element_type=jnp.float32,
            )
            total = term if total is None else total + term
        out_ref[at : at + hidden_ref.shape[0]] = total
        at += hidden_ref.shape[0]


def project_first_kernel(*refs):
    multiply(refs[:5], refs[5], refs[6])


def project_first(hidden, weight):
    return call(
        project_first_kernel,
        jax.ShapeDtypeStruct((4 * BLOCK, HEAD_DIM), jnp.float32),
        [VMEM] * 6,
        (2**29, 5 * 2**20),
    )(*hidden, weight)


def project_second_kernel(*refs):
    where_ref, first_ref, cos_ref, sin_ref, out_ref, second = (refs[0],) + refs[7:]
    half = HEAD_DIM // 2
    multiply(refs[1:6], refs[6], second)
    x, keys_first = where_ref[0], where_ref[1] == 0
    for d in range(4):
        pack = (x - d) & 3
        one, two = first_ref[d * BLOCK : (d + 1) * BLOCK], second[d * BLOCK : (d + 1) * BLOCK]
        key = jnp.where(keys_first, one, two)
        value = jnp.where(keys_first, two, one)
        a, b = key[:, :half], key[:, half:]
        cosine, sine = cos_ref[pack], sin_ref[pack]
        turned = jnp.concatenate([a * cosine - b * sine, b * cosine + a * sine], axis=1)
        out_ref[pack, 0] = turned.astype(jnp.bfloat16)
        out_ref[pack, 1] = value.T.astype(jnp.bfloat16)


def project_second(where, hidden, weight, first, cosine, sine):
    return call(
        project_second_kernel,
        jax.ShapeDtypeStruct((4, 2, BLOCK, HEAD_DIM), jnp.bfloat16),
        [SMEM] + [VMEM] * 9,
        (2**29, 5 * 2**20),
        [pltpu.VMEM((4 * BLOCK, HEAD_DIM), jnp.float32)],
    )(where, *hidden, weight, first, cosine, sine)


def attend_kernel(tiles, opening, closing, where_ref, q_ref, start_ref, *refs):
    factor = math.log2(math.e) / math.sqrt(HEAD_DIM)
    y = where_ref[0]
    shifts = [shift for tile in tiles for shift in tile]
    kv, rest = dict(zip(shifts, refs)), refs[len(shifts) :]
    if not opening:
        given, rest = rest[:3], rest[3:]
    if closing:
        out_ref, acc, top, total = rest
    else:
        acc, top, total = rest

    @pl.loop(0, 4)
    def _(z):
        block = z * 8 + y
        slot = 0 if closing else z
        start = start_ref[z]
        row_at = block * BLOCK + lax.broadcasted_iota(jnp.int32, (BLOCK, BLOCK), 1)
        if opening:
            top[slot] = jnp.full(top.shape[1:], LOW, jnp.float32)
            total[slot] = jnp.zeros(total.shape[1:], jnp.float32)
            acc[slot] = jnp.zeros(acc.shape[1:], jnp.float32)
        else:
            for ref, source in zip((acc, top, total), given):
                ref[slot] = source[z]

        def turn(step, carry):
            zz = z - step
            for tile in tiles:
                places = [zz * 8 + ((y - shift) & 7) for shift in tile]
                needed = [
                    (place <= block) & ((place + 1) * BLOCK > where_ref[1 + z])
                    for place in places
                ]

                if tile == (FAR_LOW,):
                    needed.append(zz < 2)
                if tile == (FAR_HIGH,):
                    needed.append(zz >= 2)
                halved = tile in ((FAR_LOW,), (FAR_HIGH,))
                row = zz & 1 if halved else zz

                @pl.when(functools.reduce(jnp.logical_and if halved else jnp.logical_or, needed))
                def _(row=row, tile=tile, places=places):
                    key = jnp.concatenate([kv[shift][row, 0] for shift in tile], axis=0)
                    val = jnp.concatenate([kv[shift][row, 1] for shift in tile], axis=1)
                    allowed = []
                    for place in places:
                        at = place * BLOCK + lax.broadcasted_iota(jnp.int32, (BLOCK, BLOCK), 0)
                        allowed.append((at >= start) & (at <= row_at))
                    allowed = jnp.concatenate(allowed, axis=0)
                    for h in range(GROUP):
                        cols = slice(h * BLOCK, (h + 1) * BLOCK)
                        s = jnp.dot(key, q_ref[z, :, cols], preferred_element_type=jnp.float32)
                        s = jnp.where(allowed, s, LOW)
                        old = top[slot, :, cols]
                        new = jnp.maximum(old, jnp.max(s, axis=0, keepdims=True))
                        p = jnp.exp2((s - new) * factor)
                        scale = jnp.exp2((old - new) * factor)
                        top[slot, :, cols] = new
                        total[slot, :, cols] = total[slot, :, cols] * scale + jnp.sum(
                            p, axis=0, keepdims=True
                        )
                        acc[slot, :, cols] = acc[slot, :, cols] * scale + jnp.dot(
                            val, p.astype(jnp.bfloat16), preferred_element_type=jnp.float32
                        )

            return carry

        lax.fori_loop(0, z + 1, turn, 0)
        if closing:
            for h in range(GROUP):
                cols = slice(h * BLOCK, (h + 1) * BLOCK)
                mixed = acc[slot, :, cols] / total[slot, :, cols]
                out_ref[z, :, cols] = mixed.T.astype(jnp.bfloat16)


def attend(tiles, where, q, start, kv, state=None, closing=False):
    rows = GROUP * BLOCK
    slots = 1 if closing else 4
    shapes = [(slots, HEAD_DIM, rows), (slots, 1, rows), (slots, 1, rows)]
    held = [jax.ShapeDtypeStruct(shape, jnp.float32) for shape in shapes]
    given = [] if state is None else list(state)
    shifts = [shift for tile in tiles for shift in tile]
    out = jax.ShapeDtypeStruct((4, BLOCK, rows), jnp.bfloat16)
    return call(
        functools.partial(attend_kernel, tiles, state is None, closing),
        out if closing else held,
        [SMEM] + [VMEM] * (2 + len(shifts) + len(given)),
        (len(shifts) * 2**30, 4 * 2**20),
        [pltpu.VMEM(shape, jnp.float32) for shape in shapes] if closing else (),
    )(where, q, start, *[kv[shift] for shift in shifts], *given)


def on_device(hidden, queries, weight_copies, segment_ids, owner):
    y, z = lax.axis_index(Y), lax.axis_index(Z)
    x, c, zh = lax.axis_index("x"), lax.axis_index("c"), lax.axis_index("zh")
    segment_row = segment_ids[0]
    origin = owner[0] % 16

    pieces = weight_copies[0].reshape(BLOCK, 2, 4, 128).transpose(2, 1, 0, 3)
    row = segment_row.astype(jnp.bfloat16).reshape(1, 1, 32, 128)
    pieces = jnp.concatenate([pieces, jnp.broadcast_to(row, (4, 2, 32, 128))], axis=2)
    got = exchange(pieces.reshape(8, 160, 128), ("x", "c"))
    piece = pick(got[:, :BLOCK], origin % 8)
    rows_along = pick(got.reshape(4, 2, 160, 128)[:, :, BLOCK:], c, 1)
    piece = jnp.where(zh == origin // 8, piece, lax.ppermute(piece, "zh", ring(2, 1)))

    blocks = segment_row.reshape(4, 8, BLOCK)
    start = starts_of(segment_row, pick(blocks, y, 1))
    token = (jnp.arange(4)[:, None] * 8 + y) * BLOCK + jnp.arange(BLOCK)[None]
    q_angles = jnp.swapaxes(angles_of(token - start), 1, 2)
    q_turns = (jnp.cos(q_angles), jnp.sin(q_angles))
    split = queries[0].reshape(BLOCK, 4, GROUP * HEAD_DIM).transpose(1, 0, 2)

    rows_along = rows_along.astype(jnp.int32)
    along = pick(rows_along, z * 8 + y, 1)
    start_along = jax.vmap(starts_of)(rows_along, along)
    k_angles = angles_of((z * 8 + y) * BLOCK + jnp.arange(BLOCK)[None] - start_along)
    k_turns = (jnp.cos(k_angles), jnp.sin(k_angles))

    own = hidden[0]
    left = lax.ppermute(own, "x", ring(4, 1))
    right = lax.ppermute(own, "x", ring(4, -1))
    part = spread(piece, ("z1", "y1"), 8).reshape(8 * BLOCK, 128)
    tokens = (left[:8, :128], right[:8, :128])
    part, tokens, start, q_turns, split, k_turns = lax.optimization_barrier(
        (part, tokens, start, q_turns, split, k_turns)
    )
    mine = spread(part, ("z0", "y0"), 4).reshape(32, BLOCK, 128)
    far_low = lax.ppermute(left[:64], "x", ring(4, 1))
    far_high = lax.ppermute(right[64:], "x", ring(4, -1))
    mine, tokens = lax.optimization_barrier((mine, (far_low[:8, :128], far_high[:8, :128])))
    other = lax.ppermute(mine, "c", ring(2, 1))
    rows = [own, left, far_low, far_high, right]
    first = project_first(rows, mine)
    both = project_second(
        jnp.stack([x, c]).astype(jnp.int32), rows, other, first, *k_turns
    )
    own_kv = exchange(exchange(both, "x"), Z)

    own_kv, split = lax.optimization_barrier((own_kv, split))
    q_turned = turn_queries(exchange(split, Z), *q_turns)

    where = jnp.concatenate([y[None], start[:, 0]]).astype(jnp.int32)
    start = start[:, None, :]
    kv = {0: own_kv}
    for step in range(1, 5):
        if step == 4:
            state = attend(((0,), (1, 2), (-1, -2)), where, q_turned, start, kv)
            kv[3], kv[-3], *state = lax.optimization_barrier((kv[3], kv[-3], *state))
            kv[FAR_LOW] = lax.ppermute(kv[3][:2], Y, ring(8, 1))
            kv[FAR_HIGH] = lax.ppermute(kv[-3][2:], Y, ring(8, -1))
        else:
            kv[step] = lax.ppermute(kv[step - 1], Y, ring(8, 1))
            kv[-step] = lax.ppermute(kv[1 - step], Y, ring(8, -1))
    state = attend(((3,), (-3,)), where, q_turned, start, kv, state)
    mixed = attend(((FAR_LOW,), (FAR_HIGH,)), where, q_turned, start, kv, state, closing=True)
    back = exchange(mixed, Z)
    return back.transpose(1, 0, 2).reshape(1, BLOCK, HEADS * HEAD_DIM)


def solution(mesh):
    fine = Mesh(mesh.devices.reshape(SIZES), AXES)
    placed = (
        P(REP, SEQ, None),
        P(REP, SEQ, None),
        P(REP, SEQ, None),
        P(REP, None),
        P(),
    )
    return jax.shard_map(
        on_device, mesh=fine, in_specs=placed, out_specs=P(REP, SEQ, None), check_vma=False
    )
```

```python
import functools
import math

import jax
import jax.numpy as jnp
from jax import lax
from jax.experimental import pallas as pl
from jax.experimental.pallas import tpu as pltpu
from jax.sharding import Mesh
from jax.sharding import PartitionSpec as P

HEADS = 32
KV_HEADS = 4
HEAD_DIM = 128
GROUP = HEADS // KV_HEADS
THETA = 1000000.0
BLOCK = 128
LOW = -1e30
DOCS = 6
FAR_LOW, FAR_HIGH = 4, -4

AXES = ("z1", "z0", "y1", "y0", "zh", "x", "c")
SIZES = (2, 2, 4, 2, 2, 4, 2)
SEQ = ("z1", "z0", "y1", "y0")
REP = ("zh", "x", "c")
Y = ("y1", "y0")
Z = ("z1", "z0")


def ring(size, shift):
    return [(i, (i + shift) % size) for i in range(size)]


def pick(value, index, axis=0):
    return lax.dynamic_index_in_dim(value, index, axis, keepdims=False)


def exchange(value, axes):
    return lax.all_to_all(value, axes, split_axis=0, concat_axis=0, tiled=True)


def spread(value, axes, members):
    return exchange(jnp.broadcast_to(value[None], (members,) + value.shape), axes)


def angles_of(positions):
    half = HEAD_DIM // 2
    freqs = THETA ** (-(jnp.arange(half, dtype=jnp.float32) * 2.0) / HEAD_DIM)
    return positions.astype(jnp.float32)[..., None] * freqs


def starts_of(segment_row, segments):
    first = jnp.zeros(segments.shape, jnp.int32)
    for doc in range(1, DOCS):
        begin = jnp.sum((segment_row < doc).astype(jnp.int32))
        first = jnp.where(segments >= doc, begin, first)
    return first


VMEM = pl.BlockSpec(memory_space=pltpu.VMEM)
SMEM = pl.BlockSpec(memory_space=pltpu.SMEM)


def call(kernel, out_shape, specs, cost, scratch=()):
    flops, moved = cost
    return pl.pallas_call(
        kernel,
        out_shape=out_shape,
        in_specs=specs,
        out_specs=jax.tree.map(lambda _: VMEM, out_shape),
        scratch_shapes=list(scratch),
        compiler_params=pltpu.CompilerParams(vmem_limit_bytes=32 * 2**20),
        cost_estimate=pl.CostEstimate(flops=flops, bytes_accessed=moved, transcendentals=0),
    )


def turn_kernel(q_ref, cos_ref, sin_ref, out_ref):
    half = HEAD_DIM // 2

    @pl.loop(0, 4)
    def _(z):
        cosine, sine = cos_ref[z], sin_ref[z]
        for h in range(GROUP):
            cols = slice(h * HEAD_DIM, (h + 1) * HEAD_DIM)
            t = q_ref[z, :, cols].astype(jnp.float32).T
            a, b = t[:half], t[half:]
            out_ref[z, :half, cols] = (a * cosine - b * sine).astype(jnp.bfloat16)
            out_ref[z, half:, cols] = (b * cosine + a * sine).astype(jnp.bfloat16)


def turn_queries(q, cosine, sine):
    return call(
        turn_kernel,
        jax.ShapeDtypeStruct((4, HEAD_DIM, GROUP * BLOCK), jnp.bfloat16),
        [VMEM] * 3,
        (4 * 2**20, 2 * 2**20),
    )(q, cosine, sine)


def multiply(hidden_refs, weight_ref, out_ref):
    at = 0
    for hidden_ref in hidden_refs:
        total = None
        for block in range(0, 32, 2):
            z1, z0, y1 = block // 16, block // 8 % 2, block // 2 % 4
            low = z0 * 16 + z1 * 4 + y1
            weight = jnp.concatenate([weight_ref[low], weight_ref[low + 8]], axis=0)
            term = jnp.dot(
                hidden_ref[:, block * 128 : block * 128 + 256],
                weight,
                preferred_element_type=jnp.float32,
            )
            total = term if total is None else total + term
        out_ref[at : at + hidden_ref.shape[0]] = total
        at += hidden_ref.shape[0]


def project_first_kernel(*refs):
    multiply(refs[:5], refs[5], refs[8])


def project_first(hidden, weight, arrived):
    return call(
        project_first_kernel,
        jax.ShapeDtypeStruct((4 * BLOCK, HEAD_DIM), jnp.float32),
        [VMEM] * 8,
        (2**29, 5 * 2**20),
    )(*hidden, weight, *arrived)


def project_second_kernel(*refs):
    where_ref, first_ref, cos_ref, sin_ref, out_ref, second = (refs[0],) + refs[7:]
    half = HEAD_DIM // 2
    multiply(refs[1:6], refs[6], second)
    x, keys_first = where_ref[0], where_ref[1] == 0
    for d in range(4):
        pack = (x - d) & 3
        one, two = first_ref[d * BLOCK : (d + 1) * BLOCK], second[d * BLOCK : (d + 1) * BLOCK]
        key = jnp.where(keys_first, one, two)
        value = jnp.where(keys_first, two, one)
        a, b = key[:, :half], key[:, half:]
        cosine, sine = cos_ref[pack], sin_ref[pack]
        turned = jnp.concatenate([a * cosine - b * sine, b * cosine + a * sine], axis=1)
        out_ref[pack, 0] = turned.astype(jnp.bfloat16)
        out_ref[pack, 1] = value.T.astype(jnp.bfloat16)


def project_second(where, hidden, weight, first, cosine, sine):
    return call(
        project_second_kernel,
        jax.ShapeDtypeStruct((4, 2, BLOCK, HEAD_DIM), jnp.bfloat16),
        [SMEM] + [VMEM] * 9,
        (2**29, 5 * 2**20),
        [pltpu.VMEM((4 * BLOCK, HEAD_DIM), jnp.float32)],
    )(where, *hidden, weight, first, cosine, sine)


def attend_kernel(tiles, opening, closing, where_ref, q_ref, start_ref, *refs):
    factor = math.log2(math.e) / math.sqrt(HEAD_DIM)
    y = where_ref[0]
    shifts = [shift for tile in tiles for shift in tile]
    kv, rest = dict(zip(shifts, refs)), refs[len(shifts) :]
    if not opening:
        given, rest = rest[:3], rest[3:]
    if closing:
        out_ref, acc, top, total = rest
    else:
        acc, top, total = rest

    @pl.loop(0, 4)
    def _(z):
        block = z * 8 + y
        slot = 0 if closing else z
        start = start_ref[z]
        row_at = block * BLOCK + lax.broadcasted_iota(jnp.int32, (BLOCK, BLOCK), 1)
        if opening:
            top[slot] = jnp.full(top.shape[1:], LOW, jnp.float32)
            total[slot] = jnp.zeros(total.shape[1:], jnp.float32)
            acc[slot] = jnp.zeros(acc.shape[1:], jnp.float32)
        else:
            for ref, source in zip((acc, top, total), given):
                ref[slot] = source[z]

        def turn(step, carry):
            zz = z - step
            for tile in tiles:
                places = [zz * 8 + ((y - shift) & 7) for shift in tile]
                needed = [
                    (place <= block) & ((place + 1) * BLOCK > where_ref[1 + z])
                    for place in places
                ]

                if tile == (FAR_LOW,):
                    needed.append(zz < 2)
                if tile == (FAR_HIGH,):
                    needed.append(zz >= 2)
                halved = tile in ((FAR_LOW,), (FAR_HIGH,))
                row = zz & 1 if halved else zz

                @pl.when(functools.reduce(jnp.logical_and if halved else jnp.logical_or, needed))
                def _(row=row, tile=tile, places=places):
                    key = jnp.concatenate([kv[shift][row, 0] for shift in tile], axis=0)
                    val = jnp.concatenate([kv[shift][row, 1] for shift in tile], axis=1)
                    allowed = []
                    for place in places:
                        at = place * BLOCK + lax.broadcasted_iota(jnp.int32, (BLOCK, BLOCK), 0)
                        allowed.append((at >= start) & (at <= row_at))
                    allowed = jnp.concatenate(allowed, axis=0)
                    for h in range(GROUP):
                        cols = slice(h * BLOCK, (h + 1) * BLOCK)
                        s = jnp.dot(key, q_ref[z, :, cols], preferred_element_type=jnp.float32)
                        s = jnp.where(allowed, s, LOW)
                        old = top[slot, :, cols]
                        new = jnp.maximum(old, jnp.max(s, axis=0, keepdims=True))
                        p = jnp.exp2((s - new) * factor)
                        scale = jnp.exp2((old - new) * factor)
                        top[slot, :, cols] = new
                        total[slot, :, cols] = total[slot, :, cols] * scale + jnp.sum(
                            p, axis=0, keepdims=True
                        )
                        acc[slot, :, cols] = acc[slot, :, cols] * scale + jnp.dot(
                            val, p.astype(jnp.bfloat16), preferred_element_type=jnp.float32
                        )

            return carry

        lax.fori_loop(0, z + 1, turn, 0)
        if closing:
            for h in range(GROUP):
                cols = slice(h * BLOCK, (h + 1) * BLOCK)
                mixed = acc[slot, :, cols] / total[slot, :, cols]
                out_ref[z, :, cols] = mixed.T.astype(jnp.bfloat16)


def attend(tiles, where, q, start, kv, state=None, closing=False):
    rows = GROUP * BLOCK
    slots = 1 if closing else 4
    shapes = [(slots, HEAD_DIM, rows), (slots, 1, rows), (slots, 1, rows)]
    held = [jax.ShapeDtypeStruct(shape, jnp.float32) for shape in shapes]
    given = [] if state is None else list(state)
    shifts = [shift for tile in tiles for shift in tile]
    out = jax.ShapeDtypeStruct((4, BLOCK, rows), jnp.bfloat16)
    return call(
        functools.partial(attend_kernel, tiles, state is None, closing),
        out if closing else held,
        [SMEM] + [VMEM] * (2 + len(shifts) + len(given)),
        (len(shifts) * 2**30, 4 * 2**20),
        [pltpu.VMEM(shape, jnp.float32) for shape in shapes] if closing else (),
    )(where, q, start, *[kv[shift] for shift in shifts], *given)


def on_device(hidden, queries, weight_copies, segment_ids, owner):
    y, z = lax.axis_index(Y), lax.axis_index(Z)
    x, c, zh = lax.axis_index("x"), lax.axis_index("c"), lax.axis_index("zh")
    segment_row = segment_ids[0]
    origin = owner[0] % 16

    pieces = weight_copies[0].reshape(BLOCK, 2, 4, 128).transpose(2, 1, 0, 3)
    row = segment_row.astype(jnp.bfloat16).reshape(1, 1, 32, 128)
    pieces = jnp.concatenate([pieces, jnp.broadcast_to(row, (4, 2, 32, 128))], axis=2)
    got = exchange(pieces.reshape(8, 160, 128), ("x", "c"))
    piece = pick(got[:, :BLOCK], origin % 8)
    rows_along = pick(got.reshape(4, 2, 160, 128)[:, :, BLOCK:], c, 1)
    piece = jnp.where(zh == origin // 8, piece, lax.ppermute(piece, "zh", ring(2, 1)))

    blocks = segment_row.reshape(4, 8, BLOCK)
    start = starts_of(segment_row, pick(blocks, y, 1))
    token = (jnp.arange(4)[:, None] * 8 + y) * BLOCK + jnp.arange(BLOCK)[None]
    q_angles = jnp.swapaxes(angles_of(token - start), 1, 2)
    q_turns = (jnp.cos(q_angles), jnp.sin(q_angles))
    split = queries[0].reshape(BLOCK, 4, GROUP * HEAD_DIM).transpose(1, 0, 2)

    rows_along = rows_along.astype(jnp.int32)
    along = pick(rows_along, z * 8 + y, 1)
    start_along = jax.vmap(starts_of)(rows_along, along)
    k_angles = angles_of((z * 8 + y) * BLOCK + jnp.arange(BLOCK)[None] - start_along)
    k_turns = (jnp.cos(k_angles), jnp.sin(k_angles))

    own = hidden[0]
    left = lax.ppermute(own, "x", ring(4, 1))
    right = lax.ppermute(own, "x", ring(4, -1))
    part = spread(piece, ("z1", "y1"), 8).reshape(8 * BLOCK, 128)
    part, left, right, start, q_turns, split, k_turns = lax.optimization_barrier(
        (part, left, right, start, q_turns, split, k_turns)
    )
    mine = spread(part, ("z0", "y0"), 4).reshape(32, BLOCK, 128)
    far_low = lax.ppermute(left[:64], "x", ring(4, 1))
    far_high = lax.ppermute(right[64:], "x", ring(4, -1))
    mine, *arrived = lax.optimization_barrier((mine, far_low[:8, :128], far_high[:8, :128]))
    other = lax.ppermute(mine, "c", ring(2, 1))
    rows = [own, left, far_low, far_high, right]
    first = project_first(rows, mine, arrived)
    both = project_second(
        jnp.stack([x, c]).astype(jnp.int32), rows, other, first, *k_turns
    )
    own_kv = exchange(exchange(both, "x"), Z)

    own_kv, split = lax.optimization_barrier((own_kv, split))
    q_turned = turn_queries(exchange(split, Z), *q_turns)

    where = jnp.concatenate([y[None], start[:, 0]]).astype(jnp.int32)
    start = start[:, None, :]
    kv = {0: own_kv}
    for step in range(1, 5):
        if step == 4:
            state = attend(((0,), (1, 2), (-1, -2)), where, q_turned, start, kv)
            kv[3], kv[-3], *state = lax.optimization_barrier((kv[3], kv[-3], *state))
            kv[FAR_LOW] = lax.ppermute(kv[3][:2], Y, ring(8, 1))
            kv[FAR_HIGH] = lax.ppermute(kv[-3][2:], Y, ring(8, -1))
        else:
            kv[step] = lax.ppermute(kv[step - 1], Y, ring(8, 1))
            kv[-step] = lax.ppermute(kv[1 - step], Y, ring(8, -1))
    state = attend(((3,), (-3,)), where, q_turned, start, kv, state)
    mixed = attend(((FAR_LOW,), (FAR_HIGH,)), where, q_turned, start, kv, state, closing=True)
    back = exchange(mixed, Z)
    return back.transpose(1, 0, 2).reshape(1, BLOCK, HEADS * HEAD_DIM)


def solution(mesh):
    fine = Mesh(mesh.devices.reshape(SIZES), AXES)
    placed = (
        P(REP, SEQ, None),
        P(REP, SEQ, None),
        P(REP, SEQ, None),
        P(REP, None),
        P(),
    )
    return jax.shard_map(
        on_device, mesh=fine, in_specs=placed, out_specs=P(REP, SEQ, None), check_vma=False
    )
```

```python
import functools
import math

import jax
import jax.numpy as jnp
from jax import lax
from jax.experimental import pallas as pl
from jax.experimental.pallas import tpu as pltpu
from jax.sharding import Mesh
from jax.sharding import PartitionSpec as P

HEADS = 32
KV_HEADS = 4
HEAD_DIM = 128
GROUP = HEADS // KV_HEADS
THETA = 1000000.0
BLOCK = 128
LOW = -1e30
DOCS = 6
FAR_LOW, FAR_HIGH = 4, -4

AXES = ("z1", "z0", "y1", "y0", "zh", "x", "c")
SIZES = (2, 2, 4, 2, 2, 4, 2)
SEQ = ("z1", "z0", "y1", "y0")
REP = ("zh", "x", "c")
Y = ("y1", "y0")
Z = ("z1", "z0")


def ring(size, shift):
    return [(i, (i + shift) % size) for i in range(size)]


def pick(value, index, axis=0):
    return lax.dynamic_index_in_dim(value, index, axis, keepdims=False)


def exchange(value, axes):
    return lax.all_to_all(value, axes, split_axis=0, concat_axis=0, tiled=True)


def spread(value, axes, members):
    return exchange(jnp.broadcast_to(value[None], (members,) + value.shape), axes)


def angles_of(positions):
    half = HEAD_DIM // 2
    freqs = THETA ** (-(jnp.arange(half, dtype=jnp.float32) * 2.0) / HEAD_DIM)
    return positions.astype(jnp.float32)[..., None] * freqs


def starts_of(segment_row, segments):
    first = jnp.zeros(segments.shape, jnp.int32)
    for doc in range(1, DOCS):
        begin = jnp.sum((segment_row < doc).astype(jnp.int32))
        first = jnp.where(segments >= doc, begin, first)
    return first


VMEM = pl.BlockSpec(memory_space=pltpu.VMEM)
SMEM = pl.BlockSpec(memory_space=pltpu.SMEM)


def call(kernel, out_shape, specs, cost, scratch=()):
    flops, moved = cost
    return pl.pallas_call(
        kernel,
        out_shape=out_shape,
        in_specs=specs,
        out_specs=jax.tree.map(lambda _: VMEM, out_shape),
        scratch_shapes=list(scratch),
        compiler_params=pltpu.CompilerParams(vmem_limit_bytes=32 * 2**20),
        cost_estimate=pl.CostEstimate(flops=flops, bytes_accessed=moved, transcendentals=0),
    )


def turn_kernel(q_ref, cos_ref, sin_ref, out_ref):
    half = HEAD_DIM // 2

    @pl.loop(0, 4)
    def _(z):
        cosine, sine = cos_ref[z], sin_ref[z]
        for h in range(GROUP):
            cols = slice(h * HEAD_DIM, (h + 1) * HEAD_DIM)
            t = q_ref[z, :, cols].astype(jnp.float32).T
            a, b = t[:half], t[half:]
            out_ref[z, :half, cols] = (a * cosine - b * sine).astype(jnp.bfloat16)
            out_ref[z, half:, cols] = (b * cosine + a * sine).astype(jnp.bfloat16)


def turn_queries(q, cosine, sine):
    return call(
        turn_kernel,
        jax.ShapeDtypeStruct((4, HEAD_DIM, GROUP * BLOCK), jnp.bfloat16),
        [VMEM] * 3,
        (4 * 2**20, 2 * 2**20),
    )(q, cosine, sine)


def multiply(hidden_refs, weight_ref, out_ref):
    at = 0
    for hidden_ref in hidden_refs:
        total = None
        for block in range(0, 32, 2):
            z1, z0, y1 = block // 16, block // 8 % 2, block // 2 % 4
            low = z0 * 16 + z1 * 4 + y1
            weight = jnp.concatenate([weight_ref[low], weight_ref[low + 8]], axis=0)
            term = jnp.dot(
                hidden_ref[:, block * 128 : block * 128 + 256],
                weight,
                preferred_element_type=jnp.float32,
            )
            total = term if total is None else total + term
        out_ref[at : at + hidden_ref.shape[0]] = total
        at += hidden_ref.shape[0]


def project_first_kernel(*refs):
    multiply(refs[:5], refs[5], refs[8])


def project_first(hidden, weight, arrived):
    return call(
        project_first_kernel,
        jax.ShapeDtypeStruct((4 * BLOCK, HEAD_DIM), jnp.float32),
        [VMEM] * 8,
        (2**29, 5 * 2**20),
    )(*hidden, weight, *arrived)


def project_second_kernel(*refs):
    where_ref, first_ref, cos_ref, sin_ref, out_ref, second = (refs[0],) + refs[7:]
    half = HEAD_DIM // 2
    multiply(refs[1:6], refs[6], second)
    x, keys_first = where_ref[0], where_ref[1] == 0
    for d in range(4):
        pack = (x - d) & 3
        one, two = first_ref[d * BLOCK : (d + 1) * BLOCK], second[d * BLOCK : (d + 1) * BLOCK]
        key = jnp.where(keys_first, one, two)
        value = jnp.where(keys_first, two, one)
        a, b = key[:, :half], key[:, half:]
        cosine, sine = cos_ref[pack], sin_ref[pack]
        turned = jnp.concatenate([a * cosine - b * sine, b * cosine + a * sine], axis=1)
        out_ref[pack, 0] = turned.astype(jnp.bfloat16)
        out_ref[pack, 1] = value.T.astype(jnp.bfloat16)


def project_second(where, hidden, weight, first, cosine, sine):
    return call(
        project_second_kernel,
        jax.ShapeDtypeStruct((4, 2, BLOCK, HEAD_DIM), jnp.bfloat16),
        [SMEM] + [VMEM] * 9,
        (2**29, 5 * 2**20),
        [pltpu.VMEM((4 * BLOCK, HEAD_DIM), jnp.float32)],
    )(where, *hidden, weight, first, cosine, sine)


def attend_kernel(tiles, opening, closing, where_ref, q_ref, start_ref, *refs):
    factor = math.log2(math.e) / math.sqrt(HEAD_DIM)
    y = where_ref[0]
    shifts = [shift for tile in tiles for shift in tile]
    kv, rest = dict(zip(shifts, refs)), refs[len(shifts) :]
    if not opening:
        given, rest = rest[:3], rest[3:]
    if closing:
        out_ref, acc, top, total = rest
    else:
        acc, top, total = rest

    @pl.loop(0, 4)
    def _(z):
        block = z * 8 + y
        slot = 0 if closing else z
        start = start_ref[z]
        row_at = block * BLOCK + lax.broadcasted_iota(jnp.int32, (BLOCK, BLOCK), 1)
        if opening:
            top[slot] = jnp.full(top.shape[1:], LOW, jnp.float32)
            total[slot] = jnp.zeros(total.shape[1:], jnp.float32)
            acc[slot] = jnp.zeros(acc.shape[1:], jnp.float32)
        else:
            for ref, source in zip((acc, top, total), given):
                ref[slot] = source[z]

        def turn(step, carry):
            zz = z - step
            for tile in tiles:
                places = [zz * 8 + ((y - shift) & 7) for shift in tile]
                needed = [
                    (place <= block) & ((place + 1) * BLOCK > where_ref[1 + z])
                    for place in places
                ]

                if tile == (FAR_LOW,):
                    needed.append(zz < 2)
                if tile == (FAR_HIGH,):
                    needed.append(zz >= 2)
                halved = tile in ((FAR_LOW,), (FAR_HIGH,))
                row = zz & 1 if halved else zz

                @pl.when(functools.reduce(jnp.logical_and if halved else jnp.logical_or, needed))
                def _(row=row, tile=tile, places=places):
                    key = jnp.concatenate([kv[shift][row, 0] for shift in tile], axis=0)
                    val = jnp.concatenate([kv[shift][row, 1] for shift in tile], axis=1)
                    allowed = []
                    for place in places:
                        at = place * BLOCK + lax.broadcasted_iota(jnp.int32, (BLOCK, BLOCK), 0)
                        allowed.append((at >= start) & (at <= row_at))
                    allowed = jnp.concatenate(allowed, axis=0)
                    for h in range(GROUP):
                        cols = slice(h * BLOCK, (h + 1) * BLOCK)
                        s = jnp.dot(key, q_ref[z, :, cols], preferred_element_type=jnp.float32)
                        s = jnp.where(allowed, s, LOW)
                        old = top[slot, :, cols]
                        new = jnp.maximum(old, jnp.max(s, axis=0, keepdims=True))
                        p = jnp.exp2((s - new) * factor)
                        scale = jnp.exp2((old - new) * factor)
                        top[slot, :, cols] = new
                        total[slot, :, cols] = total[slot, :, cols] * scale + jnp.sum(
                            p, axis=0, keepdims=True
                        )
                        acc[slot, :, cols] = acc[slot, :, cols] * scale + jnp.dot(
                            val, p.astype(jnp.bfloat16), preferred_element_type=jnp.float32
                        )

            return carry

        lax.fori_loop(0, z + 1, turn, 0)
        if closing:
            for h in range(GROUP):
                cols = slice(h * BLOCK, (h + 1) * BLOCK)
                mixed = acc[slot, :, cols] / total[slot, :, cols]
                out_ref[z, :, cols] = mixed.T.astype(jnp.bfloat16)


def attend(tiles, where, q, start, kv, state=None, closing=False):
    rows = GROUP * BLOCK
    slots = 1 if closing else 4
    shapes = [(slots, HEAD_DIM, rows), (slots, 1, rows), (slots, 1, rows)]
    held = [jax.ShapeDtypeStruct(shape, jnp.float32) for shape in shapes]
    given = [] if state is None else list(state)
    shifts = [shift for tile in tiles for shift in tile]
    out = jax.ShapeDtypeStruct((4, BLOCK, rows), jnp.bfloat16)
    return call(
        functools.partial(attend_kernel, tiles, state is None, closing),
        out if closing else held,
        [SMEM] + [VMEM] * (2 + len(shifts) + len(given)),
        (len(shifts) * 2**30, 4 * 2**20),
        [pltpu.VMEM(shape, jnp.float32) for shape in shapes] if closing else (),
    )(where, q, start, *[kv[shift] for shift in shifts], *given)


def on_device(hidden, queries, weight_copies, segment_ids, owner):
    y, z = lax.axis_index(Y), lax.axis_index(Z)
    x, c, zh = lax.axis_index("x"), lax.axis_index("c"), lax.axis_index("zh")
    segment_row = segment_ids[0]
    origin = owner[0] % 16

    pieces = weight_copies[0].reshape(BLOCK, 2, 4, 128).transpose(2, 1, 0, 3)
    row = segment_row.astype(jnp.bfloat16).reshape(1, 1, 32, 128)
    pieces = jnp.concatenate([pieces, jnp.broadcast_to(row, (4, 2, 32, 128))], axis=2)
    got = exchange(pieces.reshape(8, 160, 128), ("x", "c"))
    got, sent = lax.optimization_barrier((got, hidden[0]))
    piece = pick(got[:, :BLOCK], origin % 8)
    rows_along = pick(got.reshape(4, 2, 160, 128)[:, :, BLOCK:], c, 1)
    piece = jnp.where(zh == origin // 8, piece, lax.ppermute(piece, "zh", ring(2, 1)))

    blocks = segment_row.reshape(4, 8, BLOCK)
    start = starts_of(segment_row, pick(blocks, y, 1))
    token = (jnp.arange(4)[:, None] * 8 + y) * BLOCK + jnp.arange(BLOCK)[None]
    q_angles = jnp.swapaxes(angles_of(token - start), 1, 2)
    q_turns = (jnp.cos(q_angles), jnp.sin(q_angles))
    split = queries[0].reshape(BLOCK, 4, GROUP * HEAD_DIM).transpose(1, 0, 2)

    rows_along = rows_along.astype(jnp.int32)
    along = pick(rows_along, z * 8 + y, 1)
    start_along = jax.vmap(starts_of)(rows_along, along)
    k_angles = angles_of((z * 8 + y) * BLOCK + jnp.arange(BLOCK)[None] - start_along)
    k_turns = (jnp.cos(k_angles), jnp.sin(k_angles))

    own = hidden[0]
    left = lax.ppermute(sent, "x", ring(4, 1))
    right = lax.ppermute(sent, "x", ring(4, -1))
    part = spread(piece, ("z1", "y1"), 8).reshape(8 * BLOCK, 128)
    part, left, right, start, q_turns, split, k_turns = lax.optimization_barrier(
        (part, left, right, start, q_turns, split, k_turns)
    )
    mine = spread(part, ("z0", "y0"), 4).reshape(32, BLOCK, 128)
    far_low = lax.ppermute(left[:64], "x", ring(4, 1))
    far_high = lax.ppermute(right[64:], "x", ring(4, -1))
    mine, *arrived = lax.optimization_barrier((mine, far_low[:8, :128], far_high[:8, :128]))
    other = lax.ppermute(mine, "c", ring(2, 1))
    rows = [own, left, far_low, far_high, right]
    first = project_first(rows, mine, arrived)
    both = project_second(
        jnp.stack([x, c]).astype(jnp.int32), rows, other, first, *k_turns
    )
    own_kv = exchange(exchange(both, "x"), Z)

    own_kv, split = lax.optimization_barrier((own_kv, split))
    q_turned = turn_queries(exchange(split, Z), *q_turns)

    where = jnp.concatenate([y[None], start[:, 0]]).astype(jnp.int32)
    start = start[:, None, :]
    kv = {0: own_kv}
    for step in range(1, 5):
        if step == 4:
            state = attend(((0,), (1, 2), (-1, -2)), where, q_turned, start, kv)
            kv[3], kv[-3], *state = lax.optimization_barrier((kv[3], kv[-3], *state))
            kv[FAR_LOW] = lax.ppermute(kv[3][:2], Y, ring(8, 1))
            kv[FAR_HIGH] = lax.ppermute(kv[-3][2:], Y, ring(8, -1))
        else:
            kv[step] = lax.ppermute(kv[step - 1], Y, ring(8, 1))
            kv[-step] = lax.ppermute(kv[1 - step], Y, ring(8, -1))
    state = attend(((3,), (-3,)), where, q_turned, start, kv, state)
    mixed = attend(((FAR_LOW,), (FAR_HIGH,)), where, q_turned, start, kv, state, closing=True)
    back = exchange(mixed, Z)
    return back.transpose(1, 0, 2).reshape(1, BLOCK, HEADS * HEAD_DIM)


def solution(mesh):
    fine = Mesh(mesh.devices.reshape(SIZES), AXES)
    placed = (
        P(REP, SEQ, None),
        P(REP, SEQ, None),
        P(REP, SEQ, None),
        P(REP, None),
        P(),
    )
    return jax.shard_map(
        on_device, mesh=fine, in_specs=placed, out_specs=P(REP, SEQ, None), check_vma=False
    )
```

```python
import functools
import math

import jax
import jax.numpy as jnp
from jax import lax
from jax.experimental import pallas as pl
from jax.experimental.pallas import tpu as pltpu
from jax.sharding import Mesh
from jax.sharding import PartitionSpec as P

HEADS = 32
KV_HEADS = 4
HEAD_DIM = 128
GROUP = HEADS // KV_HEADS
THETA = 1000000.0
BLOCK = 128
LOW = -1e30
DOCS = 6
FAR_LOW, FAR_HIGH = 4, -4

AXES = ("z1", "z0", "y1", "y0", "zh", "x", "c")
SIZES = (2, 2, 4, 2, 2, 4, 2)
SEQ = ("z1", "z0", "y1", "y0")
REP = ("zh", "x", "c")
Y = ("y1", "y0")
Z = ("z1", "z0")


def ring(size, shift):
    return [(i, (i + shift) % size) for i in range(size)]


def pick(value, index, axis=0):
    return lax.dynamic_index_in_dim(value, index, axis, keepdims=False)


def exchange(value, axes):
    return lax.all_to_all(value, axes, split_axis=0, concat_axis=0, tiled=True)


def spread(value, axes, members):
    return exchange(jnp.broadcast_to(value[None], (members,) + value.shape), axes)


def angles_of(positions):
    half = HEAD_DIM // 2
    freqs = THETA ** (-(jnp.arange(half, dtype=jnp.float32) * 2.0) / HEAD_DIM)
    return positions.astype(jnp.float32)[..., None] * freqs


def starts_of(segment_rows, segments):
    docs = jnp.arange(1, DOCS, dtype=jnp.int32)
    begins = jnp.sum((segment_rows[..., None, :] < docs[:, None]).astype(jnp.int32), axis=-1)
    passed = segments[..., None, :] >= docs[:, None]
    return jnp.max(jnp.where(passed, begins[..., None], 0), axis=-2)


VMEM = pl.BlockSpec(memory_space=pltpu.VMEM)
SMEM = pl.BlockSpec(memory_space=pltpu.SMEM)


def call(kernel, out_shape, specs, cost, scratch=()):
    flops, moved = cost
    return pl.pallas_call(
        kernel,
        out_shape=out_shape,
        in_specs=specs,
        out_specs=jax.tree.map(lambda _: VMEM, out_shape),
        scratch_shapes=list(scratch),
        compiler_params=pltpu.CompilerParams(vmem_limit_bytes=32 * 2**20),
        cost_estimate=pl.CostEstimate(flops=flops, bytes_accessed=moved, transcendentals=0),
    )


def turn_kernel(q_ref, cos_ref, sin_ref, out_ref):
    half = HEAD_DIM // 2

    @pl.loop(0, 4)
    def _(z):
        cosine, sine = cos_ref[z], sin_ref[z]
        for h in range(GROUP):
            cols = slice(h * HEAD_DIM, (h + 1) * HEAD_DIM)
            t = q_ref[z, :, cols].astype(jnp.float32).T
            a, b = t[:half], t[half:]
            out_ref[z, :half, cols] = (a * cosine - b * sine).astype(jnp.bfloat16)
            out_ref[z, half:, cols] = (b * cosine + a * sine).astype(jnp.bfloat16)


def turn_queries(q, cosine, sine):
    return call(
        turn_kernel,
        jax.ShapeDtypeStruct((4, HEAD_DIM, GROUP * BLOCK), jnp.bfloat16),
        [VMEM] * 3,
        (4 * 2**20, 2 * 2**20),
    )(q, cosine, sine)


def multiply(hidden_refs, weight_ref, out_ref):
    at = 0
    for hidden_ref in hidden_refs:
        total = None
        for block in range(0, 32, 2):
            z1, z0, y1 = block // 16, block // 8 % 2, block // 2 % 4
            low = z0 * 16 + z1 * 4 + y1
            weight = jnp.concatenate([weight_ref[low], weight_ref[low + 8]], axis=0)
            term = jnp.dot(
                hidden_ref[:, block * 128 : block * 128 + 256],
                weight,
                preferred_element_type=jnp.float32,
            )
            total = term if total is None else total + term
        out_ref[at : at + hidden_ref.shape[0]] = total
        at += hidden_ref.shape[0]


def project_first_kernel(*refs):
    multiply(refs[:5], refs[5], refs[6])


def project_first(hidden, weight):
    return call(
        project_first_kernel,
        jax.ShapeDtypeStruct((4 * BLOCK, HEAD_DIM), jnp.float32),
        [VMEM] * 6,
        (2**29, 5 * 2**20),
    )(*hidden, weight)


def project_second_kernel(*refs):
    where_ref, first_ref, cos_ref, sin_ref, out_ref, second = (refs[0],) + refs[7:]
    half = HEAD_DIM // 2
    multiply(refs[1:6], refs[6], second)
    x, keys_first = where_ref[0], where_ref[1] == 0
    for d in range(4):
        pack = (x - d) & 3
        one, two = first_ref[d * BLOCK : (d + 1) * BLOCK], second[d * BLOCK : (d + 1) * BLOCK]
        key = jnp.where(keys_first, one, two)
        value = jnp.where(keys_first, two, one)
        a, b = key[:, :half], key[:, half:]
        cosine, sine = cos_ref[pack], sin_ref[pack]
        turned = jnp.concatenate([a * cosine - b * sine, b * cosine + a * sine], axis=1)
        out_ref[pack, 0] = turned.astype(jnp.bfloat16)
        out_ref[pack, 1] = value.T.astype(jnp.bfloat16)


def project_second(where, hidden, weight, first, cosine, sine):
    return call(
        project_second_kernel,
        jax.ShapeDtypeStruct((4, 2, BLOCK, HEAD_DIM), jnp.bfloat16),
        [SMEM] + [VMEM] * 9,
        (2**29, 5 * 2**20),
        [pltpu.VMEM((4 * BLOCK, HEAD_DIM), jnp.float32)],
    )(where, *hidden, weight, first, cosine, sine)


def attend_kernel(tiles, opening, closing, where_ref, q_ref, start_ref, *refs):
    factor = math.log2(math.e) / math.sqrt(HEAD_DIM)
    y = where_ref[0]
    shifts = [shift for tile in tiles for shift in tile]
    kv, rest = dict(zip(shifts, refs)), refs[len(shifts) :]
    if not opening:
        given, rest = rest[:3], rest[3:]
    if closing:
        out_ref, acc, top, total = rest
    else:
        acc, top, total = rest

    @pl.loop(0, 4)
    def _(z):
        block = z * 8 + y
        slot = 0 if closing else z
        start = start_ref[z]
        row_at = block * BLOCK + lax.broadcasted_iota(jnp.int32, (BLOCK, BLOCK), 1)
        if opening:
            top[slot] = jnp.full(top.shape[1:], LOW, jnp.float32)
            total[slot] = jnp.zeros(total.shape[1:], jnp.float32)
            acc[slot] = jnp.zeros(acc.shape[1:], jnp.float32)
        else:
            for ref, source in zip((acc, top, total), given):
                ref[slot] = source[z]

        def turn(step, carry):
            zz = z - step
            for tile in tiles:
                places = [zz * 8 + ((y - shift) & 7) for shift in tile]
                needed = [
                    (place <= block) & ((place + 1) * BLOCK > where_ref[1 + z])
                    for place in places
                ]

                if tile == (FAR_LOW,):
                    needed.append(zz < 2)
                if tile == (FAR_HIGH,):
                    needed.append(zz >= 2)
                halved = tile in ((FAR_LOW,), (FAR_HIGH,))
                row = zz & 1 if halved else zz

                @pl.when(functools.reduce(jnp.logical_and if halved else jnp.logical_or, needed))
                def _(row=row, tile=tile, places=places):
                    key = jnp.concatenate([kv[shift][row, 0] for shift in tile], axis=0)
                    val = jnp.concatenate([kv[shift][row, 1] for shift in tile], axis=1)
                    allowed = []
                    for place in places:
                        at = place * BLOCK + lax.broadcasted_iota(jnp.int32, (BLOCK, BLOCK), 0)
                        allowed.append((at >= start) & (at <= row_at))
                    allowed = jnp.concatenate(allowed, axis=0)
                    for h in range(GROUP):
                        cols = slice(h * BLOCK, (h + 1) * BLOCK)
                        s = jnp.dot(key, q_ref[z, :, cols], preferred_element_type=jnp.float32)
                        s = jnp.where(allowed, s, LOW)
                        old = top[slot, :, cols]
                        new = jnp.maximum(old, jnp.max(s, axis=0, keepdims=True))
                        p = jnp.exp2((s - new) * factor)
                        scale = jnp.exp2((old - new) * factor)
                        top[slot, :, cols] = new
                        total[slot, :, cols] = total[slot, :, cols] * scale + jnp.sum(
                            p, axis=0, keepdims=True
                        )
                        acc[slot, :, cols] = acc[slot, :, cols] * scale + jnp.dot(
                            val, p.astype(jnp.bfloat16), preferred_element_type=jnp.float32
                        )

            return carry

        lax.fori_loop(0, z + 1, turn, 0)
        if closing:
            for h in range(GROUP):
                cols = slice(h * BLOCK, (h + 1) * BLOCK)
                mixed = acc[slot, :, cols] / total[slot, :, cols]
                out_ref[z, :, cols] = mixed.T.astype(jnp.bfloat16)


def attend(tiles, where, q, start, kv, state=None, closing=False):
    rows = GROUP * BLOCK
    slots = 1 if closing else 4
    shapes = [(slots, HEAD_DIM, rows), (slots, 1, rows), (slots, 1, rows)]
    held = [jax.ShapeDtypeStruct(shape, jnp.float32) for shape in shapes]
    given = [] if state is None else list(state)
    shifts = [shift for tile in tiles for shift in tile]
    out = jax.ShapeDtypeStruct((4, BLOCK, rows), jnp.bfloat16)
    return call(
        functools.partial(attend_kernel, tiles, state is None, closing),
        out if closing else held,
        [SMEM] + [VMEM] * (2 + len(shifts) + len(given)),
        (len(shifts) * 2**30, 4 * 2**20),
        [pltpu.VMEM(shape, jnp.float32) for shape in shapes] if closing else (),
    )(where, q, start, *[kv[shift] for shift in shifts], *given)


def on_device(hidden, queries, weight_copies, segment_ids, owner):
    y, z = lax.axis_index(Y), lax.axis_index(Z)
    x, c, zh = lax.axis_index("x"), lax.axis_index("c"), lax.axis_index("zh")
    segment_row = segment_ids[0]
    origin = owner[0] % 16

    pieces = weight_copies[0].reshape(BLOCK, 2, 4, 128).transpose(2, 1, 0, 3)
    row = segment_row.astype(jnp.bfloat16).reshape(1, 1, 32, 128)
    pieces = jnp.concatenate([pieces, jnp.broadcast_to(row, (4, 2, 32, 128))], axis=2)
    got = exchange(pieces.reshape(8, 160, 128), ("x", "c"))
    piece = pick(got[:, :BLOCK], origin % 8)
    rows_along = pick(got.reshape(4, 2, 160, 128)[:, :, BLOCK:], c, 1)
    piece = jnp.where(zh == origin // 8, piece, lax.ppermute(piece, "zh", ring(2, 1)))

    own = hidden[0]
    left = lax.ppermute(own, "x", ring(4, 1))
    right = lax.ppermute(own, "x", ring(4, -1))
    part = spread(piece, ("z1", "y1"), 8).reshape(8 * BLOCK, 128)
    part, left, right = lax.optimization_barrier((part, left, right))
    mine = spread(part, ("z0", "y0"), 4).reshape(32, BLOCK, 128)
    far_low = lax.ppermute(left[:64], "x", ring(4, 1))
    far_high = lax.ppermute(right[64:], "x", ring(4, -1))

    blocks = segment_row.reshape(4, 8, BLOCK)
    start = starts_of(segment_row, pick(blocks, y, 1).reshape(-1)).reshape(4, BLOCK)
    token = (jnp.arange(4)[:, None] * 8 + y) * BLOCK + jnp.arange(BLOCK)[None]
    q_angles = jnp.swapaxes(angles_of(token - start), 1, 2)
    q_turns = (jnp.cos(q_angles), jnp.sin(q_angles))
    split = queries[0].reshape(BLOCK, 4, GROUP * HEAD_DIM).transpose(1, 0, 2)

    rows_along = rows_along.astype(jnp.int32)
    along = pick(rows_along, z * 8 + y, 1)
    start_along = starts_of(rows_along.reshape(4, -1), along)
    k_angles = angles_of((z * 8 + y) * BLOCK + jnp.arange(BLOCK)[None] - start_along)
    k_turns = (jnp.cos(k_angles), jnp.sin(k_angles))

    mine, far_low, far_high, start, q_turns, split, k_turns = lax.optimization_barrier(
        (mine, far_low, far_high, start, q_turns, split, k_turns)
    )
    other = lax.ppermute(mine, "c", ring(2, 1))
    rows = [own, left, far_low, far_high, right]
    first = project_first(rows, mine)
    both = project_second(
        jnp.stack([x, c]).astype(jnp.int32), rows, other, first, *k_turns
    )
    own_kv = exchange(exchange(both, "x"), Z)

    own_kv, split = lax.optimization_barrier((own_kv, split))
    q_turned = turn_queries(exchange(split, Z), *q_turns)

    where = jnp.concatenate([y[None], start[:, 0]]).astype(jnp.int32)
    start = start[:, None, :]
    kv = {0: own_kv}
    for step in range(1, 5):
        if step == 4:
            state = attend(((0,), (1, 2), (-1, -2)), where, q_turned, start, kv)
            kv[3], kv[-3], *state = lax.optimization_barrier((kv[3], kv[-3], *state))
            kv[FAR_LOW] = lax.ppermute(kv[3][:2], Y, ring(8, 1))
            kv[FAR_HIGH] = lax.ppermute(kv[-3][2:], Y, ring(8, -1))
        else:
            kv[step] = lax.ppermute(kv[step - 1], Y, ring(8, 1))
            kv[-step] = lax.ppermute(kv[1 - step], Y, ring(8, -1))
    state = attend(((3,), (-3,)), where, q_turned, start, kv, state)
    mixed = attend(((FAR_LOW,), (FAR_HIGH,)), where, q_turned, start, kv, state, closing=True)
    back = exchange(mixed, Z)
    return back.transpose(1, 0, 2).reshape(1, BLOCK, HEADS * HEAD_DIM)


def solution(mesh):
    fine = Mesh(mesh.devices.reshape(SIZES), AXES)
    placed = (
        P(REP, SEQ, None),
        P(REP, SEQ, None),
        P(REP, SEQ, None),
        P(REP, None),
        P(),
    )
    return jax.shard_map(
        on_device, mesh=fine, in_specs=placed, out_specs=P(REP, SEQ, None), check_vma=False
    )
```

```python
import functools
import math

import jax
import jax.numpy as jnp
from jax import lax
from jax.experimental import pallas as pl
from jax.experimental.pallas import tpu as pltpu
from jax.sharding import Mesh
from jax.sharding import PartitionSpec as P

HEADS = 32
KV_HEADS = 4
HEAD_DIM = 128
GROUP = HEADS // KV_HEADS
THETA = 1000000.0
BLOCK = 128
LOW = -1e30
DOCS = 6
FAR_LOW, FAR_HIGH = 4, -4

AXES = ("z1", "z0", "y1", "y0", "zh", "x", "c")
SIZES = (2, 2, 4, 2, 2, 4, 2)
SEQ = ("z1", "z0", "y1", "y0")
REP = ("zh", "x", "c")
Y = ("y1", "y0")
Z = ("z1", "z0")


def ring(size, shift):
    return [(i, (i + shift) % size) for i in range(size)]


def pick(value, index, axis=0):
    return lax.dynamic_index_in_dim(value, index, axis, keepdims=False)


def exchange(value, axes):
    return lax.all_to_all(value, axes, split_axis=0, concat_axis=0, tiled=True)


def spread(value, axes, members):
    return exchange(jnp.broadcast_to(value[None], (members,) + value.shape), axes)


def angles_of(positions):
    half = HEAD_DIM // 2
    freqs = THETA ** (-(jnp.arange(half, dtype=jnp.float32) * 2.0) / HEAD_DIM)
    return positions.astype(jnp.float32)[..., None] * freqs


def starts_of(segment_rows, segments):
    docs = jnp.arange(1, DOCS, dtype=jnp.int32)
    begins = jnp.sum((segment_rows[..., None, :] < docs[:, None]).astype(jnp.int32), axis=-1)
    passed = segments[..., None, :] >= docs[:, None]
    return jnp.max(jnp.where(passed, begins[..., None], 0), axis=-2)


VMEM = pl.BlockSpec(memory_space=pltpu.VMEM)
SMEM = pl.BlockSpec(memory_space=pltpu.SMEM)


def call(kernel, out_shape, specs, cost, scratch=()):
    flops, moved = cost
    return pl.pallas_call(
        kernel,
        out_shape=out_shape,
        in_specs=specs,
        out_specs=jax.tree.map(lambda _: VMEM, out_shape),
        scratch_shapes=list(scratch),
        compiler_params=pltpu.CompilerParams(vmem_limit_bytes=32 * 2**20),
        cost_estimate=pl.CostEstimate(flops=flops, bytes_accessed=moved, transcendentals=0),
    )


def turn_kernel(q_ref, cos_ref, sin_ref, out_ref):
    half = HEAD_DIM // 2

    @pl.loop(0, 4)
    def _(z):
        cosine, sine = cos_ref[z], sin_ref[z]
        for h in range(GROUP):
            cols = slice(h * HEAD_DIM, (h + 1) * HEAD_DIM)
            t = q_ref[z, :, cols].astype(jnp.float32).T
            a, b = t[:half], t[half:]
            out_ref[z, :half, cols] = (a * cosine - b * sine).astype(jnp.bfloat16)
            out_ref[z, half:, cols] = (b * cosine + a * sine).astype(jnp.bfloat16)


def turn_queries(q, cosine, sine):
    return call(
        turn_kernel,
        jax.ShapeDtypeStruct((4, HEAD_DIM, GROUP * BLOCK), jnp.bfloat16),
        [VMEM] * 3,
        (4 * 2**20, 2 * 2**20),
    )(q, cosine, sine)


def multiply(hidden_refs, weight_ref, out_ref):
    at = 0
    for hidden_ref in hidden_refs:
        total = None
        for block in range(0, 32, 2):
            z1, z0, y1 = block // 16, block // 8 % 2, block // 2 % 4
            low = z0 * 16 + z1 * 4 + y1
            weight = jnp.concatenate([weight_ref[low], weight_ref[low + 8]], axis=0)
            term = jnp.dot(
                hidden_ref[:, block * 128 : block * 128 + 256],
                weight,
                preferred_element_type=jnp.float32,
            )
            total = term if total is None else total + term
        out_ref[at : at + hidden_ref.shape[0]] = total
        at += hidden_ref.shape[0]


def project_first_kernel(*refs):
    multiply(refs[:5], refs[5], refs[6])


def project_first(hidden, weight):
    return call(
        project_first_kernel,
        jax.ShapeDtypeStruct((4 * BLOCK, HEAD_DIM), jnp.float32),
        [VMEM] * 6,
        (2**29, 5 * 2**20),
    )(*hidden, weight)


def project_second_kernel(*refs):
    where_ref, first_ref, cos_ref, sin_ref, out_ref, second = (refs[0],) + refs[7:]
    half = HEAD_DIM // 2
    multiply(refs[1:6], refs[6], second)
    x, keys_first = where_ref[0], where_ref[1] == 0
    for d in range(4):
        pack = (x - d) & 3
        one, two = first_ref[d * BLOCK : (d + 1) * BLOCK], second[d * BLOCK : (d + 1) * BLOCK]
        key = jnp.where(keys_first, one, two)
        value = jnp.where(keys_first, two, one)
        a, b = key[:, :half], key[:, half:]
        cosine, sine = cos_ref[pack], sin_ref[pack]
        turned = jnp.concatenate([a * cosine - b * sine, b * cosine + a * sine], axis=1)
        out_ref[pack, 0] = turned.astype(jnp.bfloat16)
        out_ref[pack, 1] = value.T.astype(jnp.bfloat16)


def project_second(where, hidden, weight, first, cosine, sine):
    return call(
        project_second_kernel,
        jax.ShapeDtypeStruct((4, 2, BLOCK, HEAD_DIM), jnp.bfloat16),
        [SMEM] + [VMEM] * 9,
        (2**29, 5 * 2**20),
        [pltpu.VMEM((4 * BLOCK, HEAD_DIM), jnp.float32)],
    )(where, *hidden, weight, first, cosine, sine)


def attend_kernel(tiles, opening, closing, where_ref, q_ref, start_ref, *refs):
    factor = math.log2(math.e) / math.sqrt(HEAD_DIM)
    y = where_ref[0]
    shifts = [shift for tile in tiles for shift in tile]
    kv, rest = dict(zip(shifts, refs)), refs[len(shifts) :]
    if not opening:
        given, rest = rest[:3], rest[3:]
    if closing:
        out_ref, acc, top, total = rest
    else:
        acc, top, total = rest

    @pl.loop(0, 4)
    def _(z):
        block = z * 8 + y
        slot = 0 if closing else z
        start = start_ref[z]
        row_at = block * BLOCK + lax.broadcasted_iota(jnp.int32, (BLOCK, BLOCK), 1)
        if opening:
            top[slot] = jnp.full(top.shape[1:], LOW, jnp.float32)
            total[slot] = jnp.zeros(total.shape[1:], jnp.float32)
            acc[slot] = jnp.zeros(acc.shape[1:], jnp.float32)
        else:
            for ref, source in zip((acc, top, total), given):
                ref[slot] = source[z]

        def turn(step, carry):
            zz = z - step
            for tile in tiles:
                places = [zz * 8 + ((y - shift) & 7) for shift in tile]
                needed = [
                    (place <= block) & ((place + 1) * BLOCK > where_ref[1 + z])
                    for place in places
                ]

                if tile == (FAR_LOW,):
                    needed.append(zz < 2)
                if tile == (FAR_HIGH,):
                    needed.append(zz >= 2)
                halved = tile in ((FAR_LOW,), (FAR_HIGH,))
                row = zz & 1 if halved else zz

                @pl.when(functools.reduce(jnp.logical_and if halved else jnp.logical_or, needed))
                def _(row=row, tile=tile, places=places):
                    key = jnp.concatenate([kv[shift][row, 0] for shift in tile], axis=0)
                    val = jnp.concatenate([kv[shift][row, 1] for shift in tile], axis=1)
                    allowed = []
                    for place in places:
                        at = place * BLOCK + lax.broadcasted_iota(jnp.int32, (BLOCK, BLOCK), 0)
                        allowed.append((at >= start) & (at <= row_at))
                    allowed = jnp.concatenate(allowed, axis=0)
                    for h in range(GROUP):
                        cols = slice(h * BLOCK, (h + 1) * BLOCK)
                        s = jnp.dot(key, q_ref[z, :, cols], preferred_element_type=jnp.float32)
                        s = jnp.where(allowed, s, LOW)
                        old = top[slot, :, cols]
                        new = jnp.maximum(old, jnp.max(s, axis=0, keepdims=True))
                        p = jnp.exp2((s - new) * factor)
                        scale = jnp.exp2((old - new) * factor)
                        top[slot, :, cols] = new
                        total[slot, :, cols] = total[slot, :, cols] * scale + jnp.sum(
                            p, axis=0, keepdims=True
                        )
                        acc[slot, :, cols] = acc[slot, :, cols] * scale + jnp.dot(
                            val, p.astype(jnp.bfloat16), preferred_element_type=jnp.float32
                        )

            return carry

        lax.fori_loop(0, z + 1, turn, 0)
        if closing:
            for h in range(GROUP):
                cols = slice(h * BLOCK, (h + 1) * BLOCK)
                mixed = acc[slot, :, cols] / total[slot, :, cols]
                out_ref[z, :, cols] = mixed.T.astype(jnp.bfloat16)


def attend(tiles, where, q, start, kv, state=None, closing=False):
    rows = GROUP * BLOCK
    slots = 1 if closing else 4
    shapes = [(slots, HEAD_DIM, rows), (slots, 1, rows), (slots, 1, rows)]
    held = [jax.ShapeDtypeStruct(shape, jnp.float32) for shape in shapes]
    given = [] if state is None else list(state)
    shifts = [shift for tile in tiles for shift in tile]
    out = jax.ShapeDtypeStruct((4, BLOCK, rows), jnp.bfloat16)
    return call(
        functools.partial(attend_kernel, tiles, state is None, closing),
        out if closing else held,
        [SMEM] + [VMEM] * (2 + len(shifts) + len(given)),
        (len(shifts) * 2**30, 4 * 2**20),
        [pltpu.VMEM(shape, jnp.float32) for shape in shapes] if closing else (),
    )(where, q, start, *[kv[shift] for shift in shifts], *given)


def on_device(hidden, queries, weight_copies, segment_ids, owner):
    y, z = lax.axis_index(Y), lax.axis_index(Z)
    x, c, zh = lax.axis_index("x"), lax.axis_index("c"), lax.axis_index("zh")
    segment_row = segment_ids[0]
    origin = owner[0] % 16

    pieces = weight_copies[0].reshape(BLOCK, 2, 4, 128).transpose(2, 1, 0, 3)
    row = segment_row.astype(jnp.bfloat16).reshape(1, 1, 32, 128)
    pieces = jnp.concatenate([pieces, jnp.broadcast_to(row, (4, 2, 32, 128))], axis=2)
    got = exchange(pieces.reshape(8, 160, 128), ("x", "c"))
    piece = pick(got[:, :BLOCK], origin % 8)
    rows_along = pick(got.reshape(4, 2, 160, 128)[:, :, BLOCK:], c, 1)
    piece = jnp.where(zh == origin // 8, piece, lax.ppermute(piece, "zh", ring(2, 1)))

    own = hidden[0]
    left = lax.ppermute(own, "x", ring(4, 1))
    right = lax.ppermute(own, "x", ring(4, -1))
    part = spread(piece, ("z1", "y1"), 8).reshape(8 * BLOCK, 128)
    part, left, right = lax.optimization_barrier((part, left, right))
    mine = spread(part, ("z0", "y0"), 4).reshape(32, BLOCK, 128)
    far_low = lax.ppermute(left[:64], "x", ring(4, 1))
    far_high = lax.ppermute(right[64:], "x", ring(4, -1))

    blocks = segment_row.reshape(4, 8, BLOCK)
    start = starts_of(segment_row, pick(blocks, y, 1).reshape(-1)).reshape(4, BLOCK)
    token = (jnp.arange(4)[:, None] * 8 + y) * BLOCK + jnp.arange(BLOCK)[None]
    q_angles = jnp.swapaxes(angles_of(token - start), 1, 2)
    q_turns = (jnp.cos(q_angles), jnp.sin(q_angles))
    split = queries[0].reshape(BLOCK, 4, GROUP * HEAD_DIM).transpose(1, 0, 2)

    rows_along = rows_along.astype(jnp.int32)
    along = pick(rows_along, z * 8 + y, 1)
    start_along = starts_of(rows_along.reshape(4, -1), along)
    k_angles = angles_of((z * 8 + y) * BLOCK + jnp.arange(BLOCK)[None] - start_along)
    k_turns = (jnp.cos(k_angles), jnp.sin(k_angles))

    mine, far_low, far_high, start, q_turns, split, k_turns = lax.optimization_barrier(
        (mine, far_low, far_high, start, q_turns, split, k_turns)
    )
    other = lax.ppermute(mine, "c", ring(2, 1))
    rows = [own, left, far_low, far_high, right]
    first = project_first(rows, mine)
    both = project_second(
        jnp.stack([x, c]).astype(jnp.int32), rows, other, first, *k_turns
    )
    own_kv = exchange(exchange(both, "x"), Z)

    own_kv, split = lax.optimization_barrier((own_kv, split))
    q_turned = turn_queries(exchange(split, Z), *q_turns)

    where = jnp.concatenate([y[None], start[:, 0]]).astype(jnp.int32)
    start = start[:, None, :]
    kv = {0: own_kv}
    for step in (1, 2):
        kv[step] = lax.ppermute(kv[step - 1], Y, ring(8, 1))
        kv[-step] = lax.ppermute(kv[1 - step], Y, ring(8, -1))
    kv[3] = lax.ppermute(kv[2], Y, ring(8, 1))
    state = attend(((0,), (1, 2)), where, q_turned, start, kv)
    kv[-2], *state = lax.optimization_barrier((kv[-2], *state))
    kv[-3] = lax.ppermute(kv[-2], Y, ring(8, -1))
    state = attend(((-1, -2),), where, q_turned, start, kv, state)
    kv[3], *state = lax.optimization_barrier((kv[3], *state))
    kv[FAR_LOW] = lax.ppermute(kv[3][:2], Y, ring(8, 1))
    state = attend(((3,),), where, q_turned, start, kv, state)
    kv[-3], *state = lax.optimization_barrier((kv[-3], *state))
    kv[FAR_HIGH] = lax.ppermute(kv[-3][2:], Y, ring(8, -1))
    state = attend(((-3,),), where, q_turned, start, kv, state)
    mixed = attend(((FAR_LOW,), (FAR_HIGH,)), where, q_turned, start, kv, state, closing=True)
    back = exchange(mixed, Z)
    return back.transpose(1, 0, 2).reshape(1, BLOCK, HEADS * HEAD_DIM)


def solution(mesh):
    fine = Mesh(mesh.devices.reshape(SIZES), AXES)
    placed = (
        P(REP, SEQ, None),
        P(REP, SEQ, None),
        P(REP, SEQ, None),
        P(REP, None),
        P(),
    )
    return jax.shard_map(
        on_device, mesh=fine, in_specs=placed, out_specs=P(REP, SEQ, None), check_vma=False
    )
```

```python
import functools
import math

import jax
import jax.numpy as jnp
from jax import lax
from jax.experimental import pallas as pl
from jax.experimental.pallas import tpu as pltpu
from jax.sharding import Mesh
from jax.sharding import PartitionSpec as P

HEADS = 32
KV_HEADS = 4
HEAD_DIM = 128
GROUP = HEADS // KV_HEADS
THETA = 1000000.0
BLOCK = 128
LOW = -1e30
DOCS = 6

AXES = ("z1", "z0", "y1", "y0", "zh", "x", "c")
SIZES = (2, 2, 4, 2, 2, 4, 2)
SEQ = ("z1", "z0", "y1", "y0")
REP = ("zh", "x", "c")
Y = ("y1", "y0")
Z = ("z1", "z0")


def ring(size, shift):
    return [(i, (i + shift) % size) for i in range(size)]


def pick(value, index, axis=0):
    return lax.dynamic_index_in_dim(value, index, axis, keepdims=False)


def exchange(value, axes):
    return lax.all_to_all(value, axes, split_axis=0, concat_axis=0, tiled=True)


def spread(value, axes, members):
    return exchange(jnp.broadcast_to(value[None], (members,) + value.shape), axes)


def angles_of(positions):
    half = HEAD_DIM // 2
    freqs = THETA ** (-(jnp.arange(half, dtype=jnp.float32) * 2.0) / HEAD_DIM)
    return positions.astype(jnp.float32)[..., None] * freqs


def starts_of(segment_rows, segments):
    docs = jnp.arange(1, DOCS, dtype=jnp.int32)
    begins = jnp.sum((segment_rows[..., None, :] < docs[:, None]).astype(jnp.int32), axis=-1)
    passed = segments[..., None, :] >= docs[:, None]
    return jnp.max(jnp.where(passed, begins[..., None], 0), axis=-2)


VMEM = pl.BlockSpec(memory_space=pltpu.VMEM)
SMEM = pl.BlockSpec(memory_space=pltpu.SMEM)


def call(kernel, out_shape, specs, cost, scratch=()):
    flops, moved = cost
    return pl.pallas_call(
        kernel,
        out_shape=out_shape,
        in_specs=specs,
        out_specs=jax.tree.map(lambda _: VMEM, out_shape),
        scratch_shapes=list(scratch),
        compiler_params=pltpu.CompilerParams(vmem_limit_bytes=32 * 2**20),
        cost_estimate=pl.CostEstimate(flops=flops, bytes_accessed=moved, transcendentals=0),
    )


def turn_kernel(q_ref, cos_ref, sin_ref, out_ref):
    half = HEAD_DIM // 2

    @pl.loop(0, 4)
    def _(z):
        cosine, sine = cos_ref[z], sin_ref[z]
        for h in range(GROUP):
            cols = slice(h * HEAD_DIM, (h + 1) * HEAD_DIM)
            t = q_ref[z, :, cols].astype(jnp.float32).T
            a, b = t[:half], t[half:]
            out_ref[z, :half, cols] = (a * cosine - b * sine).astype(jnp.bfloat16)
            out_ref[z, half:, cols] = (b * cosine + a * sine).astype(jnp.bfloat16)


def turn_queries(q, cosine, sine):
    return call(
        turn_kernel,
        jax.ShapeDtypeStruct((4, HEAD_DIM, GROUP * BLOCK), jnp.bfloat16),
        [VMEM] * 3,
        (4 * 2**20, 2 * 2**20),
    )(q, cosine, sine)


def multiply(hidden_refs, weight_ref, out_ref):
    at = 0
    for hidden_ref in hidden_refs:
        total = None
        for block in range(0, 32, 2):
            z1, z0, y1 = block // 16, block // 8 % 2, block // 2 % 4
            low = z0 * 16 + z1 * 4 + y1
            weight = jnp.concatenate([weight_ref[low], weight_ref[low + 8]], axis=0)
            term = jnp.dot(
                hidden_ref[:, block * 128 : block * 128 + 256],
                weight,
                preferred_element_type=jnp.float32,
            )
            total = term if total is None else total + term
        out_ref[at : at + hidden_ref.shape[0]] = total
        at += hidden_ref.shape[0]


def project_first_kernel(*refs):
    multiply(refs[:5], refs[5], refs[6])


def project_first(hidden, weight):
    return call(
        project_first_kernel,
        jax.ShapeDtypeStruct((4 * BLOCK, HEAD_DIM), jnp.float32),
        [VMEM] * 6,
        (2**29, 5 * 2**20),
    )(*hidden, weight)


def project_second_kernel(*refs):
    where_ref, first_ref, cos_ref, sin_ref, out_ref, second = (refs[0],) + refs[7:]
    half = HEAD_DIM // 2
    multiply(refs[1:6], refs[6], second)
    x, keys_first = where_ref[0], where_ref[1] == 0
    for d in range(4):
        pack = (x - d) & 3
        one, two = first_ref[d * BLOCK : (d + 1) * BLOCK], second[d * BLOCK : (d + 1) * BLOCK]
        key = jnp.where(keys_first, one, two)
        value = jnp.where(keys_first, two, one)
        a, b = key[:, :half], key[:, half:]
        cosine, sine = cos_ref[pack], sin_ref[pack]
        turned = jnp.concatenate([a * cosine - b * sine, b * cosine + a * sine], axis=1)
        out_ref[pack, 0] = turned.astype(jnp.bfloat16)
        out_ref[pack, 1] = value.T.astype(jnp.bfloat16)


def project_second(where, hidden, weight, first, cosine, sine):
    return call(
        project_second_kernel,
        jax.ShapeDtypeStruct((4, 2, BLOCK, HEAD_DIM), jnp.bfloat16),
        [SMEM] + [VMEM] * 9,
        (2**29, 5 * 2**20),
        [pltpu.VMEM((4 * BLOCK, HEAD_DIM), jnp.float32)],
    )(where, *hidden, weight, first, cosine, sine)


def attend_kernel(tiles, opening, closing, where_ref, q_ref, start_ref, *refs):
    factor = math.log2(math.e) / math.sqrt(HEAD_DIM)
    y = where_ref[0]
    shifts = [shift for tile in tiles for shift in tile]
    kv, rest = dict(zip(shifts, refs)), refs[len(shifts) :]
    if not opening:
        given, rest = rest[:3], rest[3:]
    if closing:
        out_ref, acc, top, total = rest
    else:
        acc, top, total = rest

    @pl.loop(0, 4)
    def _(z):
        block = z * 8 + y
        slot = 0 if closing else z
        start = start_ref[z]
        row_at = block * BLOCK + lax.broadcasted_iota(jnp.int32, (BLOCK, BLOCK), 1)
        if opening:
            top[slot] = jnp.full(top.shape[1:], LOW, jnp.float32)
            total[slot] = jnp.zeros(total.shape[1:], jnp.float32)
            acc[slot] = jnp.zeros(acc.shape[1:], jnp.float32)
        else:
            for ref, source in zip((acc, top, total), given):
                ref[slot] = source[z]

        def turn(step, carry):
            zz = z - step
            for tile in tiles:
                places = [zz * 8 + ((y - shift) & 7) for shift in tile]
                needed = [
                    (place <= block) & ((place + 1) * BLOCK > where_ref[1 + z])
                    for place in places
                ]


                @pl.when(functools.reduce(jnp.logical_or, needed))
                def _(tile=tile, places=places):
                    key = jnp.concatenate([kv[shift][zz, 0] for shift in tile], axis=0)
                    val = jnp.concatenate([kv[shift][zz, 1] for shift in tile], axis=1)
                    allowed = []
                    for place in places:
                        at = place * BLOCK + lax.broadcasted_iota(jnp.int32, (BLOCK, BLOCK), 0)
                        allowed.append((at >= start) & (at <= row_at))
                    allowed = jnp.concatenate(allowed, axis=0)
                    for h in range(GROUP):
                        cols = slice(h * BLOCK, (h + 1) * BLOCK)
                        s = jnp.dot(key, q_ref[z, :, cols], preferred_element_type=jnp.float32)
                        s = jnp.where(allowed, s, LOW)
                        old = top[slot, :, cols]
                        new = jnp.maximum(old, jnp.max(s, axis=0, keepdims=True))
                        p = jnp.exp2((s - new) * factor)
                        scale = jnp.exp2((old - new) * factor)
                        top[slot, :, cols] = new
                        total[slot, :, cols] = total[slot, :, cols] * scale + jnp.sum(
                            p, axis=0, keepdims=True
                        )
                        acc[slot, :, cols] = acc[slot, :, cols] * scale + jnp.dot(
                            val, p.astype(jnp.bfloat16), preferred_element_type=jnp.float32
                        )

            return carry

        lax.fori_loop(0, z + 1, turn, 0)
        if closing:
            for h in range(GROUP):
                cols = slice(h * BLOCK, (h + 1) * BLOCK)
                mixed = acc[slot, :, cols] / total[slot, :, cols]
                out_ref[z, :, cols] = mixed.T.astype(jnp.bfloat16)


def attend(tiles, where, q, start, kv, state=None, closing=False):
    rows = GROUP * BLOCK
    slots = 1 if closing else 4
    shapes = [(slots, HEAD_DIM, rows), (slots, 1, rows), (slots, 1, rows)]
    held = [jax.ShapeDtypeStruct(shape, jnp.float32) for shape in shapes]
    given = [] if state is None else list(state)
    shifts = [shift for tile in tiles for shift in tile]
    out = jax.ShapeDtypeStruct((4, BLOCK, rows), jnp.bfloat16)
    return call(
        functools.partial(attend_kernel, tiles, state is None, closing),
        out if closing else held,
        [SMEM] + [VMEM] * (2 + len(shifts) + len(given)),
        (len(shifts) * 2**30, 4 * 2**20),
        [pltpu.VMEM(shape, jnp.float32) for shape in shapes] if closing else (),
    )(where, q, start, *[kv[shift] for shift in shifts], *given)


def on_device(hidden, queries, weight_copies, segment_ids, owner):
    y, z = lax.axis_index(Y), lax.axis_index(Z)
    x, c, zh = lax.axis_index("x"), lax.axis_index("c"), lax.axis_index("zh")
    segment_row = segment_ids[0]
    origin = owner[0] % 16

    pieces = weight_copies[0].reshape(BLOCK, 2, 4, 128).transpose(2, 1, 0, 3)
    row = segment_row.astype(jnp.bfloat16).reshape(1, 1, 32, 128)
    pieces = jnp.concatenate([pieces, jnp.broadcast_to(row, (4, 2, 32, 128))], axis=2)
    got = exchange(pieces.reshape(8, 160, 128), ("x", "c"))
    piece = pick(got[:, :BLOCK], origin % 8)
    rows_along = pick(got.reshape(4, 2, 160, 128)[:, :, BLOCK:], c, 1)
    piece = jnp.where(zh == origin // 8, piece, lax.ppermute(piece, "zh", ring(2, 1)))

    own = hidden[0]
    left = lax.ppermute(own, "x", ring(4, 1))
    right = lax.ppermute(own, "x", ring(4, -1))
    part = spread(piece, ("z1", "y1"), 8).reshape(8 * BLOCK, 128)
    part, left, right = lax.optimization_barrier((part, left, right))
    mine = spread(part, ("z0", "y0"), 4).reshape(32, BLOCK, 128)
    far_low = lax.ppermute(left[:64], "x", ring(4, 1))
    far_high = lax.ppermute(right[64:], "x", ring(4, -1))

    blocks = segment_row.reshape(4, 8, BLOCK)
    start = starts_of(segment_row, pick(blocks, y, 1).reshape(-1)).reshape(4, BLOCK)
    token = (jnp.arange(4)[:, None] * 8 + y) * BLOCK + jnp.arange(BLOCK)[None]
    q_angles = jnp.swapaxes(angles_of(token - start), 1, 2)
    q_turns = (jnp.cos(q_angles), jnp.sin(q_angles))
    split = queries[0].reshape(BLOCK, 4, GROUP * HEAD_DIM).transpose(1, 0, 2)

    rows_along = rows_along.astype(jnp.int32)
    along = pick(rows_along, z * 8 + y, 1)
    start_along = starts_of(rows_along.reshape(4, -1), along)
    k_angles = angles_of((z * 8 + y) * BLOCK + jnp.arange(BLOCK)[None] - start_along)
    k_turns = (jnp.cos(k_angles), jnp.sin(k_angles))

    mine, far_low, far_high, start, q_turns, split, k_turns = lax.optimization_barrier(
        (mine, far_low, far_high, start, q_turns, split, k_turns)
    )
    other = lax.ppermute(mine, "c", ring(2, 1))
    rows = [own, left, far_low, far_high, right]
    first = project_first(rows, mine)
    both = project_second(
        jnp.stack([x, c]).astype(jnp.int32), rows, other, first, *k_turns
    )
    own_kv = exchange(exchange(both, "x"), Z)

    own_kv, split = lax.optimization_barrier((own_kv, split))
    q_turned = turn_queries(exchange(split, Z), *q_turns)

    where = jnp.concatenate([y[None], start[:, 0]]).astype(jnp.int32)
    start = start[:, None, :]
    kv = {0: own_kv}
    for step in (1, 2, 3):
        kv[step] = lax.ppermute(kv[step - 1], Y, ring(8, 1))
        kv[-step] = lax.ppermute(kv[1 - step], Y, ring(8, -1))
    state = attend(((0,), (1, 2)), where, q_turned, start, kv)
    kv[3], *state = lax.optimization_barrier((kv[3], *state))
    kv[4] = lax.ppermute(kv[3], Y, ring(8, 1))
    state = attend(((-1, -2), (3,), (-3,)), where, q_turned, start, kv, state)
    mixed = attend(((4,),), where, q_turned, start, kv, state, closing=True)
    back = exchange(mixed, Z)
    return back.transpose(1, 0, 2).reshape(1, BLOCK, HEADS * HEAD_DIM)


def solution(mesh):
    fine = Mesh(mesh.devices.reshape(SIZES), AXES)
    placed = (
        P(REP, SEQ, None),
        P(REP, SEQ, None),
        P(REP, SEQ, None),
        P(REP, None),
        P(),
    )
    return jax.shard_map(
        on_device, mesh=fine, in_specs=placed, out_specs=P(REP, SEQ, None), check_vma=False
    )
```

```python
import functools
import math

import jax
import jax.numpy as jnp
from jax import lax
from jax.experimental import pallas as pl
from jax.experimental.pallas import tpu as pltpu
from jax.sharding import Mesh
from jax.sharding import PartitionSpec as P

HEADS = 32
KV_HEADS = 4
HEAD_DIM = 128
GROUP = HEADS // KV_HEADS
THETA = 1000000.0
BLOCK = 128
LOW = -1e30
DOCS = 6

AXES = ("z1", "z0", "y1", "y0", "zh", "x", "c")
SIZES = (2, 2, 4, 2, 2, 4, 2)
SEQ = ("z1", "z0", "y1", "y0")
REP = ("zh", "x", "c")
Y = ("y1", "y0")
Z = ("z1", "z0")


def ring(size, shift):
    return [(i, (i + shift) % size) for i in range(size)]


def pick(value, index, axis=0):
    return lax.dynamic_index_in_dim(value, index, axis, keepdims=False)


def exchange(value, axes):
    return lax.all_to_all(value, axes, split_axis=0, concat_axis=0, tiled=True)


def spread(value, axes, members):
    return exchange(jnp.broadcast_to(value[None], (members,) + value.shape), axes)


def angles_of(positions):
    half = HEAD_DIM // 2
    freqs = THETA ** (-(jnp.arange(half, dtype=jnp.float32) * 2.0) / HEAD_DIM)
    return positions.astype(jnp.float32)[..., None] * freqs


def starts_of(segment_rows, segments):
    docs = jnp.arange(1, DOCS, dtype=jnp.int32)
    begins = jnp.sum((segment_rows[..., None, :] < docs[:, None]).astype(jnp.int32), axis=-1)
    passed = segments[..., None, :] >= docs[:, None]
    return jnp.max(jnp.where(passed, begins[..., None], 0), axis=-2)


VMEM = pl.BlockSpec(memory_space=pltpu.VMEM)
SMEM = pl.BlockSpec(memory_space=pltpu.SMEM)


def call(kernel, out_shape, specs, cost, scratch=()):
    flops, moved = cost
    return pl.pallas_call(
        kernel,
        out_shape=out_shape,
        in_specs=specs,
        out_specs=jax.tree.map(lambda _: VMEM, out_shape),
        scratch_shapes=list(scratch),
        compiler_params=pltpu.CompilerParams(vmem_limit_bytes=32 * 2**20),
        cost_estimate=pl.CostEstimate(flops=flops, bytes_accessed=moved, transcendentals=0),
    )


def turn_kernel(q_ref, cos_ref, sin_ref, out_ref):
    half = HEAD_DIM // 2

    @pl.loop(0, 4)
    def _(z):
        cosine, sine = cos_ref[z], sin_ref[z]
        for h in range(GROUP):
            cols = slice(h * HEAD_DIM, (h + 1) * HEAD_DIM)
            t = q_ref[z, :, cols].astype(jnp.float32).T
            a, b = t[:half], t[half:]
            out_ref[z, :half, cols] = (a * cosine - b * sine).astype(jnp.bfloat16)
            out_ref[z, half:, cols] = (b * cosine + a * sine).astype(jnp.bfloat16)


def turn_queries(q, cosine, sine):
    return call(
        turn_kernel,
        jax.ShapeDtypeStruct((4, HEAD_DIM, GROUP * BLOCK), jnp.bfloat16),
        [VMEM] * 3,
        (4 * 2**20, 2 * 2**20),
    )(q, cosine, sine)


def multiply(hidden_refs, weight_ref, out_ref):
    at = 0
    for hidden_ref in hidden_refs:
        total = None
        for block in range(0, 32, 2):
            z1, z0, y1 = block // 16, block // 8 % 2, block // 2 % 4
            low = z0 * 16 + z1 * 4 + y1
            weight = jnp.concatenate([weight_ref[low], weight_ref[low + 8]], axis=0)
            term = jnp.dot(
                hidden_ref[:, block * 128 : block * 128 + 256],
                weight,
                preferred_element_type=jnp.float32,
            )
            total = term if total is None else total + term
        out_ref[at : at + hidden_ref.shape[0]] = total
        at += hidden_ref.shape[0]


def project_first_kernel(*refs):
    multiply(refs[:5], refs[5], refs[6])


def project_first(hidden, weight):
    return call(
        project_first_kernel,
        jax.ShapeDtypeStruct((4 * BLOCK, HEAD_DIM), jnp.float32),
        [VMEM] * 6,
        (2**29, 5 * 2**20),
    )(*hidden, weight)


def project_second_kernel(*refs):
    where_ref, first_ref, cos_ref, sin_ref, out_ref, second = (refs[0],) + refs[7:]
    half = HEAD_DIM // 2
    multiply(refs[1:6], refs[6], second)
    x, keys_first = where_ref[0], where_ref[1] == 0
    for d in range(4):
        pack = (x - d) & 3
        one, two = first_ref[d * BLOCK : (d + 1) * BLOCK], second[d * BLOCK : (d + 1) * BLOCK]
        key = jnp.where(keys_first, one, two)
        value = jnp.where(keys_first, two, one)
        a, b = key[:, :half], key[:, half:]
        cosine, sine = cos_ref[pack], sin_ref[pack]
        turned = jnp.concatenate([a * cosine - b * sine, b * cosine + a * sine], axis=1)
        out_ref[pack, 0] = turned.astype(jnp.bfloat16)
        out_ref[pack, 1] = value.T.astype(jnp.bfloat16)


def project_second(where, hidden, weight, first, cosine, sine):
    return call(
        project_second_kernel,
        jax.ShapeDtypeStruct((4, 2, BLOCK, HEAD_DIM), jnp.bfloat16),
        [SMEM] + [VMEM] * 9,
        (2**29, 5 * 2**20),
        [pltpu.VMEM((4 * BLOCK, HEAD_DIM), jnp.float32)],
    )(where, *hidden, weight, first, cosine, sine)


def attend_kernel(tiles, opening, closing, where_ref, q_ref, start_ref, *refs):
    factor = math.log2(math.e) / math.sqrt(HEAD_DIM)
    y = where_ref[0]
    shifts = [shift for tile in tiles for shift in tile]
    kv, rest = dict(zip(shifts, refs)), refs[len(shifts) :]
    if not opening:
        given, rest = rest[:3], rest[3:]
    if closing:
        out_ref, acc, top, total = rest
    else:
        acc, top, total = rest

    @pl.loop(0, 4)
    def _(z):
        block = z * 8 + y
        slot = 0 if closing else z
        start = start_ref[z]
        row_at = block * BLOCK + lax.broadcasted_iota(jnp.int32, (BLOCK, BLOCK), 1)
        if opening:
            top[slot] = jnp.full(top.shape[1:], LOW, jnp.float32)
            total[slot] = jnp.zeros(total.shape[1:], jnp.float32)
            acc[slot] = jnp.zeros(acc.shape[1:], jnp.float32)
        else:
            for ref, source in zip((acc, top, total), given):
                ref[slot] = source[z]

        def turn(step, carry):
            zz = z - step
            for tile in tiles:
                places = [zz * 8 + ((y - shift) & 7) for shift in tile]
                needed = [
                    (place <= block) & ((place + 1) * BLOCK > where_ref[1 + z])
                    for place in places
                ]


                @pl.when(functools.reduce(jnp.logical_or, needed))
                def _(tile=tile, places=places):
                    key = jnp.concatenate([kv[shift][zz, 0] for shift in tile], axis=0)
                    val = jnp.concatenate([kv[shift][zz, 1] for shift in tile], axis=1)
                    allowed = []
                    for place in places:
                        at = place * BLOCK + lax.broadcasted_iota(jnp.int32, (BLOCK, BLOCK), 0)
                        allowed.append((at >= start) & (at <= row_at))
                    allowed = jnp.concatenate(allowed, axis=0)
                    for h in range(GROUP):
                        cols = slice(h * BLOCK, (h + 1) * BLOCK)
                        s = jnp.dot(key, q_ref[z, :, cols], preferred_element_type=jnp.float32)
                        s = jnp.where(allowed, s, LOW)
                        old = top[slot, :, cols]
                        new = jnp.maximum(old, jnp.max(s, axis=0, keepdims=True))
                        p = jnp.exp2((s - new) * factor)
                        scale = jnp.exp2((old - new) * factor)
                        top[slot, :, cols] = new
                        total[slot, :, cols] = total[slot, :, cols] * scale + jnp.sum(
                            p, axis=0, keepdims=True
                        )
                        acc[slot, :, cols] = acc[slot, :, cols] * scale + jnp.dot(
                            val, p.astype(jnp.bfloat16), preferred_element_type=jnp.float32
                        )

            return carry

        lax.fori_loop(0, z + 1, turn, 0)
        if closing:
            for h in range(GROUP):
                cols = slice(h * BLOCK, (h + 1) * BLOCK)
                mixed = acc[slot, :, cols] / total[slot, :, cols]
                out_ref[z, :, cols] = mixed.T.astype(jnp.bfloat16)


def attend(tiles, where, q, start, kv, state=None, closing=False):
    rows = GROUP * BLOCK
    slots = 1 if closing else 4
    shapes = [(slots, HEAD_DIM, rows), (slots, 1, rows), (slots, 1, rows)]
    held = [jax.ShapeDtypeStruct(shape, jnp.float32) for shape in shapes]
    given = [] if state is None else list(state)
    shifts = [shift for tile in tiles for shift in tile]
    out = jax.ShapeDtypeStruct((4, BLOCK, rows), jnp.bfloat16)
    return call(
        functools.partial(attend_kernel, tiles, state is None, closing),
        out if closing else held,
        [SMEM] + [VMEM] * (2 + len(shifts) + len(given)),
        (len(shifts) * 2**30, 4 * 2**20),
        [pltpu.VMEM(shape, jnp.float32) for shape in shapes] if closing else (),
    )(where, q, start, *[kv[shift] for shift in shifts], *given)


def lay_out_kernel(heads_ref, out_ref, done):
    width = GROUP * HEAD_DIM
    copies = [
        pltpu.make_async_copy(
            heads_ref.at[j], out_ref.at[:, pl.ds(j * width, width)], done.at[j]
        )
        for j in range(KV_HEADS)
    ]
    for copy in copies:
        copy.start()
    for copy in copies:
        copy.wait()


def lay_out(heads):
    return pl.pallas_call(
        lay_out_kernel,
        out_shape=jax.ShapeDtypeStruct((BLOCK, HEADS * HEAD_DIM), jnp.bfloat16),
        in_specs=[VMEM],
        out_specs=pl.BlockSpec(memory_space=pl.ANY),
        scratch_shapes=[pltpu.SemaphoreType.DMA((KV_HEADS,))],
        compiler_params=pltpu.CompilerParams(vmem_limit_bytes=32 * 2**20),
    )(heads)


def on_device(hidden, queries, weight_copies, segment_ids, owner):
    y, z = lax.axis_index(Y), lax.axis_index(Z)
    x, c, zh = lax.axis_index("x"), lax.axis_index("c"), lax.axis_index("zh")
    segment_row = segment_ids[0]
    origin = owner[0] % 16

    pieces = weight_copies[0].reshape(BLOCK, 2, 4, 128).transpose(2, 1, 0, 3)
    row = segment_row.astype(jnp.bfloat16).reshape(1, 1, 32, 128)
    pieces = jnp.concatenate([pieces, jnp.broadcast_to(row, (4, 2, 32, 128))], axis=2)
    got = exchange(pieces.reshape(8, 160, 128), ("x", "c"))
    piece = pick(got[:, :BLOCK], origin % 8)
    rows_along = pick(got.reshape(4, 2, 160, 128)[:, :, BLOCK:], c, 1)
    piece = jnp.where(zh == origin // 8, piece, lax.ppermute(piece, "zh", ring(2, 1)))

    own = hidden[0]
    left = lax.ppermute(own, "x", ring(4, 1))
    right = lax.ppermute(own, "x", ring(4, -1))
    part = spread(piece, ("z1", "y1"), 8).reshape(8 * BLOCK, 128)
    part, left, right = lax.optimization_barrier((part, left, right))
    mine = spread(part, ("z0", "y0"), 4).reshape(32, BLOCK, 128)
    far_low = lax.ppermute(left[:64], "x", ring(4, 1))
    far_high = lax.ppermute(right[64:], "x", ring(4, -1))

    blocks = segment_row.reshape(4, 8, BLOCK)
    start = starts_of(segment_row, pick(blocks, y, 1).reshape(-1)).reshape(4, BLOCK)
    token = (jnp.arange(4)[:, None] * 8 + y) * BLOCK + jnp.arange(BLOCK)[None]
    split = queries[0].reshape(BLOCK, 4, GROUP * HEAD_DIM).transpose(1, 0, 2)

    rows_along = rows_along.astype(jnp.int32)
    along = pick(rows_along, z * 8 + y, 1)
    start_along = starts_of(rows_along.reshape(4, -1), along)
    k_angles = angles_of((z * 8 + y) * BLOCK + jnp.arange(BLOCK)[None] - start_along)
    k_turns = (jnp.cos(k_angles), jnp.sin(k_angles))

    mine, far_low, far_high, start, split, k_turns = lax.optimization_barrier(
        (mine, far_low, far_high, start, split, k_turns)
    )
    q_angles = jnp.swapaxes(angles_of(token - start), 1, 2)
    q_turns = (jnp.cos(q_angles), jnp.sin(q_angles))
    other = lax.ppermute(mine, "c", ring(2, 1))
    rows = [own, left, far_low, far_high, right]
    first = project_first(rows, mine)
    both = project_second(
        jnp.stack([x, c]).astype(jnp.int32), rows, other, first, *k_turns
    )
    own_kv = exchange(exchange(both, "x"), Z)

    own_kv, split = lax.optimization_barrier((own_kv, split))
    q_turned = turn_queries(exchange(split, Z), *q_turns)

    where = jnp.concatenate([y[None], start[:, 0]]).astype(jnp.int32)
    start = start[:, None, :]
    kv = {0: own_kv}
    for step in (1, 2, 3):
        kv[step] = lax.ppermute(kv[step - 1], Y, ring(8, 1))
        kv[-step] = lax.ppermute(kv[1 - step], Y, ring(8, -1))
    state = attend(((0,), (1, 2)), where, q_turned, start, kv)
    kv[3], *state = lax.optimization_barrier((kv[3], *state))
    kv[4] = lax.ppermute(kv[3], Y, ring(8, 1))
    state = attend(((-1, -2), (3,), (-3,)), where, q_turned, start, kv, state)
    mixed = attend(((4,),), where, q_turned, start, kv, state, closing=True)
    back = exchange(mixed, Z)
    return lay_out(back)[None]


def solution(mesh):
    fine = Mesh(mesh.devices.reshape(SIZES), AXES)
    placed = (
        P(REP, SEQ, None),
        P(REP, SEQ, None),
        P(REP, SEQ, None),
        P(REP, None),
        P(),
    )
    return jax.shard_map(
        on_device, mesh=fine, in_specs=placed, out_specs=P(REP, SEQ, None), check_vma=False
    )
```

```python
import functools
import math

import jax
import jax.numpy as jnp
from jax import lax
from jax.experimental import pallas as pl
from jax.experimental.pallas import tpu as pltpu
from jax.sharding import Mesh
from jax.sharding import PartitionSpec as P

HEADS = 32
KV_HEADS = 4
HEAD_DIM = 128
GROUP = HEADS // KV_HEADS
THETA = 1000000.0
BLOCK = 128
LOW = -1e30
DOCS = 6

AXES = ("z1", "z0", "y1", "y0", "zh", "x", "c")
SIZES = (2, 2, 4, 2, 2, 4, 2)
SEQ = ("z1", "z0", "y1", "y0")
REP = ("zh", "x", "c")
Y = ("y1", "y0")
Z = ("z1", "z0")


def ring(size, shift):
    return [(i, (i + shift) % size) for i in range(size)]


def pick(value, index, axis=0):
    return lax.dynamic_index_in_dim(value, index, axis, keepdims=False)


def exchange(value, axes):
    return lax.all_to_all(value, axes, split_axis=0, concat_axis=0, tiled=True)


def spread(value, axes, members):
    return exchange(jnp.broadcast_to(value[None], (members,) + value.shape), axes)


def angles_of(positions):
    half = HEAD_DIM // 2
    freqs = THETA ** (-(jnp.arange(half, dtype=jnp.float32) * 2.0) / HEAD_DIM)
    return positions.astype(jnp.float32)[..., None] * freqs


def starts_of(segment_rows, segments):
    docs = jnp.arange(1, DOCS, dtype=jnp.int32)
    begins = jnp.sum((segment_rows[..., None, :] < docs[:, None]).astype(jnp.int32), axis=-1)
    passed = segments[..., None, :] >= docs[:, None]
    return jnp.max(jnp.where(passed, begins[..., None], 0), axis=-2)


VMEM = pl.BlockSpec(memory_space=pltpu.VMEM)
SMEM = pl.BlockSpec(memory_space=pltpu.SMEM)


def call(kernel, out_shape, specs, cost, scratch=()):
    flops, moved = cost
    return pl.pallas_call(
        kernel,
        out_shape=out_shape,
        in_specs=specs,
        out_specs=jax.tree.map(lambda _: VMEM, out_shape),
        scratch_shapes=list(scratch),
        compiler_params=pltpu.CompilerParams(vmem_limit_bytes=32 * 2**20),
        cost_estimate=pl.CostEstimate(flops=flops, bytes_accessed=moved, transcendentals=0),
    )


def turn_kernel(q_ref, cos_ref, sin_ref, out_ref):
    half = HEAD_DIM // 2

    @pl.loop(0, 4)
    def _(z):
        cosine, sine = cos_ref[z], sin_ref[z]
        for h in range(GROUP):
            cols = slice(h * HEAD_DIM, (h + 1) * HEAD_DIM)
            t = q_ref[z, :, cols].astype(jnp.float32).T
            a, b = t[:half], t[half:]
            out_ref[z, :half, cols] = (a * cosine - b * sine).astype(jnp.bfloat16)
            out_ref[z, half:, cols] = (b * cosine + a * sine).astype(jnp.bfloat16)


def turn_queries(q, cosine, sine):
    return call(
        turn_kernel,
        jax.ShapeDtypeStruct((4, HEAD_DIM, GROUP * BLOCK), jnp.bfloat16),
        [VMEM] * 3,
        (4 * 2**20, 2 * 2**20),
    )(q, cosine, sine)


def multiply(hidden_refs, weight_ref, out_ref):
    at = 0
    for hidden_ref in hidden_refs:
        total = None
        for block in range(0, 32, 2):
            z1, z0, y1 = block // 16, block // 8 % 2, block // 2 % 4
            low = z0 * 16 + z1 * 4 + y1
            weight = jnp.concatenate([weight_ref[low], weight_ref[low + 8]], axis=0)
            term = jnp.dot(
                hidden_ref[:, block * 128 : block * 128 + 256],
                weight,
                preferred_element_type=jnp.float32,
            )
            total = term if total is None else total + term
        out_ref[at : at + hidden_ref.shape[0]] = total
        at += hidden_ref.shape[0]


def project_first_kernel(*refs):
    multiply(refs[:5], refs[5], refs[6])


def project_first(hidden, weight):
    return call(
        project_first_kernel,
        jax.ShapeDtypeStruct((4 * BLOCK, HEAD_DIM), jnp.float32),
        [VMEM] * 6,
        (2**29, 5 * 2**20),
    )(*hidden, weight)


def project_second_kernel(*refs):
    where_ref, first_ref, cos_ref, sin_ref, out_ref, second = (refs[0],) + refs[7:]
    half = HEAD_DIM // 2
    multiply(refs[1:6], refs[6], second)
    x, keys_first = where_ref[0], where_ref[1] == 0
    for d in range(4):
        pack = (x - d) & 3
        one, two = first_ref[d * BLOCK : (d + 1) * BLOCK], second[d * BLOCK : (d + 1) * BLOCK]
        key = jnp.where(keys_first, one, two)
        value = jnp.where(keys_first, two, one)
        a, b = key[:, :half], key[:, half:]
        cosine, sine = cos_ref[pack], sin_ref[pack]
        turned = jnp.concatenate([a * cosine - b * sine, b * cosine + a * sine], axis=1)
        out_ref[pack, 0] = turned.astype(jnp.bfloat16)
        out_ref[pack, 1] = value.T.astype(jnp.bfloat16)


def project_second(where, hidden, weight, first, cosine, sine):
    return call(
        project_second_kernel,
        jax.ShapeDtypeStruct((4, 2, BLOCK, HEAD_DIM), jnp.bfloat16),
        [SMEM] + [VMEM] * 9,
        (2**29, 5 * 2**20),
        [pltpu.VMEM((4 * BLOCK, HEAD_DIM), jnp.float32)],
    )(where, *hidden, weight, first, cosine, sine)


def attend_kernel(tiles, opening, closing, where_ref, q_ref, start_ref, *refs):
    factor = math.log2(math.e) / math.sqrt(HEAD_DIM)
    y = where_ref[0]
    shifts = [shift for tile in tiles for shift in tile]
    kv, rest = dict(zip(shifts, refs)), refs[len(shifts) :]
    if not opening:
        given, rest = rest[:3], rest[3:]
    if closing:
        out_ref, acc, top, total = rest
    else:
        acc, top, total = rest

    @pl.loop(0, 4)
    def _(z):
        block = z * 8 + y
        slot = 0 if closing else z
        start = start_ref[z]
        row_at = block * BLOCK + lax.broadcasted_iota(jnp.int32, (BLOCK, BLOCK), 1)
        if opening:
            top[slot] = jnp.full(top.shape[1:], LOW, jnp.float32)
            total[slot] = jnp.zeros(total.shape[1:], jnp.float32)
            acc[slot] = jnp.zeros(acc.shape[1:], jnp.float32)
        else:
            for ref, source in zip((acc, top, total), given):
                ref[slot] = source[z]

        def turn(step, carry):
            zz = z - step
            for tile in tiles:
                places = [zz * 8 + ((y - shift) & 7) for shift in tile]
                needed = [
                    (place <= block) & ((place + 1) * BLOCK > where_ref[1 + z])
                    for place in places
                ]


                @pl.when(functools.reduce(jnp.logical_or, needed))
                def _(tile=tile, places=places):
                    key = jnp.concatenate([kv[shift][zz, 0] for shift in tile], axis=0)
                    val = jnp.concatenate([kv[shift][zz, 1] for shift in tile], axis=1)
                    allowed = []
                    for place in places:
                        at = place * BLOCK + lax.broadcasted_iota(jnp.int32, (BLOCK, BLOCK), 0)
                        allowed.append((at >= start) & (at <= row_at))
                    allowed = jnp.concatenate(allowed, axis=0)
                    for h in range(GROUP):
                        cols = slice(h * BLOCK, (h + 1) * BLOCK)
                        s = jnp.dot(key, q_ref[z, :, cols], preferred_element_type=jnp.float32)
                        s = jnp.where(allowed, s, LOW)
                        old = top[slot, :, cols]
                        new = jnp.maximum(old, jnp.max(s, axis=0, keepdims=True))
                        p = jnp.exp2((s - new) * factor)
                        scale = jnp.exp2((old - new) * factor)
                        top[slot, :, cols] = new
                        total[slot, :, cols] = total[slot, :, cols] * scale + jnp.sum(
                            p, axis=0, keepdims=True
                        )
                        acc[slot, :, cols] = acc[slot, :, cols] * scale + jnp.dot(
                            val, p.astype(jnp.bfloat16), preferred_element_type=jnp.float32
                        )

            return carry

        lax.fori_loop(0, z + 1, turn, 0)
        if closing:
            for h in range(GROUP):
                cols = slice(h * BLOCK, (h + 1) * BLOCK)
                mixed = acc[slot, :, cols] / total[slot, :, cols]
                out_ref[z, :, cols] = mixed.T.astype(jnp.bfloat16)


def attend(tiles, where, q, start, kv, state=None, closing=False):
    rows = GROUP * BLOCK
    slots = 1 if closing else 4
    shapes = [(slots, HEAD_DIM, rows), (slots, 1, rows), (slots, 1, rows)]
    held = [jax.ShapeDtypeStruct(shape, jnp.float32) for shape in shapes]
    given = [] if state is None else list(state)
    shifts = [shift for tile in tiles for shift in tile]
    out = jax.ShapeDtypeStruct((4, BLOCK, rows), jnp.bfloat16)
    return call(
        functools.partial(attend_kernel, tiles, state is None, closing),
        out if closing else held,
        [SMEM] + [VMEM] * (2 + len(shifts) + len(given)),
        (len(shifts) * 2**30, 4 * 2**20),
        [pltpu.VMEM(shape, jnp.float32) for shape in shapes] if closing else (),
    )(where, q, start, *[kv[shift] for shift in shifts], *given)


def repeat_kernel(rows_ref, out_ref):
    for j in range(4):
        out_ref[j] = rows_ref[...]


def repeat_rows(rows):
    out = jax.ShapeDtypeStruct((4,) + rows.shape, rows.dtype)
    return call(repeat_kernel, out, [VMEM], (0, 5 * 2**18))(rows)


def lay_out_kernel(heads_ref, out_ref, done):
    width = GROUP * HEAD_DIM
    copies = [
        pltpu.make_async_copy(
            heads_ref.at[j], out_ref.at[:, pl.ds(j * width, width)], done.at[j]
        )
        for j in range(KV_HEADS)
    ]
    for copy in copies:
        copy.start()
    for copy in copies:
        copy.wait()


def lay_out(heads):
    return pl.pallas_call(
        lay_out_kernel,
        out_shape=jax.ShapeDtypeStruct((BLOCK, HEADS * HEAD_DIM), jnp.bfloat16),
        in_specs=[VMEM],
        out_specs=pl.BlockSpec(memory_space=pl.ANY),
        scratch_shapes=[pltpu.SemaphoreType.DMA((KV_HEADS,))],
        compiler_params=pltpu.CompilerParams(vmem_limit_bytes=32 * 2**20),
    )(heads)


def on_device(hidden, queries, weight_copies, segment_ids, owner):
    y, z = lax.axis_index(Y), lax.axis_index(Z)
    x, c, zh = lax.axis_index("x"), lax.axis_index("c"), lax.axis_index("zh")
    segment_row = segment_ids[0]
    origin = owner[0] % 16

    pieces = weight_copies[0].reshape(BLOCK, 2, 4, 128).transpose(2, 1, 0, 3)
    row = segment_row.astype(jnp.bfloat16).reshape(1, 1, 32, 128)
    pieces = jnp.concatenate([pieces, jnp.broadcast_to(row, (4, 2, 32, 128))], axis=2)
    got = exchange(pieces.reshape(8, 160, 128), ("x", "c"))
    piece = pick(got[:, :BLOCK], origin % 8)
    rows_along = pick(got.reshape(4, 2, 160, 128)[:, :, BLOCK:], c, 1)
    piece = jnp.where(zh == origin // 8, piece, lax.ppermute(piece, "zh", ring(2, 1)))

    own = hidden[0]
    left = lax.ppermute(own, "x", ring(4, 1))
    right = lax.ppermute(own, "x", ring(4, -1))
    part = spread(piece, ("z1", "y1"), 8).reshape(8 * BLOCK, 128)
    part, left, right = lax.optimization_barrier((part, left, right))
    mine = exchange(repeat_rows(part), ("z0", "y0")).reshape(32, BLOCK, 128)
    far_low = lax.ppermute(left[:64], "x", ring(4, 1))
    far_high = lax.ppermute(right[64:], "x", ring(4, -1))

    blocks = segment_row.reshape(4, 8, BLOCK)
    start = starts_of(segment_row, pick(blocks, y, 1).reshape(-1)).reshape(4, BLOCK)
    token = (jnp.arange(4)[:, None] * 8 + y) * BLOCK + jnp.arange(BLOCK)[None]
    split = queries[0].reshape(BLOCK, 4, GROUP * HEAD_DIM).transpose(1, 0, 2)

    rows_along = rows_along.astype(jnp.int32)
    along = pick(rows_along, z * 8 + y, 1)
    start_along = starts_of(rows_along.reshape(4, -1), along)
    k_angles = angles_of((z * 8 + y) * BLOCK + jnp.arange(BLOCK)[None] - start_along)
    k_turns = (jnp.cos(k_angles), jnp.sin(k_angles))

    mine, far_low, far_high, start, split, k_turns = lax.optimization_barrier(
        (mine, far_low, far_high, start, split, k_turns)
    )
    q_angles = jnp.swapaxes(angles_of(token - start), 1, 2)
    q_turns = (jnp.cos(q_angles), jnp.sin(q_angles))
    other = lax.ppermute(mine, "c", ring(2, 1))
    rows = [own, left, far_low, far_high, right]
    first = project_first(rows, mine)
    both = project_second(
        jnp.stack([x, c]).astype(jnp.int32), rows, other, first, *k_turns
    )
    own_kv = exchange(exchange(both, "x"), Z)

    own_kv, split = lax.optimization_barrier((own_kv, split))
    q_turned = turn_queries(exchange(split, Z), *q_turns)

    where = jnp.concatenate([y[None], start[:, 0]]).astype(jnp.int32)
    start = start[:, None, :]
    kv = {0: own_kv}
    for step in (1, 2, 3):
        kv[step] = lax.ppermute(kv[step - 1], Y, ring(8, 1))
        kv[-step] = lax.ppermute(kv[1 - step], Y, ring(8, -1))
    state = attend(((0,), (1, 2)), where, q_turned, start, kv)
    kv[3], *state = lax.optimization_barrier((kv[3], *state))
    kv[4] = lax.ppermute(kv[3], Y, ring(8, 1))
    state = attend(((-1, -2), (3,), (-3,)), where, q_turned, start, kv, state)
    mixed = attend(((4,),), where, q_turned, start, kv, state, closing=True)
    back = exchange(mixed, Z)
    return lay_out(back)[None]


def solution(mesh):
    fine = Mesh(mesh.devices.reshape(SIZES), AXES)
    placed = (
        P(REP, SEQ, None),
        P(REP, SEQ, None),
        P(REP, SEQ, None),
        P(REP, None),
        P(),
    )
    return jax.shard_map(
        on_device, mesh=fine, in_specs=placed, out_specs=P(REP, SEQ, None), check_vma=False
    )
```

```python
import functools
import math

import jax
import jax.numpy as jnp
from jax import lax
from jax.experimental import pallas as pl
from jax.experimental.pallas import tpu as pltpu
from jax.sharding import Mesh
from jax.sharding import PartitionSpec as P

HEADS = 32
KV_HEADS = 4
HEAD_DIM = 128
GROUP = HEADS // KV_HEADS
THETA = 1000000.0
BLOCK = 128
LOW = -1e30
DOCS = 6

AXES = ("z1", "z0", "y1", "y0", "zh", "x", "c")
SIZES = (2, 2, 4, 2, 2, 4, 2)
SEQ = ("z1", "z0", "y1", "y0")
REP = ("zh", "x", "c")
Y = ("y1", "y0")
Z = ("z1", "z0")


def ring(size, shift):
    return [(i, (i + shift) % size) for i in range(size)]


def pick(value, index, axis=0):
    return lax.dynamic_index_in_dim(value, index, axis, keepdims=False)


def exchange(value, axes):
    return lax.all_to_all(value, axes, split_axis=0, concat_axis=0, tiled=True)


def spread(value, axes, members):
    return exchange(jnp.broadcast_to(value[None], (members,) + value.shape), axes)


def angles_of(positions):
    half = HEAD_DIM // 2
    freqs = THETA ** (-(jnp.arange(half, dtype=jnp.float32) * 2.0) / HEAD_DIM)
    return positions.astype(jnp.float32)[..., None] * freqs


def starts_of(segment_rows, segments):
    docs = jnp.arange(1, DOCS, dtype=jnp.int32)
    begins = jnp.sum((segment_rows[..., None, :] < docs[:, None]).astype(jnp.int32), axis=-1)
    passed = segments[..., None, :] >= docs[:, None]
    return jnp.max(jnp.where(passed, begins[..., None], 0), axis=-2)


VMEM = pl.BlockSpec(memory_space=pltpu.VMEM)
SMEM = pl.BlockSpec(memory_space=pltpu.SMEM)


def call(kernel, out_shape, specs, cost, scratch=()):
    flops, moved = cost
    return pl.pallas_call(
        kernel,
        out_shape=out_shape,
        in_specs=specs,
        out_specs=jax.tree.map(lambda _: VMEM, out_shape),
        scratch_shapes=list(scratch),
        compiler_params=pltpu.CompilerParams(vmem_limit_bytes=8 * 2**20),
        cost_estimate=pl.CostEstimate(flops=flops, bytes_accessed=moved, transcendentals=0),
    )


def turn_kernel(q_ref, cos_ref, sin_ref, out_ref):
    half = HEAD_DIM // 2

    @pl.loop(0, 4)
    def _(z):
        cosine, sine = cos_ref[z], sin_ref[z]
        for h in range(GROUP):
            cols = slice(h * HEAD_DIM, (h + 1) * HEAD_DIM)
            t = q_ref[z, :, cols].astype(jnp.float32).T
            a, b = t[:half], t[half:]
            out_ref[z, :half, cols] = (a * cosine - b * sine).astype(jnp.bfloat16)
            out_ref[z, half:, cols] = (b * cosine + a * sine).astype(jnp.bfloat16)


def turn_queries(q, cosine, sine):
    return call(
        turn_kernel,
        jax.ShapeDtypeStruct((4, HEAD_DIM, GROUP * BLOCK), jnp.bfloat16),
        [VMEM] * 3,
        (4 * 2**20, 2 * 2**20),
    )(q, cosine, sine)


def multiply(hidden_refs, weight_ref, out_ref):
    at = 0
    for hidden_ref in hidden_refs:
        total = None
        for block in range(0, 32, 2):
            z1, z0, y1 = block // 16, block // 8 % 2, block // 2 % 4
            low = z0 * 16 + z1 * 4 + y1
            weight = jnp.concatenate([weight_ref[low], weight_ref[low + 8]], axis=0)
            term = jnp.dot(
                hidden_ref[:, block * 128 : block * 128 + 256],
                weight,
                preferred_element_type=jnp.float32,
            )
            total = term if total is None else total + term
        out_ref[at : at + hidden_ref.shape[0]] = total
        at += hidden_ref.shape[0]


def project_first_kernel(*refs):
    multiply(refs[:5], refs[5], refs[6])


def project_first(hidden, weight):
    return call(
        project_first_kernel,
        jax.ShapeDtypeStruct((4 * BLOCK, HEAD_DIM), jnp.float32),
        [VMEM] * 6,
        (2**29, 5 * 2**20),
    )(*hidden, weight)


def project_second_kernel(*refs):
    where_ref, first_ref, cos_ref, sin_ref, out_ref, second = (refs[0],) + refs[7:]
    half = HEAD_DIM // 2
    multiply(refs[1:6], refs[6], second)
    x, keys_first = where_ref[0], where_ref[1] == 0
    for d in range(4):
        pack = (x - d) & 3
        one, two = first_ref[d * BLOCK : (d + 1) * BLOCK], second[d * BLOCK : (d + 1) * BLOCK]
        key = jnp.where(keys_first, one, two)
        value = jnp.where(keys_first, two, one)
        a, b = key[:, :half], key[:, half:]
        cosine, sine = cos_ref[pack], sin_ref[pack]
        turned = jnp.concatenate([a * cosine - b * sine, b * cosine + a * sine], axis=1)
        out_ref[pack, 0] = turned.astype(jnp.bfloat16)
        out_ref[pack, 1] = value.T.astype(jnp.bfloat16)


def project_second(where, hidden, weight, first, cosine, sine):
    return call(
        project_second_kernel,
        jax.ShapeDtypeStruct((4, 2, BLOCK, HEAD_DIM), jnp.bfloat16),
        [SMEM] + [VMEM] * 9,
        (2**29, 5 * 2**20),
        [pltpu.VMEM((4 * BLOCK, HEAD_DIM), jnp.float32)],
    )(where, *hidden, weight, first, cosine, sine)


def attend_kernel(tiles, opening, closing, where_ref, q_ref, start_ref, *refs):
    factor = math.log2(math.e) / math.sqrt(HEAD_DIM)
    y = where_ref[0]
    shifts = [shift for tile in tiles for shift in tile]
    kv, rest = dict(zip(shifts, refs)), refs[len(shifts) :]
    if not opening:
        given, rest = rest[:3], rest[3:]
    if closing:
        out_ref, acc, top, total = rest
    else:
        acc, top, total = rest

    @pl.loop(0, 4)
    def _(z):
        block = z * 8 + y
        slot = 0 if closing else z
        start = start_ref[z]
        row_at = block * BLOCK + lax.broadcasted_iota(jnp.int32, (BLOCK, BLOCK), 1)
        if opening:
            top[slot] = jnp.full(top.shape[1:], LOW, jnp.float32)
            total[slot] = jnp.zeros(total.shape[1:], jnp.float32)
            acc[slot] = jnp.zeros(acc.shape[1:], jnp.float32)
        else:
            for ref, source in zip((acc, top, total), given):
                ref[slot] = source[z]

        def turn(step, carry):
            zz = z - step
            for tile in tiles:
                places = [zz * 8 + ((y - shift) & 7) for shift in tile]
                needed = [
                    (place <= block) & ((place + 1) * BLOCK > where_ref[1 + z])
                    for place in places
                ]


                @pl.when(functools.reduce(jnp.logical_or, needed))
                def _(tile=tile, places=places):
                    key = jnp.concatenate([kv[shift][zz, 0] for shift in tile], axis=0)
                    val = jnp.concatenate([kv[shift][zz, 1] for shift in tile], axis=1)
                    allowed = []
                    for place in places:
                        at = place * BLOCK + lax.broadcasted_iota(jnp.int32, (BLOCK, BLOCK), 0)
                        allowed.append((at >= start) & (at <= row_at))
                    allowed = jnp.concatenate(allowed, axis=0)
                    for h in range(GROUP):
                        cols = slice(h * BLOCK, (h + 1) * BLOCK)
                        s = jnp.dot(key, q_ref[z, :, cols], preferred_element_type=jnp.float32)
                        s = jnp.where(allowed, s, LOW)
                        old = top[slot, :, cols]
                        new = jnp.maximum(old, jnp.max(s, axis=0, keepdims=True))
                        p = jnp.exp2((s - new) * factor)
                        scale = jnp.exp2((old - new) * factor)
                        top[slot, :, cols] = new
                        total[slot, :, cols] = total[slot, :, cols] * scale + jnp.sum(
                            p, axis=0, keepdims=True
                        )
                        acc[slot, :, cols] = acc[slot, :, cols] * scale + jnp.dot(
                            val, p.astype(jnp.bfloat16), preferred_element_type=jnp.float32
                        )

            return carry

        lax.fori_loop(0, z + 1, turn, 0)
        if closing:
            for h in range(GROUP):
                cols = slice(h * BLOCK, (h + 1) * BLOCK)
                mixed = acc[slot, :, cols] / total[slot, :, cols]
                out_ref[z, :, cols] = mixed.T.astype(jnp.bfloat16)


def attend(tiles, where, q, start, kv, state=None, closing=False):
    rows = GROUP * BLOCK
    slots = 1 if closing else 4
    shapes = [(slots, HEAD_DIM, rows), (slots, 1, rows), (slots, 1, rows)]
    held = [jax.ShapeDtypeStruct(shape, jnp.float32) for shape in shapes]
    given = [] if state is None else list(state)
    shifts = [shift for tile in tiles for shift in tile]
    out = jax.ShapeDtypeStruct((4, BLOCK, rows), jnp.bfloat16)
    return call(
        functools.partial(attend_kernel, tiles, state is None, closing),
        out if closing else held,
        [SMEM] + [VMEM] * (2 + len(shifts) + len(given)),
        (len(shifts) * 2**30, 4 * 2**20),
        [pltpu.VMEM(shape, jnp.float32) for shape in shapes] if closing else (),
    )(where, q, start, *[kv[shift] for shift in shifts], *given)


def repeat_kernel(rows_ref, out_ref):
    for j in range(4):
        out_ref[j] = rows_ref[...]


def repeat_rows(rows):
    out = jax.ShapeDtypeStruct((4,) + rows.shape, rows.dtype)
    return call(repeat_kernel, out, [VMEM], (0, 5 * 2**18))(rows)


def lay_out_kernel(heads_ref, out_ref, done):
    width = GROUP * HEAD_DIM
    copies = [
        pltpu.make_async_copy(
            heads_ref.at[j], out_ref.at[:, pl.ds(j * width, width)], done.at[j]
        )
        for j in range(KV_HEADS)
    ]
    for copy in copies:
        copy.start()
    for copy in copies:
        copy.wait()


def lay_out(heads):
    return pl.pallas_call(
        lay_out_kernel,
        out_shape=jax.ShapeDtypeStruct((BLOCK, HEADS * HEAD_DIM), jnp.bfloat16),
        in_specs=[VMEM],
        out_specs=pl.BlockSpec(memory_space=pl.ANY),
        scratch_shapes=[pltpu.SemaphoreType.DMA((KV_HEADS,))],
        compiler_params=pltpu.CompilerParams(vmem_limit_bytes=8 * 2**20),
    )(heads)


def on_device(hidden, queries, weight_copies, segment_ids, owner):
    y, z = lax.axis_index(Y), lax.axis_index(Z)
    x, c, zh = lax.axis_index("x"), lax.axis_index("c"), lax.axis_index("zh")
    segment_row = segment_ids[0]
    origin = owner[0] % 16

    pieces = weight_copies[0].reshape(BLOCK, 2, 4, 128).transpose(2, 1, 0, 3)
    row = segment_row.astype(jnp.bfloat16).reshape(1, 1, 32, 128)
    pieces = jnp.concatenate([pieces, jnp.broadcast_to(row, (4, 2, 32, 128))], axis=2)
    got = exchange(pieces.reshape(8, 160, 128), ("x", "c"))
    piece = pick(got[:, :BLOCK], origin % 8)
    rows_along = pick(got.reshape(4, 2, 160, 128)[:, :, BLOCK:], c, 1)
    piece = jnp.where(zh == origin // 8, piece, lax.ppermute(piece, "zh", ring(2, 1)))

    own = hidden[0]
    left = lax.ppermute(own, "x", ring(4, 1))
    right = lax.ppermute(own, "x", ring(4, -1))
    part = spread(piece, ("z1", "y1"), 8).reshape(8 * BLOCK, 128)
    part, left, right = lax.optimization_barrier((part, left, right))
    mine = exchange(repeat_rows(part), ("z0", "y0")).reshape(32, BLOCK, 128)
    far_low = lax.ppermute(left[:64], "x", ring(4, 1))
    far_high = lax.ppermute(right[64:], "x", ring(4, -1))

    blocks = segment_row.reshape(4, 8, BLOCK)
    start = starts_of(segment_row, pick(blocks, y, 1).reshape(-1)).reshape(4, BLOCK)
    token = (jnp.arange(4)[:, None] * 8 + y) * BLOCK + jnp.arange(BLOCK)[None]
    split = queries[0].reshape(BLOCK, 4, GROUP * HEAD_DIM).transpose(1, 0, 2)

    rows_along = rows_along.astype(jnp.int32)
    along = pick(rows_along, z * 8 + y, 1)
    start_along = starts_of(rows_along.reshape(4, -1), along)
    k_angles = angles_of((z * 8 + y) * BLOCK + jnp.arange(BLOCK)[None] - start_along)
    k_turns = (jnp.cos(k_angles), jnp.sin(k_angles))

    mine, far_low, far_high, start, split, k_turns = lax.optimization_barrier(
        (mine, far_low, far_high, start, split, k_turns)
    )
    q_angles = jnp.swapaxes(angles_of(token - start), 1, 2)
    q_turns = (jnp.cos(q_angles), jnp.sin(q_angles))
    other = lax.ppermute(mine, "c", ring(2, 1))
    rows = [own, left, far_low, far_high, right]
    first = project_first(rows, mine)
    both = project_second(
        jnp.stack([x, c]).astype(jnp.int32), rows, other, first, *k_turns
    )
    own_kv = exchange(exchange(both, "x"), Z)

    own_kv, split = lax.optimization_barrier((own_kv, split))
    q_turned = turn_queries(exchange(split, Z), *q_turns)

    where = jnp.concatenate([y[None], start[:, 0]]).astype(jnp.int32)
    start = start[:, None, :]
    kv = {0: own_kv}
    for step in (1, 2, 3):
        kv[step] = lax.ppermute(kv[step - 1], Y, ring(8, 1))
        kv[-step] = lax.ppermute(kv[1 - step], Y, ring(8, -1))
    state = attend(((0,), (1, 2)), where, q_turned, start, kv)
    kv[3], *state = lax.optimization_barrier((kv[3], *state))
    kv[4] = lax.ppermute(kv[3], Y, ring(8, 1))
    state = attend(((-1, -2), (3,), (-3,)), where, q_turned, start, kv, state)
    mixed = attend(((4,),), where, q_turned, start, kv, state, closing=True)
    back = exchange(mixed, Z)
    return lay_out(back)[None]


def solution(mesh):
    fine = Mesh(mesh.devices.reshape(SIZES), AXES)
    placed = (
        P(REP, SEQ, None),
        P(REP, SEQ, None),
        P(REP, SEQ, None),
        P(REP, None),
        P(),
    )
    return jax.shard_map(
        on_device, mesh=fine, in_specs=placed, out_specs=P(REP, SEQ, None), check_vma=False
    )
```

```python
import functools
import math

import jax
import jax.numpy as jnp
from jax import lax
from jax.experimental import pallas as pl
from jax.experimental.pallas import tpu as pltpu
from jax.sharding import Mesh
from jax.sharding import PartitionSpec as P

HEADS = 32
KV_HEADS = 4
HEAD_DIM = 128
GROUP = HEADS // KV_HEADS
THETA = 1000000.0
BLOCK = 128
LOW = -1e30
DOCS = 6

AXES = ("z1", "z0", "y1", "y0", "zh", "x", "c")
SIZES = (2, 2, 4, 2, 2, 4, 2)
SEQ = ("z1", "z0", "y1", "y0")
REP = ("zh", "x", "c")
Y = ("y1", "y0")
Z = ("z1", "z0")


def ring(size, shift):
    return [(i, (i + shift) % size) for i in range(size)]


def pick(value, index, axis=0):
    return lax.dynamic_index_in_dim(value, index, axis, keepdims=False)


def exchange(value, axes):
    return lax.all_to_all(value, axes, split_axis=0, concat_axis=0, tiled=True)


def spread(value, axes, members):
    return exchange(jnp.broadcast_to(value[None], (members,) + value.shape), axes)


def angles_of(positions):
    half = HEAD_DIM // 2
    freqs = THETA ** (-(jnp.arange(half, dtype=jnp.float32) * 2.0) / HEAD_DIM)
    return positions.astype(jnp.float32)[..., None] * freqs


def starts_of(segment_rows, segments):
    docs = jnp.arange(1, DOCS, dtype=jnp.int32)
    begins = jnp.sum((segment_rows[..., None, :] < docs[:, None]).astype(jnp.int32), axis=-1)
    passed = segments[..., None, :] >= docs[:, None]
    return jnp.max(jnp.where(passed, begins[..., None], 0), axis=-2)


VMEM = pl.BlockSpec(memory_space=pltpu.VMEM)
SMEM = pl.BlockSpec(memory_space=pltpu.SMEM)


def call(kernel, out_shape, specs, cost, scratch=()):
    flops, moved = cost
    return pl.pallas_call(
        kernel,
        out_shape=out_shape,
        in_specs=specs,
        out_specs=jax.tree.map(lambda _: VMEM, out_shape),
        scratch_shapes=list(scratch),
        compiler_params=pltpu.CompilerParams(vmem_limit_bytes=8 * 2**20),
        cost_estimate=pl.CostEstimate(flops=flops, bytes_accessed=moved, transcendentals=0),
    )


def turn_kernel(q_ref, cos_ref, sin_ref, out_ref):
    half = HEAD_DIM // 2

    @pl.loop(0, 4)
    def _(z):
        cosine, sine = cos_ref[z], sin_ref[z]
        for h in range(GROUP):
            cols = slice(h * HEAD_DIM, (h + 1) * HEAD_DIM)
            t = q_ref[z, :, cols].astype(jnp.float32).T
            a, b = t[:half], t[half:]
            out_ref[z, :half, cols] = (a * cosine - b * sine).astype(jnp.bfloat16)
            out_ref[z, half:, cols] = (b * cosine + a * sine).astype(jnp.bfloat16)


def turn_queries(q, cosine, sine):
    return call(
        turn_kernel,
        jax.ShapeDtypeStruct((4, HEAD_DIM, GROUP * BLOCK), jnp.bfloat16),
        [VMEM] * 3,
        (4 * 2**20, 2 * 2**20),
    )(q, cosine, sine)


def multiply(hidden_refs, weight_ref, out_ref):
    at = 0
    for hidden_ref in hidden_refs:
        total = None
        for block in range(0, 32, 2):
            z1, z0, y1 = block // 16, block // 8 % 2, block // 2 % 4
            low = z0 * 16 + z1 * 4 + y1
            weight = jnp.concatenate([weight_ref[low], weight_ref[low + 8]], axis=0)
            term = jnp.dot(
                hidden_ref[:, block * 128 : block * 128 + 256],
                weight,
                preferred_element_type=jnp.float32,
            )
            total = term if total is None else total + term
        out_ref[at : at + hidden_ref.shape[0]] = total
        at += hidden_ref.shape[0]


def project_first_kernel(*refs):
    multiply(refs[:5], refs[5], refs[6])


def project_first(hidden, weight):
    return call(
        project_first_kernel,
        jax.ShapeDtypeStruct((4 * BLOCK, HEAD_DIM), jnp.float32),
        [VMEM] * 6,
        (2**29, 5 * 2**20),
    )(*hidden, weight)


def project_second_kernel(*refs):
    where_ref, first_ref, cos_ref, sin_ref, out_ref, second = (refs[0],) + refs[7:]
    half = HEAD_DIM // 2
    multiply(refs[1:6], refs[6], second)
    x, keys_first = where_ref[0], where_ref[1] == 0
    for d in range(4):
        pack = (x - d) & 3
        one, two = first_ref[d * BLOCK : (d + 1) * BLOCK], second[d * BLOCK : (d + 1) * BLOCK]
        key = jnp.where(keys_first, one, two)
        value = jnp.where(keys_first, two, one)
        a, b = key[:, :half], key[:, half:]
        cosine, sine = cos_ref[pack], sin_ref[pack]
        turned = jnp.concatenate([a * cosine - b * sine, b * cosine + a * sine], axis=1)
        out_ref[pack, 0] = turned.astype(jnp.bfloat16)
        out_ref[pack, 1] = value.T.astype(jnp.bfloat16)


def project_second(where, hidden, weight, first, cosine, sine):
    return call(
        project_second_kernel,
        jax.ShapeDtypeStruct((4, 2, BLOCK, HEAD_DIM), jnp.bfloat16),
        [SMEM] + [VMEM] * 9,
        (2**29, 5 * 2**20),
        [pltpu.VMEM((4 * BLOCK, HEAD_DIM), jnp.float32)],
    )(where, *hidden, weight, first, cosine, sine)


def attend_kernel(tiles, opening, closing, where_ref, q_ref, start_ref, *refs):
    factor = math.log2(math.e) / math.sqrt(HEAD_DIM)
    y = where_ref[0]
    shifts = [shift for tile in tiles for shift in tile]
    kv, rest = dict(zip(shifts, refs)), refs[len(shifts) :]
    if not opening:
        given, rest = rest[:3], rest[3:]
    if closing:
        out_ref, acc, top, total = rest
    else:
        acc, top, total = rest

    @pl.loop(0, 4)
    def _(z):
        block = z * 8 + y
        slot = 0 if closing else z
        start = start_ref[z]
        row_at = block * BLOCK + lax.broadcasted_iota(jnp.int32, (BLOCK, BLOCK), 1)
        if opening:
            top[slot] = jnp.full(top.shape[1:], LOW, jnp.float32)
            total[slot] = jnp.zeros(total.shape[1:], jnp.float32)
            acc[slot] = jnp.zeros(acc.shape[1:], jnp.float32)
        else:
            for ref, source in zip((acc, top, total), given):
                ref[slot] = source[z]

        def turn(step, carry):
            zz = z - step
            for tile in tiles:
                places = [zz * 8 + ((y - shift) & 7) for shift in tile]
                needed = [
                    (place <= block) & ((place + 1) * BLOCK > where_ref[1 + z])
                    for place in places
                ]


                @pl.when(functools.reduce(jnp.logical_or, needed))
                def _(tile=tile, places=places):
                    key = jnp.concatenate([kv[shift][zz, 0] for shift in tile], axis=0)
                    val = jnp.concatenate([kv[shift][zz, 1] for shift in tile], axis=1)
                    allowed = []
                    for place in places:
                        at = place * BLOCK + lax.broadcasted_iota(jnp.int32, (BLOCK, BLOCK), 0)
                        allowed.append((at >= start) & (at <= row_at))
                    allowed = jnp.concatenate(allowed, axis=0)
                    for h in range(GROUP):
                        cols = slice(h * BLOCK, (h + 1) * BLOCK)
                        s = jnp.dot(key, q_ref[z, :, cols], preferred_element_type=jnp.float32)
                        s = jnp.where(allowed, s, LOW)
                        old = top[slot, :, cols]
                        new = jnp.maximum(old, jnp.max(s, axis=0, keepdims=True))
                        p = jnp.exp2((s - new) * factor)
                        scale = jnp.exp2((old - new) * factor)
                        top[slot, :, cols] = new
                        total[slot, :, cols] = total[slot, :, cols] * scale + jnp.sum(
                            p, axis=0, keepdims=True
                        )
                        acc[slot, :, cols] = acc[slot, :, cols] * scale + jnp.dot(
                            val, p.astype(jnp.bfloat16), preferred_element_type=jnp.float32
                        )

            return carry

        lax.fori_loop(0, z + 1, turn, 0)
        if closing:
            for h in range(GROUP):
                cols = slice(h * BLOCK, (h + 1) * BLOCK)
                mixed = acc[slot, :, cols] / total[slot, :, cols]
                out_ref[z, :, cols] = mixed.T.astype(jnp.bfloat16)


def attend(tiles, where, q, start, kv, state=None, closing=False):
    rows = GROUP * BLOCK
    slots = 1 if closing else 4
    shapes = [(slots, HEAD_DIM, rows), (slots, 1, rows), (slots, 1, rows)]
    held = [jax.ShapeDtypeStruct(shape, jnp.float32) for shape in shapes]
    given = [] if state is None else list(state)
    shifts = [shift for tile in tiles for shift in tile]
    out = jax.ShapeDtypeStruct((4, BLOCK, rows), jnp.bfloat16)
    return call(
        functools.partial(attend_kernel, tiles, state is None, closing),
        out if closing else held,
        [SMEM] + [VMEM] * (2 + len(shifts) + len(given)),
        (len(shifts) * 2**30, 4 * 2**20),
        [pltpu.VMEM(shape, jnp.float32) for shape in shapes] if closing else (),
    )(where, q, start, *[kv[shift] for shift in shifts], *given)


def repeat_kernel(rows_ref, out_ref):
    for j in range(4):
        out_ref[j] = rows_ref[...]


def repeat_rows(rows):
    out = jax.ShapeDtypeStruct((4,) + rows.shape, rows.dtype)
    return call(repeat_kernel, out, [VMEM], (0, 5 * 2**18))(rows)


def choose_kernel(held_ref, own_ref, other_ref, out_ref):
    chosen = jnp.where(held_ref[0] == 1, own_ref[...], other_ref[...])
    for j in range(8):
        out_ref[j] = chosen


def choose_rows(held, own, other):
    out = jax.ShapeDtypeStruct((8,) + own.shape, own.dtype)
    return call(choose_kernel, out, [SMEM, VMEM, VMEM], (0, 2**18))(held, own, other)


def lay_out_kernel(heads_ref, out_ref, done):
    width = GROUP * HEAD_DIM
    copies = [
        pltpu.make_async_copy(
            heads_ref.at[j], out_ref.at[:, pl.ds(j * width, width)], done.at[j]
        )
        for j in range(KV_HEADS)
    ]
    for copy in copies:
        copy.start()
    for copy in copies:
        copy.wait()


def lay_out(heads):
    return pl.pallas_call(
        lay_out_kernel,
        out_shape=jax.ShapeDtypeStruct((BLOCK, HEADS * HEAD_DIM), jnp.bfloat16),
        in_specs=[VMEM],
        out_specs=pl.BlockSpec(memory_space=pl.ANY),
        scratch_shapes=[pltpu.SemaphoreType.DMA((KV_HEADS,))],
        compiler_params=pltpu.CompilerParams(vmem_limit_bytes=8 * 2**20),
    )(heads)


def on_device(hidden, queries, weight_copies, segment_ids, owner):
    y, z = lax.axis_index(Y), lax.axis_index(Z)
    x, c, zh = lax.axis_index("x"), lax.axis_index("c"), lax.axis_index("zh")
    segment_row = segment_ids[0]
    origin = owner[0] % 16

    pieces = weight_copies[0].reshape(BLOCK, 2, 4, 128).transpose(2, 1, 0, 3)
    row = segment_row.astype(jnp.bfloat16).reshape(1, 1, 32, 128)
    pieces = jnp.concatenate([pieces, jnp.broadcast_to(row, (4, 2, 32, 128))], axis=2)
    got = exchange(pieces.reshape(8, 160, 128), ("x", "c"))
    piece = pick(got[:, :BLOCK], origin % 8)
    rows_along = pick(got.reshape(4, 2, 160, 128)[:, :, BLOCK:], c, 1)
    held = (zh == origin // 8).astype(jnp.int32)[None]
    pieces = choose_rows(held, piece, lax.ppermute(piece, "zh", ring(2, 1)))

    own = hidden[0]
    left = lax.ppermute(own, "x", ring(4, 1))
    right = lax.ppermute(own, "x", ring(4, -1))
    part = exchange(pieces, ("z1", "y1")).reshape(8 * BLOCK, 128)
    part, left, right = lax.optimization_barrier((part, left, right))
    mine = exchange(repeat_rows(part), ("z0", "y0")).reshape(32, BLOCK, 128)
    far_low = lax.ppermute(left[:64], "x", ring(4, 1))
    far_high = lax.ppermute(right[64:], "x", ring(4, -1))

    blocks = segment_row.reshape(4, 8, BLOCK)
    start = starts_of(segment_row, pick(blocks, y, 1).reshape(-1)).reshape(4, BLOCK)
    token = (jnp.arange(4)[:, None] * 8 + y) * BLOCK + jnp.arange(BLOCK)[None]
    split = queries[0].reshape(BLOCK, 4, GROUP * HEAD_DIM).transpose(1, 0, 2)

    rows_along = rows_along.astype(jnp.int32)
    along = pick(rows_along, z * 8 + y, 1)
    start_along = starts_of(rows_along.reshape(4, -1), along)
    k_angles = angles_of((z * 8 + y) * BLOCK + jnp.arange(BLOCK)[None] - start_along)
    k_turns = (jnp.cos(k_angles), jnp.sin(k_angles))

    mine, far_low, far_high, start, split, k_turns = lax.optimization_barrier(
        (mine, far_low, far_high, start, split, k_turns)
    )
    q_angles = jnp.swapaxes(angles_of(token - start), 1, 2)
    q_turns = (jnp.cos(q_angles), jnp.sin(q_angles))
    other = lax.ppermute(mine, "c", ring(2, 1))
    rows = [own, left, far_low, far_high, right]
    first = project_first(rows, mine)
    both = project_second(
        jnp.stack([x, c]).astype(jnp.int32), rows, other, first, *k_turns
    )
    own_kv = exchange(exchange(both, "x"), Z)

    own_kv, split = lax.optimization_barrier((own_kv, split))
    q_turned = turn_queries(exchange(split, Z), *q_turns)

    where = jnp.concatenate([y[None], start[:, 0]]).astype(jnp.int32)
    start = start[:, None, :]
    kv = {0: own_kv}
    for step in (1, 2, 3):
        kv[step] = lax.ppermute(kv[step - 1], Y, ring(8, 1))
        kv[-step] = lax.ppermute(kv[1 - step], Y, ring(8, -1))
    state = attend(((0,), (1, 2)), where, q_turned, start, kv)
    kv[3], *state = lax.optimization_barrier((kv[3], *state))
    kv[4] = lax.ppermute(kv[3], Y, ring(8, 1))
    state = attend(((-1, -2), (3,), (-3,)), where, q_turned, start, kv, state)
    mixed = attend(((4,),), where, q_turned, start, kv, state, closing=True)
    back = exchange(mixed, Z)
    return lay_out(back)[None]


def solution(mesh):
    fine = Mesh(mesh.devices.reshape(SIZES), AXES)
    placed = (
        P(REP, SEQ, None),
        P(REP, SEQ, None),
        P(REP, SEQ, None),
        P(REP, None),
        P(),
    )
    return jax.shard_map(
        on_device, mesh=fine, in_specs=placed, out_specs=P(REP, SEQ, None), check_vma=False
    )
```
